32 devices in a mesh: section: 2 (over y), dp: 4 (over x, core), tensor: 4 (over z).
Axes of the slice: x: 2, y: 2, z: 4, core: 2. Of those that a mesh axis runs over, the one named last changes fastest.
Arguments:
- block_input: bfloat16 [4, 4096, 1024], P(None, ('dp', 'tensor')), may hold values from -6 to 6
- seq_lengths: int32 [4, 4, 4], P(None, 'dp'), may hold values from 1 to 512, as said below
- w_qkv: bfloat16 [2, 1024, 3, 1024], P('section', 'dp', None, 'tensor'), may hold values from -0.25 to 0.25
- w_out: bfloat16 [2, 1024, 1024], P('section', 'tensor', 'dp'), may hold values from -0.5 to 0.5
- w_in: bfloat16 [2, 1024, 4096], P('section', 'dp', 'tensor'), may hold values from -0.1875 to 0.1875
- w_back: bfloat16 [2, 4096, 1024], P('section', 'tensor', 'dp'), may hold values from -0.09375 to 0.09375
- gains: bfloat16 [2, 2, 1024], P('section', None, 'dp'), may hold values from 0.25 to 1.75
- biases: bfloat16 [2, 6, 1024], P('section', None, 'dp'), may hold values from -3 to 3
- ffn_bias: bfloat16 [2, 4096], P('section', 'dp'), may hold values from -3 to 3
- out_grad: bfloat16 [4, 4096, 1024], P(None, ('dp', 'tensor')), may hold values from -6 to 6
Outputs:
- layer_outputs: float32 [2, 4, 4096, 1024], P('section', None, ('dp', 'tensor'))
- input_grads: float32 [2, 4, 4096, 1024], P('section', None, ('dp', 'tensor'))
- grad_w_qkv: float32 [2, 1024, 3, 1024], P('section', 'dp', None, 'tensor')
- grad_w_out: float32 [2, 1024, 1024], P('section', 'tensor', 'dp')
- grad_w_in: float32 [2, 1024, 4096], P('section', 'dp', 'tensor')
- grad_w_back: float32 [2, 4096, 1024], P('section', 'tensor', 'dp')
- grad_gains: float32 [2, 2, 1024], P('section', None, 'dp')
- grad_biases: float32 [2, 6, 1024], P('section', None, 'dp')
- grad_ffn_bias: float32 [2, 4096], P('section', 'dp')
The draws below stay inside these ranges and needn't reach their ends.
Inputs may be any that keep to these rules, and one draw needn't show every extreme that they name: `seq_lengths`: in each micro-batch and group the 4 lengths add up to at most 1024, and exactly 1024 in one group among all micro-batches and groups; the longest length of every group is exactly 512.
All inputs are finite; a program needn't handle non-finite values.
Results may differ from the reference program's by a relative error of at most 0.03.
Values may be sent and summed in bfloat16 or wider, within the bound.
No kernel may reach another device: no remote copies, remote signals or barrier semaphores. Data moves between devices by JAX's collectives and lax.ppermute only.
A program may use at most 512 MiB of HBM per device.

```python
import jax
import jax.numpy as jnp
from jax import lax

D = 1024
HEADS = 16
HEAD_DIM = 64
FF = 4096
GROUP_ROWS = 1024
SEQ_MAX = 512
MICRO = 4
LAYERS = 2
GROUPS = 4
SEQS = 4
TOKENS = 4096


def draw_seq_lengths(key, part):
    key = jax.random.fold_in(key, 11)
    pick_key, full_key, order_key = jax.random.split(key, 3)
    other_most = (GROUP_ROWS - SEQ_MAX) // (SEQS - 1)
    others = jax.random.randint(pick_key, (MICRO, GROUPS, SEQS - 1), 1, other_most + 1).astype(jnp.int32)
    full_group = jax.random.randint(full_key, (), 0, MICRO * GROUPS).astype(jnp.int32)
    is_full = (jnp.arange(MICRO * GROUPS, dtype=jnp.int32).reshape(MICRO, GROUPS) == full_group)[:, :, None]
    remainder = GROUP_ROWS - SEQ_MAX - (SEQS - 1) * other_most
    filled = other_most + remainder * (jnp.arange(SEQS - 1, dtype=jnp.int32) == 0).astype(jnp.int32)
    others = jnp.where(is_full, filled[None, None, :], others)
    longest = jnp.full((MICRO, GROUPS, 1), SEQ_MAX, jnp.int32)
    lengths = jnp.concatenate([longest, others], axis=-1)
    return jax.random.permutation(order_key, lengths, axis=-1, independent=True).astype(jnp.int32)


def shard_levels(stream_key, dims, cuts, smallest, high):
    level = 1.0
    for axis_at, blocks in cuts:
        draws = jax.random.uniform(jax.random.fold_in(jax.random.fold_in(stream_key, 6), axis_at), (blocks,), jnp.float32, smallest / len(cuts), high / len(cuts))
        level = level * jnp.repeat(jnp.exp(draws), dims[axis_at] // blocks).reshape((-1,) + (1,) * (len(dims) - 1 - axis_at))
    return level


def noise(stream_key, shape, width, bound, cuts=(), kind=jnp.bfloat16):
    result = width * jax.random.normal(stream_key, shape, jnp.float32)
    if cuts:
        result = result * shard_levels(stream_key, shape, cuts, -0.22, 0.18)
    return jnp.clip(result, -bound, bound).astype(kind)


def setup_inputs(seed: int = 0) -> dict:
    splits = jax.random.split(jax.random.key(seed), 11)
    return {
        "block_input": noise(splits[0], (MICRO, TOKENS, D), 1.0, 6.0, ((1, 16),)),
        "seq_lengths": draw_seq_lengths(jax.random.fold_in(splits[10], 71), 0),
        "w_qkv": noise(splits[2], (LAYERS, D, 3, D), (D // 2) ** -0.5, 0.25, ((0, 2), (1, 4), (3, 4))),
        "w_out": noise(splits[3], (LAYERS, D, D), (D // 8) ** -0.5, 0.5, ((0, 2), (1, 4), (2, 4))),
        "w_in": noise(splits[4], (LAYERS, D, FF), D ** -0.5, 0.1875, ((0, 2), (1, 4), (2, 4))),
        "w_back": noise(splits[5], (LAYERS, FF, D), FF ** -0.5, 0.09375, ((0, 2), (1, 4), (2, 4))),
        "gains": jnp.clip(1.0 + 0.15 * jax.random.normal(splits[6], (LAYERS, 2, D), jnp.float32), 0.25, 1.75).astype(jnp.bfloat16),
        "biases": noise(splits[7], (LAYERS, 6, D), 0.5, 3.0, ((0, 2), (2, 4))),
        "ffn_bias": noise(splits[8], (LAYERS, FF), 0.5, 3.0, ((0, 2), (1, 4))),
        "out_grad": noise(splits[9], (MICRO, TOKENS, D), 1.0, 6.0, ((1, 16),)),
    }


@jax.custom_vjp
def low(v):
    return lax.optimization_barrier(v.astype(jnp.bfloat16)).astype(jnp.float32)

@jax.custom_vjp
def low_back(v):
    return v

def low_keep(v):
    return (low(v), None)

def low_pass(kept, grad):
    return (grad,)

def back_keep(v):
    return (v, None)

def back_low(kept, grad):
    return (low(grad),)
low.defvjp(low_keep, low_pass)
low_back.defvjp(back_keep, back_low)

def product(lhs_mat, rhs_mat):
    return jnp.dot(lhs_mat, rhs_mat, precision=lax.Precision.HIGHEST, preferred_element_type=jnp.float32)

def normalize(summed, gain_row, bias_row):
    centered = summed - lax.optimization_barrier(jnp.mean(summed, axis=-1, keepdims=True))
    variance = lax.optimization_barrier(jnp.mean(centered * centered, axis=-1, keepdims=True))
    return centered * lax.rsqrt(variance + 1e-05) * gain_row + bias_row

def segment_ids(seq_lens, row_count):
    seq_ends = jnp.cumsum(seq_lens).astype(jnp.int32)
    positions = jnp.arange(row_count, dtype=jnp.int32)
    return lax.optimization_barrier(jnp.sum((positions[:, None] >= seq_ends[None, :]).astype(jnp.int32), axis=1)).astype(jnp.int32)

def attend(queries, key_rows, value_rows, segments):
    row_count = queries.shape[0]
    block_rows = min(512, row_count)
    blocks = row_count // block_rows
    factor = HEAD_DIM ** (-0.5)

    def one_block(query_block, segment_block):
        scores = jnp.einsum('qhd,khd->hqk', query_block, key_rows, precision=lax.Precision.HIGHEST) * factor
        scores = low_back(scores)
        allowed = segment_block[:, None] == segments[None, :]
        scores = jnp.where(allowed[None], scores, -1000000000.0)
        weights = low(jax.nn.softmax(scores, axis=-1))
        return jnp.einsum('hqk,khd->qhd', weights, value_rows, precision=lax.Precision.HIGHEST)
    checked = jax.checkpoint(one_block)
    context_parts = lax.map(lambda block_pair: checked(block_pair[0], block_pair[1]), (queries.reshape(blocks, block_rows, HEADS, HEAD_DIM), segments.reshape(blocks, block_rows)))
    return context_parts.reshape(row_count, HEADS * HEAD_DIM)

def encoder_layer(inputs, segments, w_qkv, w_out, w_in, w_back, gains, biases, ffn_bias):
    row_count = inputs.shape[0]
    mixed_rows = low_back(product(inputs, w_qkv.reshape(D, 3 * D)))
    offset = jnp.concatenate([biases[0], jnp.zeros((D,), jnp.float32), biases[1]])
    packed = low(mixed_rows + offset).reshape(row_count, 3, HEADS, HEAD_DIM)
    context = attend(packed[:, 0], packed[:, 1], packed[:, 2], segments)
    context = low(low_back(context))
    attended = low_back(product(context, w_out)) + biases[2]
    middle = low(normalize(inputs + attended, gains[0], biases[3]))
    hidden = low_back(product(middle, w_in)) + ffn_bias
    active = low(jax.nn.gelu(hidden, approximate=False))
    branch = low_back(product(active, w_back)) + biases[4]
    return normalize(middle + branch, gains[1], biases[5])

def run_section(inputs, segments, params):

    def group_forward(group_input, group_segments, group_params):
        return encoder_layer(group_input, group_segments, *group_params)
    checked = jax.checkpoint(group_forward)

    def advance(carried, group_pair):
        return (carried, checked(group_pair[0], group_pair[1], params))
    _, results = lax.scan(advance, jnp.zeros((), jnp.float32), (inputs, segments))
    return results

def reference(block_input, seq_lengths, w_qkv, w_out, w_in, w_back, gains, biases, ffn_bias, out_grad):
    groups_all = MICRO * GROUPS
    inputs = block_input.astype(jnp.float32).reshape(groups_all, GROUP_ROWS, D)
    segments = jax.vmap(lambda seq_lens: segment_ids(seq_lens, GROUP_ROWS))(seq_lengths.reshape(groups_all, SEQS))
    live_rows = (segments < SEQS).astype(jnp.float32)
    weights_all = (w_qkv, w_out, w_in, w_back, gains, biases, ffn_bias)
    params_one = tuple((weight[0].astype(jnp.float32) for weight in weights_all))
    params_two = tuple((weight[1].astype(jnp.float32) for weight in weights_all))

    def section_map(section_in, params):
        return run_section(section_in, segments, params)
    first_out, back_one = jax.vjp(section_map, inputs, params_one)
    second_in = low(first_out)
    second_out, back_two = jax.vjp(section_map, second_in, params_two)
    cotangent = out_grad.astype(jnp.float32).reshape(groups_all, GROUP_ROWS, D) * live_rows[:, :, None]
    middle_grad, grads_two = back_two(cotangent)
    input_grad, grads_one = back_one(low(middle_grad))

    def joined(position):
        return jnp.stack([grads_one[position], grads_two[position]])
    layer_outputs = jnp.stack([first_out, second_out]).reshape(LAYERS, MICRO, TOKENS, D)
    input_grads = jnp.stack([input_grad, middle_grad]).reshape(LAYERS, MICRO, TOKENS, D)
    return (layer_outputs, input_grads, joined(0), joined(1), joined(2), joined(3), joined(4), joined(5), joined(6))
```

```python
import jax
import jax.numpy as jnp
from jax import lax
from jax.experimental import pallas as pl
from jax.experimental.pallas import tpu as pltpu
from jax.sharding import PartitionSpec as P

HEAD_DIM = 64
AXES = ("section", "dp", "tensor")
LOW = jnp.bfloat16
WIDE = jnp.float32


def move(value, target):
    sections, copies, ranks = (lax.axis_size(axis) for axis in AXES)
    pairs = []
    for s in range(sections):
        for d in range(copies):
            for t in range(ranks):
                goal = target(s, d, t)
                if goal is not None:
                    pairs.append(
                        ((s * copies + d) * ranks + t, (goal[0] * copies + goal[1]) * ranks + goal[2])
                    )
    return lax.ppermute(value, AXES, pairs)


def to_other_core(value):
    return move(value, lambda s, d, t: (s, d ^ 1, t))


def by_core(core, kept, received, axis):
    first = jnp.where(core == 0, kept, received)
    second = jnp.where(core == 0, received, kept)
    return jnp.stack([first, second], axis=axis)


def matmul(lhs_mat, rhs_mat):
    return jnp.dot(lhs_mat, rhs_mat, preferred_element_type=WIDE)


def lhs_inner(lhs_mat, rhs_mat):
    return lax.dot_general(
        lhs_mat, rhs_mat, (((0,), (0,)), ((), ())), preferred_element_type=WIDE
    )


def rhs_inner(lhs_mat, rhs_mat):
    return lax.dot_general(
        lhs_mat, rhs_mat, (((1,), (1,)), ((), ())), preferred_element_type=WIDE
    )


def core_sum(partial):
    low = partial.astype(LOW)
    return low.astype(WIDE) + to_other_core(low).astype(WIDE)


def norm_parts(summed):
    centered = summed - jnp.mean(summed, axis=-1, keepdims=True)
    variance = jnp.mean(centered * centered, axis=-1, keepdims=True)
    scale = lax.rsqrt(variance + 1e-05)
    return centered * scale, scale


def norm_backward(summed, gain_row, grad):
    unit, scale = norm_parts(summed)
    gain_grad = jnp.sum(grad * unit, axis=0)
    bias_grad = jnp.sum(grad, axis=0)
    inner = grad * gain_row
    result = scale * (
        inner
        - jnp.mean(inner, axis=-1, keepdims=True)
        - unit * jnp.mean(inner * unit, axis=-1, keepdims=True)
    )
    return result, gain_grad, bias_grad


def gelu_pair(values):
    below = 0.5 * (1.0 + lax.erf(values * (0.5**0.5)))
    density = jnp.exp(-0.5 * values * values) * (0.3989422804014327)
    return values * below, below + values * density


def segment_ids(seq_lens, row_count):
    seq_ends = jnp.cumsum(seq_lens)
    positions = jnp.arange(row_count, dtype=jnp.int32)
    return jnp.sum((positions[:, None] >= seq_ends[None, :]).astype(jnp.int32), axis=1)


def flash_params(flops, transcendentals, moved):
    return dict(
        cost_estimate=pl.CostEstimate(
            flops=flops, transcendentals=transcendentals, bytes_accessed=moved
        ),
        compiler_params=pltpu.CompilerParams(vmem_limit_bytes=48 * 1024 * 1024),
    )


def head_lanes(values, head):
    lane = lax.broadcasted_iota(jnp.int32, values.shape, 1)
    return jnp.where((lane // HEAD_DIM) == head, values, jnp.zeros_like(values))


def keys_by_queries(keys, queries):
    return lax.dot_general(keys, queries, (((1,), (1,)), ((), ())), preferred_element_type=WIDE)


def forward_kernel(query_ref, key_ref, value_ref, seg_key_ref, seg_query_ref, out_ref, logsum_ref):
    allowed = seg_key_ref[...] == seg_query_ref[...]
    queries = query_ref[...] * jnp.asarray(HEAD_DIM ** (-0.5), LOW)
    heads = queries.shape[1] // HEAD_DIM
    parts = []
    for head in range(heads):
        scores = keys_by_queries(key_ref[...], head_lanes(queries, head))
        scores = jnp.where(allowed, scores, -1000000000.0)
        highest = jnp.max(scores, axis=0, keepdims=True)
        raised = jnp.exp(scores - highest)
        totals = jnp.sum(raised, axis=0, keepdims=True)
        context = lhs_inner(value_ref[...], raised.astype(LOW))
        rows = slice(head * HEAD_DIM, (head + 1) * HEAD_DIM)
        parts.append(context[rows] / totals)
        logsum_ref[0, head : head + 1, :] = highest + jnp.log(totals)
    out_ref[...] = jnp.concatenate(parts, axis=0).T.astype(LOW)


def backward_kernel(
    query_ref, key_ref, value_ref, seg_key_ref, seg_query_ref, logsum_ref, grad_ref,
    out_ref, sum_ref, key_grad, value_grad,
):
    block = pl.program_id(1)
    size, lanes = query_ref.shape
    heads = lanes // HEAD_DIM
    factor = HEAD_DIM ** (-0.5)

    @pl.when(block == 0)
    def _():
        key_grad[...] = jnp.zeros_like(key_grad)
        value_grad[...] = jnp.zeros_like(value_grad)
        sum_ref[...] = jnp.zeros_like(sum_ref)

    allowed = seg_key_ref[...] == seg_query_ref[...]
    queries = query_ref[...] * jnp.asarray(factor, LOW)
    grads = grad_ref[...]
    weight_low, score_low, query_heads, grad_heads, query_parts = [], [], [], [], []
    for head in range(heads):
        query_head, grad_head = head_lanes(queries, head), head_lanes(grads, head)
        scores = jnp.where(allowed, keys_by_queries(key_ref[...], query_head), -1000000000.0)
        weights = jnp.exp(scores - logsum_ref[0, head : head + 1, :])
        weight_grad = keys_by_queries(value_ref[...], grad_head)
        centre = jnp.sum(weight_grad * weights, axis=0, keepdims=True)
        score_grad = (weights * (weight_grad - centre)).astype(LOW)
        rows = slice(head * HEAD_DIM, (head + 1) * HEAD_DIM)
        query_parts.append(lhs_inner(key_ref[...], score_grad)[rows] * factor)
        weight_low.append(weights.astype(LOW))
        score_low.append(score_grad)
        query_heads.append(query_head)
        grad_heads.append(grad_head)
    key_grad[...] += matmul(jnp.concatenate(score_low, axis=1), jnp.concatenate(query_heads, axis=0))
    value_grad[...] += matmul(jnp.concatenate(weight_low, axis=1), jnp.concatenate(grad_heads, axis=0))
    query_grad = jnp.concatenate(query_parts, axis=0).T
    out_ref[pl.ds(pl.multiple_of(block * size, size), size), :lanes] = query_grad.astype(LOW)
    sum_ref[0, 0:1, :] += jnp.sum(query_grad, axis=0, keepdims=True)

    @pl.when(block == pl.num_programs(1) - 1)
    def _():
        out_ref[:, lanes : 2 * lanes] = key_grad[...].astype(LOW)
        out_ref[:, 2 * lanes :] = value_grad[...].astype(LOW)
        sum_ref[0, 1:2, :] = jnp.sum(value_grad[...], axis=0, keepdims=True)


def attention_specs(rows, lanes, size):
    return [
        pl.BlockSpec((size, lanes), lambda pair, block: (block, 3 * pair)),
        pl.BlockSpec((rows, lanes), lambda pair, block: (0, 3 * pair + 1)),
        pl.BlockSpec((rows, lanes), lambda pair, block: (0, 3 * pair + 2)),
        pl.BlockSpec((rows, 1), lambda pair, block: (0, 0)),
        pl.BlockSpec((1, size), lambda pair, block: (0, block)),
    ]


def attend_forward(packed, segments, lanes):
    rows = packed.shape[0]
    pairs = packed.shape[1] // (3 * lanes)
    heads = lanes // HEAD_DIM
    size = min(256, rows)
    squares = pairs * heads * rows * rows
    return pl.pallas_call(
        forward_kernel,
        grid=(pairs, rows // size),
        in_specs=attention_specs(rows, lanes, size),
        out_specs=[
            pl.BlockSpec((size, lanes), lambda pair, block: (block, pair)),
            pl.BlockSpec((1, heads, size), lambda pair, block: (pair, 0, block)),
        ],
        out_shape=[
            jax.ShapeDtypeStruct((rows, pairs * lanes), LOW),
            jax.ShapeDtypeStruct((pairs, heads, rows), WIDE),
        ],
        **flash_params(8 * squares * HEAD_DIM, squares, 4 * rows * pairs * lanes * 2),
    )(packed, packed, packed, segments[:, None], segments[None, :])


def attend_backward(packed, segments, logsums, context_grad, lanes):
    rows = packed.shape[0]
    pairs = packed.shape[1] // (3 * lanes)
    heads = lanes // HEAD_DIM
    size = min(256, rows)
    squares = pairs * heads * rows * rows
    return pl.pallas_call(
        backward_kernel,
        grid=(pairs, rows // size),
        in_specs=attention_specs(rows, lanes, size)
        + [
            pl.BlockSpec((1, heads, size), lambda pair, block: (pair, 0, block)),
            pl.BlockSpec((size, lanes), lambda pair, block: (block, pair)),
        ],
        out_specs=[
            pl.BlockSpec((rows, 3 * lanes), lambda pair, block: (0, pair)),
            pl.BlockSpec((1, 2, lanes), lambda pair, block: (pair, 0, 0)),
        ],
        out_shape=[
            jax.ShapeDtypeStruct((rows, pairs * 3 * lanes), LOW),
            jax.ShapeDtypeStruct((pairs, 2, lanes), WIDE),
        ],
        scratch_shapes=[pltpu.VMEM((rows, lanes), WIDE), pltpu.VMEM((rows, lanes), WIDE)],
        **flash_params(20 * squares * HEAD_DIM, squares, 8 * rows * pairs * lanes * 2),
    )(packed, packed, packed, segments[:, None], segments[None, :], logsums, context_grad)


def pair_columns(packed, head_half, lanes, back=False):
    ranks = lanes // head_half
    if ranks == 1:
        return packed
    order = (3, ranks) if back else (ranks, 3)
    shaped = packed.reshape(packed.shape[0], -1, order[0], order[1], head_half)
    return jnp.swapaxes(shaped, 2, 3).reshape(packed.shape)


def layer_forward(rows, segments, weights, small):
    w_qkv, w_out, w_in, w_back = weights
    gains, biases, offset, inner_bias, head_half = small
    lanes = max(head_half, 128)
    packed = (rhs_inner(rows, w_qkv) + offset).astype(LOW)
    packed = pair_columns(packed, head_half, lanes)
    context, logsums = attend_forward(packed, segments, lanes)
    first_sum = rows.astype(WIDE) + core_sum(matmul(context, w_out)) + biases[2]
    middle = (norm_parts(first_sum)[0] * gains[0] + biases[3]).astype(LOW)
    active, slope = gelu_pair(rhs_inner(middle, w_in) + inner_bias)
    active, slope = active.astype(LOW), slope.astype(LOW)
    second_sum = middle.astype(WIDE) + core_sum(matmul(active, w_back)) + biases[4]
    result = norm_parts(second_sum)[0] * gains[1] + biases[5]
    return result, (rows, packed, logsums, context, first_sum, middle, active, slope, second_sum)


def slab_grads(hidden, features, chips):
    cut = features.shape[1] // chips
    return [lhs_inner(hidden, features[:, k * cut : (k + 1) * cut]).astype(LOW) for k in range(chips)]


def layer_backward(saved, segments, grad_rows, weights, small, chips):
    w_qkv, w_out, w_in, w_back = weights
    gains, biases, _, _, head_half = small
    lanes = max(head_half, 128)
    rows, packed, logsums, context, first_sum, middle, active, slope, second_sum = saved
    second_grad, gain_two, bias_two = norm_backward(second_sum, gains[1], grad_rows.astype(WIDE))
    branch_grad = second_grad.astype(LOW)
    hidden_grad = rhs_inner(branch_grad, w_back) * slope.astype(WIDE)
    hidden_low = hidden_grad.astype(LOW)
    middle_grad = second_grad + core_sum(matmul(hidden_low, w_in))
    back_grad = slab_grads(active, branch_grad, chips)
    in_grad = slab_grads(hidden_low, middle, chips)
    first_grad, gain_one, bias_one = norm_backward(first_sum, gains[0], middle_grad)
    attended_grad = first_grad.astype(LOW)
    context_grad = rhs_inner(attended_grad, w_out).astype(LOW)
    packed_low, sums = attend_backward(packed, segments, logsums, context_grad, lanes)
    packed_low = pair_columns(packed_low, head_half, lanes, back=True)
    input_grad = first_grad + core_sum(matmul(packed_low, w_qkv))
    out_grad = slab_grads(context, attended_grad, chips)
    qkv_grad = slab_grads(packed_low, rows, chips)
    shared = (gain_one, gain_two, jnp.sum(first_grad, axis=0), bias_one, jnp.sum(second_grad, axis=0), bias_two)
    own = (sums[:, 0].reshape(-1), sums[:, 1].reshape(-1), jnp.sum(hidden_grad, axis=0))
    return input_grad, (qkv_grad, out_grad, in_grad, back_grad), shared, own


def on_device(
    block_input, seq_lengths, w_qkv, w_out, w_in, w_back, gains, biases, ffn_bias, out_grad
):
    ranks = lax.axis_size("tensor")
    copies = lax.axis_size("dp")
    chips = copies // 2
    section = lax.axis_index("section")
    copy_at = lax.axis_index("dp")
    rank = lax.axis_index("tensor")
    core = copy_at % 2
    chip = copy_at // 2
    micro_count, own_rows, width = block_input.shape
    repeats = ranks // micro_count
    local = gains.shape[-1]
    counted = (rank % repeats) == 0

    def relative(value):
        parts = value.reshape(value.shape[:-1] + (chips, width // chips))
        axis = parts.ndim - 2
        ordered = [lax.dynamic_index_in_dim(parts, chip ^ k, axis, keepdims=False) for k in range(chips)]
        return jnp.concatenate(ordered, axis=-1)

    def fetch_rows(block):
        parts = block.reshape(micro_count, 2, own_rows // 2, width)
        kept = lax.dynamic_index_in_dim(parts, core, 1, keepdims=False)
        given = lax.dynamic_index_in_dim(parts, 1 - core, 1, keepdims=False)
        received = move(given, lambda s, d, t: (s, d ^ 1, t) if d % 2 == s else None)
        mine = jnp.where(core == section, kept, received)
        mine = jnp.repeat(mine, repeats, axis=0) if repeats > 1 else mine
        mine = lax.all_to_all(mine, "tensor", split_axis=0, concat_axis=0, tiled=True)
        whole = by_core(core, mine, to_other_core(mine), 1)
        return relative(whole.reshape(ranks * own_rows, width))

    def return_rows(first, second):
        chosen = relative(jnp.where(core == 0, first, second).astype(LOW))
        chosen = chosen.reshape(ranks, own_rows, width)
        spread = lax.all_to_all(chosen, "tensor", split_axis=0, concat_axis=0, tiled=True)
        spread = spread.reshape(micro_count, repeats, own_rows, width)[:, 0]
        placed = move(spread, lambda s, d, t: (d % 2, (d // 2) * 2 + s, t))
        return placed.astype(WIDE)[None]

    def gather_weight(halves):
        kept = lax.dynamic_index_in_dim(halves, core, 0, keepdims=False)
        given = lax.dynamic_index_in_dim(halves, 1 - core, 0, keepdims=False)
        received = to_other_core(given)
        own = jnp.where(
            core == 0,
            jnp.concatenate([kept, received], axis=1),
            jnp.concatenate([received, kept], axis=1),
        )
        upward, downward = [own], [own]
        for _ in range(1, ranks):
            upward.append(move(upward[-1], lambda s, d, t: (s, d, t + 1) if t + 1 < ranks else None))
            downward.append(move(downward[-1], lambda s, d, t: (s, d, t - 1) if t > 0 else None))
        item = jnp.zeros((ranks,) + own.shape, LOW)
        item = lax.dynamic_update_index_in_dim(item, own, rank, 0)
        for j in range(1, ranks):
            arrived = jnp.where(rank >= j, upward[j], downward[ranks - j])
            item = lax.dynamic_update_index_in_dim(item, arrived, (rank + ranks - j) % ranks, 0)
        across = move(item, lambda s, d, t: (1 - s, d, t))
        along = [move(item, lambda s, d, t: (s, d ^ (2 * k), t)) for k in range(1, chips)]
        cut = ranks // 2
        far = []
        for k in range(1, chips):
            upper = move(across[:cut], lambda s, d, t: (s, d ^ (2 * k), t))
            lower = move(along[k - 1][cut:], lambda s, d, t: (1 - s, d, t))
            far.append(jnp.concatenate([upper, lower], axis=0))
        mine, other = [item] + along, [across] + far
        result = []
        for layer in range(2):
            slabs = [jnp.where(section == layer, m, o) for m, o in zip(mine, other)]
            result.append(jnp.concatenate(slabs, axis=2))
        return result

    def fold(parts, layer):
        cut = ranks // 4
        off = lambda s: s != layer
        near = parts[0][cut:].astype(WIDE)
        uppers = []
        for k in range(1, chips):
            sent = move(parts[k][:cut], lambda s, d, t: (layer, d, t) if off(s) else None)
            uppers.append((parts[k][:cut].astype(WIDE) + sent.astype(WIDE)).astype(LOW))
            got = move(parts[k][cut:], lambda s, d, t: (s, d ^ (2 * k), t) if off(s) else None)
            near = near + got.astype(WIDE)
        near = jnp.concatenate([parts[0][:cut], near.astype(LOW)], axis=0)
        total = near.astype(WIDE)
        total = total + move(near, lambda s, d, t: (layer, d, t) if off(s) else None).astype(WIDE)
        for k in range(1, chips):
            whole = jnp.concatenate([uppers[k - 1], parts[k][cut:]], axis=0)
            got = move(whole, lambda s, d, t: (s, d ^ (2 * k), t) if not off(s) else None)
            total = total + got.astype(WIDE)
        return total.astype(LOW)

    def reduce_grad(first, second):
        folded = []
        for layer, slabs in enumerate((first, second)):
            slabs = [slab.reshape(ranks, -1, slab.shape[1]) for slab in slabs]
            if repeats > 1:
                slabs = [jnp.where(counted, slab, jnp.zeros((), LOW)) for slab in slabs]
            folded.append(fold(slabs, layer))
        chosen = jnp.where(section == 0, folded[0], folded[1])
        shard = lax.psum_scatter(chosen, "tensor", scatter_dimension=0, tiled=False).astype(LOW)
        shard = shard.reshape(shard.shape[0], 2, local)
        kept = lax.dynamic_index_in_dim(shard, core, 1, keepdims=False)
        given = lax.dynamic_index_in_dim(shard, 1 - core, 1, keepdims=False)
        return by_core(core, kept, to_other_core(given), 0).astype(WIDE)

    rows = fetch_rows(block_input)
    head_half = w_qkv.shape[-1] // 2
    hidden_half = w_in.shape[-1] // 2
    in_first = jnp.moveaxis(w_in[0].reshape(local, 2, hidden_half), 0, 2)
    qkv_first = jnp.transpose(w_qkv[0].reshape(local, 3, 2, head_half), (2, 1, 3, 0))
    qkv_first = qkv_first.reshape(2, 3 * head_half, local)
    out_first = w_out[0].reshape(2, head_half, local)
    attention_all = gather_weight(jnp.concatenate([qkv_first, out_first], axis=1))
    in_all = gather_weight(in_first)
    back_all = gather_weight(w_back[0].reshape(2, hidden_half, local))
    weights = [
        (
            attention_all[layer][:, : 3 * head_half].reshape(-1, width),
            attention_all[layer][:, 3 * head_half :].reshape(-1, width),
            in_all[layer].reshape(-1, width),
            back_all[layer].reshape(-1, width),
        )
        for layer in range(2)
    ]

    gain_count, bias_count = gains.shape[1], biases.shape[1]
    packed_small = jnp.concatenate([gains, biases, ffn_bias.reshape(1, -1, local)], axis=1)
    small_all = lax.all_gather(packed_small, ("section", "dp"), axis=0, tiled=True).astype(WIDE)
    small_all = small_all.reshape(2, copies, -1, local)

    def head_columns(row):
        return lax.dynamic_index_in_dim(row.reshape(ranks, 2, -1), core, 1, keepdims=False).reshape(-1)

    small = []
    for layer in range(2):
        table = jnp.moveaxis(small_all[layer, :, : gain_count + bias_count], 0, 1).reshape(-1, width)
        query_bias = head_columns(table[gain_count])
        value_bias = head_columns(table[gain_count + 1])
        query_bias, value_bias = query_bias.reshape(ranks, 1, -1), value_bias.reshape(ranks, 1, -1)
        offset = jnp.concatenate([query_bias, jnp.zeros_like(query_bias), value_bias], axis=1).reshape(-1)
        inner_bias = head_columns(small_all[layer, :, gain_count + bias_count :].reshape(-1))
        table = relative(table)
        small.append((table[:gain_count], table[gain_count:], offset, inner_bias, head_half))

    lengths = lax.all_gather(seq_lengths, "dp", axis=1, tiled=True)
    group_at = chip * 2 + section
    lengths = lengths[rank // repeats, group_at]
    segments = segment_ids(lengths, ranks * own_rows)
    cotangent = fetch_rows(out_grad)
    cotangent = jnp.where((segments < lengths.shape[0])[:, None], cotangent, jnp.zeros((), LOW))

    first_out, first_saved = layer_forward(rows, segments, weights[0], small[0])
    second_out, second_saved = layer_forward(first_out.astype(LOW), segments, weights[1], small[1])
    outputs = return_rows(first_out, second_out)
    second_in, second_grads, second_shared, second_own = layer_backward(
        second_saved, segments, cotangent, weights[1], small[1], chips
    )
    first_in, first_grads, first_shared, first_own = layer_backward(
        first_saved, segments, second_in.astype(LOW), weights[0], small[0], chips
    )
    input_grads = return_rows(first_in, second_in)

    back_shard, in_shard, out_shard, qkv_shard = [
        reduce_grad(first_grads[at], second_grads[at]) for at in (3, 2, 1, 0)
    ]
    qkv_grad = jnp.transpose(qkv_shard.reshape(2, 3, head_half, local), (3, 1, 0, 2)).reshape(local, 3, -1)
    out_grad_w = out_shard.reshape(-1, local)
    in_grad = jnp.transpose(in_shard.reshape(-1, local))
    back_grad = back_shard.reshape(-1, local)

    def spread_columns(row):
        blocks = row.reshape(ranks, 1, -1)
        both = jnp.where(jnp.arange(2)[None, :, None] == core, blocks, 0.0)
        return both.reshape(-1, width)

    tables = []
    for shared, own in ((first_shared, first_own), (second_shared, second_own)):
        common = jnp.where(core == 0, relative(jnp.stack(shared)), 0.0)
        tables.append(
            jnp.concatenate(
                [common[:2], spread_columns(own[0]), spread_columns(own[1]), common[2:], spread_columns(own[2])]
            )
        )
    table = jnp.stack(tables)
    table = jnp.where(counted, table, 0.0) if repeats > 1 else table
    table = lax.dynamic_index_in_dim(lax.psum(table, AXES), section, 0, keepdims=False)
    sliced = lax.dynamic_slice_in_dim(table[: gain_count + bias_count], copy_at * local, local, 1)
    inner = lax.dynamic_index_in_dim(
        table[gain_count + bias_count :].reshape(copies, -1), copy_at, 0, keepdims=False
    )
    return (
        outputs,
        input_grads,
        qkv_grad[None],
        out_grad_w[None],
        in_grad[None],
        back_grad[None],
        sliced[None, :gain_count],
        sliced[None, gain_count:],
        inner[None],
    )


def solution(mesh):
    return jax.shard_map(
        on_device,
        mesh=mesh,
        in_specs=(
            P(None, ("dp", "tensor"), None),
            P(None, "dp", None),
            P("section", "dp", None, "tensor"),
            P("section", "tensor", "dp"),
            P("section", "dp", "tensor"),
            P("section", "tensor", "dp"),
            P("section", None, "dp"),
            P("section", None, "dp"),
            P("section", "dp"),
            P(None, ("dp", "tensor"), None),
        ),
        out_specs=(
            P("section", None, ("dp", "tensor"), None),
            P("section", None, ("dp", "tensor"), None),
            P("section", "dp", None, "tensor"),
            P("section", "tensor", "dp"),
            P("section", "dp", "tensor"),
            P("section", "tensor", "dp"),
            P("section", None, "dp"),
            P("section", None, "dp"),
            P("section", "dp"),
        ),
        check_vma=False,
    )
```

```python
import jax
import jax.numpy as jnp
from jax import lax
from jax.experimental import pallas as pl
from jax.experimental.pallas import tpu as pltpu
from jax.sharding import PartitionSpec as P

HEAD_DIM = 64
AXES = ("section", "dp", "tensor")
LOW = jnp.bfloat16
WIDE = jnp.float32


def move(value, target):
    sections, copies, ranks = (lax.axis_size(axis) for axis in AXES)
    pairs = []
    for s in range(sections):
        for d in range(copies):
            for t in range(ranks):
                goal = target(s, d, t)
                if goal is not None:
                    pairs.append(
                        ((s * copies + d) * ranks + t, (goal[0] * copies + goal[1]) * ranks + goal[2])
                    )
    return lax.ppermute(value, AXES, pairs)


def to_other_core(value):
    return move(value, lambda s, d, t: (s, d ^ 1, t))


def by_core(core, kept, received, axis):
    return jnp.where(
        core == 0,
        jnp.concatenate([kept, received], axis=axis),
        jnp.concatenate([received, kept], axis=axis),
    )


def choose(place, options):
    chosen = options[0]
    for at, option in enumerate(options[1:], 1):
        chosen = jnp.where(place == at, option, chosen)
    return chosen


def after(value, *others):
    return lax.optimization_barrier((value,) + others)[0]


def matmul(lhs_mat, rhs_mat):
    return jnp.dot(lhs_mat, rhs_mat, preferred_element_type=WIDE)


def lhs_inner(lhs_mat, rhs_mat):
    return lax.dot_general(
        lhs_mat, rhs_mat, (((0,), (0,)), ((), ())), preferred_element_type=WIDE
    )


def rhs_inner(lhs_mat, rhs_mat):
    return lax.dot_general(
        lhs_mat, rhs_mat, (((1,), (1,)), ((), ())), preferred_element_type=WIDE
    )


def core_sum(partial):
    low = partial.astype(LOW)
    return low.astype(WIDE) + to_other_core(low).astype(WIDE)


def norm_parts(summed):
    centered = summed - jnp.mean(summed, axis=-1, keepdims=True)
    variance = jnp.mean(centered * centered, axis=-1, keepdims=True)
    scale = lax.rsqrt(variance + 1e-05)
    return centered * scale, scale


def norm_backward(summed, gain_row, grad):
    unit, scale = norm_parts(summed)
    gain_grad = jnp.sum(grad * unit, axis=0)
    bias_grad = jnp.sum(grad, axis=0)
    inner = grad * gain_row
    result = scale * (
        inner
        - jnp.mean(inner, axis=-1, keepdims=True)
        - unit * jnp.mean(inner * unit, axis=-1, keepdims=True)
    )
    return result, gain_grad, bias_grad


def gelu_pair(values):
    below = 0.5 * (1.0 + lax.erf(values * (0.5**0.5)))
    density = jnp.exp(-0.5 * values * values) * (0.3989422804014327)
    return values * below, below + values * density


def segment_ids(seq_lens, row_count):
    seq_ends = jnp.cumsum(seq_lens)
    positions = jnp.arange(row_count, dtype=jnp.int32)
    return jnp.sum((positions[:, None] >= seq_ends[None, :]).astype(jnp.int32), axis=1)


def flash_params(flops, transcendentals, moved):
    return dict(
        cost_estimate=pl.CostEstimate(
            flops=flops, transcendentals=transcendentals, bytes_accessed=moved
        ),
        compiler_params=pltpu.CompilerParams(vmem_limit_bytes=48 * 1024 * 1024),
    )


def head_lanes(values, head):
    lane = lax.broadcasted_iota(jnp.int32, values.shape, 1)
    return jnp.where((lane // HEAD_DIM) == head, values, jnp.zeros_like(values))


def keys_by_queries(keys, queries):
    return lax.dot_general(keys, queries, (((1,), (1,)), ((), ())), preferred_element_type=WIDE)


def forward_kernel(query_ref, key_ref, value_ref, seg_key_ref, seg_query_ref, out_ref, logsum_ref):
    allowed = seg_key_ref[...] == seg_query_ref[...]
    queries = query_ref[...] * jnp.asarray(HEAD_DIM ** (-0.5), LOW)
    heads = queries.shape[1] // HEAD_DIM
    parts = []
    for head in range(heads):
        scores = keys_by_queries(key_ref[...], head_lanes(queries, head))
        scores = jnp.where(allowed, scores, -1000000000.0)
        highest = jnp.max(scores, axis=0, keepdims=True)
        raised = jnp.exp(scores - highest)
        totals = jnp.sum(raised, axis=0, keepdims=True)
        context = lhs_inner(value_ref[...], raised.astype(LOW))
        rows = slice(head * HEAD_DIM, (head + 1) * HEAD_DIM)
        parts.append(context[rows] / totals)
        logsum_ref[0, head : head + 1, :] = highest + jnp.log(totals)
    out_ref[...] = jnp.concatenate(parts, axis=0).T.astype(LOW)


def backward_kernel(
    query_ref, key_ref, value_ref, seg_key_ref, seg_query_ref, logsum_ref, grad_ref,
    out_ref, sum_ref, key_grad, value_grad,
):
    block = pl.program_id(1)
    size, lanes = query_ref.shape
    heads = lanes // HEAD_DIM
    factor = HEAD_DIM ** (-0.5)

    @pl.when(block == 0)
    def _():
        key_grad[...] = jnp.zeros_like(key_grad)
        value_grad[...] = jnp.zeros_like(value_grad)
        sum_ref[...] = jnp.zeros_like(sum_ref)

    allowed = seg_key_ref[...] == seg_query_ref[...]
    queries = query_ref[...] * jnp.asarray(factor, LOW)
    grads = grad_ref[...]
    weight_low, score_low, query_heads, grad_heads, query_parts = [], [], [], [], []
    for head in range(heads):
        query_head, grad_head = head_lanes(queries, head), head_lanes(grads, head)
        scores = jnp.where(allowed, keys_by_queries(key_ref[...], query_head), -1000000000.0)
        weights = jnp.exp(scores - logsum_ref[0, head : head + 1, :])
        weight_grad = keys_by_queries(value_ref[...], grad_head)
        centre = jnp.sum(weight_grad * weights, axis=0, keepdims=True)
        score_grad = (weights * (weight_grad - centre)).astype(LOW)
        rows = slice(head * HEAD_DIM, (head + 1) * HEAD_DIM)
        query_parts.append(lhs_inner(key_ref[...], score_grad)[rows] * factor)
        weight_low.append(weights.astype(LOW))
        score_low.append(score_grad)
        query_heads.append(query_head)
        grad_heads.append(grad_head)
    key_grad[...] += matmul(jnp.concatenate(score_low, axis=1), jnp.concatenate(query_heads, axis=0))
    value_grad[...] += matmul(jnp.concatenate(weight_low, axis=1), jnp.concatenate(grad_heads, axis=0))
    query_grad = jnp.concatenate(query_parts, axis=0).T
    out_ref[pl.ds(pl.multiple_of(block * size, size), size), :lanes] = query_grad.astype(LOW)
    sum_ref[0, 0:1, :] += jnp.sum(query_grad, axis=0, keepdims=True)

    @pl.when(block == pl.num_programs(1) - 1)
    def _():
        out_ref[:, lanes : 2 * lanes] = key_grad[...].astype(LOW)
        out_ref[:, 2 * lanes :] = value_grad[...].astype(LOW)
        sum_ref[0, 1:2, :] = jnp.sum(value_grad[...], axis=0, keepdims=True)


def attention_specs(rows, lanes, size):
    return [
        pl.BlockSpec((size, lanes), lambda pair, block: (block, 3 * pair)),
        pl.BlockSpec((rows, lanes), lambda pair, block: (0, 3 * pair + 1)),
        pl.BlockSpec((rows, lanes), lambda pair, block: (0, 3 * pair + 2)),
        pl.BlockSpec((rows, 1), lambda pair, block: (0, 0)),
        pl.BlockSpec((1, size), lambda pair, block: (0, block)),
    ]


def attend_forward(packed, segments, lanes):
    rows = packed.shape[0]
    pairs = packed.shape[1] // (3 * lanes)
    heads = lanes // HEAD_DIM
    size = min(256, rows)
    squares = pairs * heads * rows * rows
    return pl.pallas_call(
        forward_kernel,
        grid=(pairs, rows // size),
        in_specs=attention_specs(rows, lanes, size),
        out_specs=[
            pl.BlockSpec((size, lanes), lambda pair, block: (block, pair)),
            pl.BlockSpec((1, heads, size), lambda pair, block: (pair, 0, block)),
        ],
        out_shape=[
            jax.ShapeDtypeStruct((rows, pairs * lanes), LOW),
            jax.ShapeDtypeStruct((pairs, heads, rows), WIDE),
        ],
        **flash_params(8 * squares * HEAD_DIM, squares, 4 * rows * pairs * lanes * 2),
    )(packed, packed, packed, segments[:, None], segments[None, :])


def attend_backward(packed, segments, logsums, context_grad, lanes):
    rows = packed.shape[0]
    pairs = packed.shape[1] // (3 * lanes)
    heads = lanes // HEAD_DIM
    size = min(256, rows)
    squares = pairs * heads * rows * rows
    return pl.pallas_call(
        backward_kernel,
        grid=(pairs, rows // size),
        in_specs=attention_specs(rows, lanes, size)
        + [
            pl.BlockSpec((1, heads, size), lambda pair, block: (pair, 0, block)),
            pl.BlockSpec((size, lanes), lambda pair, block: (block, pair)),
        ],
        out_specs=[
            pl.BlockSpec((rows, 3 * lanes), lambda pair, block: (0, pair)),
            pl.BlockSpec((1, 2, lanes), lambda pair, block: (pair, 0, 0)),
        ],
        out_shape=[
            jax.ShapeDtypeStruct((rows, pairs * 3 * lanes), LOW),
            jax.ShapeDtypeStruct((pairs, 2, lanes), WIDE),
        ],
        scratch_shapes=[pltpu.VMEM((rows, lanes), WIDE), pltpu.VMEM((rows, lanes), WIDE)],
        **flash_params(20 * squares * HEAD_DIM, squares, 8 * rows * pairs * lanes * 2),
    )(packed, packed, packed, segments[:, None], segments[None, :], logsums, context_grad)


def pair_columns(packed, head_half, lanes, back=False):
    ranks = lanes // head_half
    if ranks == 1:
        return packed
    order = (3, ranks) if back else (ranks, 3)
    shaped = packed.reshape(packed.shape[0], -1, order[0], order[1], head_half)
    return jnp.swapaxes(shaped, 2, 3).reshape(packed.shape)


def layer_forward(rows, segments, weights, small):
    w_qkv, w_out, w_in, w_back = weights
    gains, biases, offset, inner_bias, head_half = small
    lanes = max(head_half, 128)
    packed = (rhs_inner(rows, w_qkv) + offset).astype(LOW)
    packed = pair_columns(packed, head_half, lanes)
    context, logsums = attend_forward(packed, segments, lanes)
    first_sum = rows.astype(WIDE) + core_sum(matmul(context, w_out)) + biases[2]
    middle = (norm_parts(first_sum)[0] * gains[0] + biases[3]).astype(LOW)
    active, slope = gelu_pair(rhs_inner(middle, w_in) + inner_bias)
    active, slope = active.astype(LOW), slope.astype(LOW)
    second_sum = middle.astype(WIDE) + core_sum(matmul(active, w_back)) + biases[4]
    result = norm_parts(second_sum)[0] * gains[1] + biases[5]
    return result, (rows, packed, logsums, context, first_sum, middle, active, slope, second_sum)


def slab_grads(hidden, features, chips):
    cut = features.shape[1] // chips
    return [lhs_inner(hidden, features[:, k * cut : (k + 1) * cut]).astype(LOW) for k in range(chips)]


def backward_hidden(saved, grad_rows, weights, small):
    _, _, w_in, w_back = weights
    gains = small[0]
    middle, active, slope, second_sum = saved[5:]
    second_grad, gain_two, bias_two = norm_backward(second_sum, gains[1], grad_rows.astype(WIDE))
    branch_grad = second_grad.astype(LOW)
    hidden_grad = rhs_inner(branch_grad, w_back) * slope.astype(WIDE)
    hidden_low = hidden_grad.astype(LOW)
    middle_grad = second_grad + core_sum(matmul(hidden_low, w_in))
    sums = (gain_two, jnp.sum(second_grad, axis=0), bias_two, jnp.sum(hidden_grad, axis=0))
    return middle_grad, branch_grad, hidden_low, sums


def backward_attention(saved, segments, middle_grad, weights, small):
    _, w_out, _, _ = weights
    gains, head_half = small[0], small[4]
    _, packed, logsums, _, first_sum = saved[:5]
    first_grad, gain_one, bias_one = norm_backward(first_sum, gains[0], middle_grad)
    attended_grad = first_grad.astype(LOW)
    context_grad = rhs_inner(attended_grad, w_out).astype(LOW)
    lanes = max(head_half, 128)
    packed_low, column_sums = attend_backward(packed, segments, logsums, context_grad, lanes)
    packed_low = pair_columns(packed_low, head_half, lanes, back=True)
    sums = (gain_one, jnp.sum(first_grad, axis=0), bias_one) + tuple(
        column_sums[:, at].reshape(-1) for at in range(2)
    )
    return first_grad, attended_grad, packed_low, sums


def on_device(
    block_input, seq_lengths, w_qkv, w_out, w_in, w_back, gains, biases, ffn_bias, out_grad
):
    ranks = lax.axis_size("tensor")
    copies = lax.axis_size("dp")
    chips = copies // 2
    section = lax.axis_index("section")
    copy_at = lax.axis_index("dp")
    rank = lax.axis_index("tensor")
    core = copy_at % 2
    chip = copy_at // 2
    micro_count, own_rows, width = block_input.shape
    repeats = ranks // micro_count
    local = gains.shape[-1]
    counted = (rank % repeats) == 0

    def relative(value):
        slabs = jnp.split(value, chips, axis=-1)
        return jnp.concatenate([choose(chip ^ k, slabs) for k in range(chips)], axis=-1)

    def fetch_rows(block):
        parts = block.reshape(micro_count, 2, own_rows // 2, width)
        kept = choose(core, (parts[:, 0], parts[:, 1]))
        given = choose(core, (parts[:, 1], parts[:, 0]))
        received = move(given, lambda s, d, t: (s, d ^ 1, t) if d % 2 == s else None)
        mine = jnp.where(core == section, kept, received)
        mine = jnp.repeat(mine, repeats, axis=0) if repeats > 1 else mine
        mine = lax.all_to_all(mine, "tensor", split_axis=0, concat_axis=0, tiled=True)
        whole = by_core(core, mine, to_other_core(mine), 1)
        return relative(whole.reshape(ranks * own_rows, width))

    def return_rows(first, second):
        chosen = relative(jnp.where(core == 0, first, second).astype(LOW))
        chosen = chosen.reshape(ranks, own_rows, width)
        spread = lax.all_to_all(chosen, "tensor", split_axis=0, concat_axis=0, tiled=True)
        spread = spread.reshape(micro_count, repeats, own_rows, width)[:, 0]
        placed = move(spread, lambda s, d, t: (d % 2, (d // 2) * 2 + s, t))
        return placed.astype(WIDE)[None]

    def own_half(halves):
        kept = choose(core, (halves[0], halves[1]))
        given = choose(core, (halves[1], halves[0]))
        return by_core(core, kept, to_other_core(given), 1)

    def over_ranks(own):
        upward, downward = [own], [own]
        for _ in range(1, ranks):
            upward.append(move(upward[-1], lambda s, d, t: (s, d, t + 1) if t + 1 < ranks else None))
            downward.append(move(downward[-1], lambda s, d, t: (s, d, t - 1) if t > 0 else None))
        item = jnp.zeros((ranks,) + own.shape, LOW)
        item = lax.dynamic_update_index_in_dim(item, own, rank, 0)
        for j in range(1, ranks):
            arrived = jnp.where(rank >= j, upward[j], downward[ranks - j])
            item = lax.dynamic_update_index_in_dim(item, arrived, (rank + ranks - j) % ranks, 0)
        return item

    def over_chips(item):
        part = item.shape[0] // 2
        across = move(item, lambda s, d, t: (1 - s, d, t))
        along = [move(item, lambda s, d, t: (s, d ^ (2 * k), t)) for k in range(1, chips)]
        far = []
        for k in range(1, chips):
            upper = move(across[:part], lambda s, d, t: (s, d ^ (2 * k), t))
            lower = move(along[k - 1][part:], lambda s, d, t: (1 - s, d, t))
            far.append(jnp.concatenate([upper, lower], axis=0))
        mine, other = [item] + along, [across] + far
        result = []
        for layer in range(2):
            slabs = [jnp.where(section == layer, m, o) for m, o in zip(mine, other)]
            result.append(jnp.concatenate(slabs, axis=-1))
        return result

    def gather_weight(own):
        return over_chips(over_ranks(own))

    def gather_weight_late(own):
        both = over_ranks(jnp.stack(over_chips(own)))
        return [both[:, layer] for layer in range(2)]

    def along_x(parts):
        slabs = jnp.split(parts, chips, axis=-1)
        total = slabs[0].astype(WIDE)
        for k in range(1, chips):
            total = total + move(slabs[k], lambda s, d, t: (s, d ^ (2 * k), t)).astype(WIDE)
        return total.astype(LOW)

    def slabs_along_x(slabs):
        total = slabs[0].astype(WIDE)
        for k in range(1, chips):
            total = total + move(slabs[k], lambda s, d, t: (s, d ^ (2 * k), t)).astype(WIDE)
        return total.astype(LOW)

    def to_layer(part, layer):
        sent = move(part, lambda s, d, t: (layer, d, t) if s != layer else None)
        return (part.astype(WIDE) + sent.astype(WIDE)).astype(LOW)

    def over_z(parts):
        parts = parts.reshape((ranks, -1) + parts.shape[1:])
        return lax.psum_scatter(parts, "tensor", scatter_dimension=0, tiled=False).astype(LOW)

    def counted_only(slabs):
        return [jnp.where(counted, slab, jnp.zeros((), LOW)) for slab in slabs] if repeats > 1 else slabs

    def finish(shard):
        parts = jnp.split(shard, 2, axis=1)
        kept = choose(core, parts)
        given = choose(core, parts[::-1])
        return by_core(core, kept[None], to_other_core(given)[None], 0).astype(WIDE)

    rows = fetch_rows(block_input)
    head_half = w_qkv.shape[-1] // 2
    hidden_half = w_in.shape[-1] // 2
    in_first = jnp.moveaxis(w_in[0].reshape(local, 2, hidden_half), 0, 2)
    qkv_first = jnp.transpose(w_qkv[0].reshape(local, 3, 2, head_half), (2, 1, 3, 0))
    qkv_first = qkv_first.reshape(2, 3 * head_half, local)
    out_first = w_out[0].reshape(2, head_half, local)
    back_first = w_back[0].reshape(2, hidden_half, local)
    later = hidden_half // 2
    attention_all = gather_weight(own_half(jnp.concatenate([qkv_first, out_first], axis=1)))
    back_own = own_half(back_first)
    in_all = gather_weight(own_half(in_first))
    back_one = gather_weight(back_own[:later])
    back_two = gather_weight_late(back_own[later:])
    back_all = [jnp.concatenate(pair, axis=1) for pair in zip(back_one, back_two)]
    weights = [
        (
            attention_all[layer][:, : 3 * head_half].reshape(-1, width),
            attention_all[layer][:, 3 * head_half :].reshape(-1, width),
            in_all[layer].reshape(-1, width),
            back_all[layer].reshape(-1, width),
        )
        for layer in range(2)
    ]

    gain_count, bias_count = gains.shape[1], biases.shape[1]
    packed_small = jnp.concatenate([gains, biases, ffn_bias.reshape(1, -1, local)], axis=1)
    table_parts = [
        [
            packed_small
            if a == 0 and b == 0
            else move(packed_small, lambda s, d, t: (s ^ a, d ^ b, t))
            for b in range(copies)
        ]
        for a in range(2)
    ]
    table_all = jnp.stack([jnp.stack(row) for row in table_parts])[:, :, 0].astype(WIDE)
    small_all = jnp.stack([choose(section, (table_all[at], table_all[1 - at])) for at in range(2)])
    order = [[at ^ b for b in range(copies)] for at in range(copies)]
    small_all = jnp.stack(
        [choose(copy_at, [small_all[:, order[at][b]] for b in range(copies)]) for at in range(copies)],
        axis=1,
    )

    def head_columns(row):
        halves = row.reshape(ranks, 2, -1)
        return choose(core, (halves[:, 0], halves[:, 1])).reshape(-1)

    small = []
    for layer in range(2):
        table = jnp.moveaxis(small_all[layer, :, : gain_count + bias_count], 0, 1).reshape(-1, width)
        query_bias = head_columns(table[gain_count])
        value_bias = head_columns(table[gain_count + 1])
        query_bias, value_bias = query_bias.reshape(ranks, 1, -1), value_bias.reshape(ranks, 1, -1)
        offset = jnp.concatenate([query_bias, jnp.zeros_like(query_bias), value_bias], axis=1).reshape(-1)
        inner_bias = head_columns(small_all[layer, :, gain_count + bias_count :].reshape(-1))
        table = relative(table)
        small.append((table[:gain_count], table[gain_count:], offset, inner_bias, head_half))

    lengths = jnp.where(core == section, seq_lengths, to_other_core(seq_lengths))[:, 0]
    lengths = lax.dynamic_index_in_dim(lengths, rank // repeats, 0, keepdims=False)
    segments = segment_ids(lengths, ranks * own_rows)
    cotangent = fetch_rows(out_grad)
    cotangent = jnp.where((segments < lengths.shape[0])[:, None], cotangent, jnp.zeros((), LOW))

    first_out, first_saved = layer_forward(rows, segments, weights[0], small[0])
    second_out, second_saved = layer_forward(first_out.astype(LOW), segments, weights[1], small[1])
    outputs = return_rows(first_out, second_out)

    def feed_forward_grads(saved, branch_grad, hidden_low):
        back = counted_only(slab_grads(saved[6], branch_grad, chips))
        inner = counted_only([lhs_inner(hidden_low, saved[5]).astype(LOW)])[0]
        return back, inner

    def attention_grads(saved, attended_grad, packed_low):
        out = slab_grads(saved[3], attended_grad, chips)
        qkv = slab_grads(packed_low, saved[0], chips)
        return counted_only(out), counted_only(qkv)

    middle_grad, branch_grad, hidden_low, second_sums = backward_hidden(
        second_saved, cotangent, weights[1], small[1]
    )
    back_slabs, inner = feed_forward_grads(second_saved, branch_grad, hidden_low)
    back_two = slabs_along_x(back_slabs)
    in_two = over_z(inner)
    first_grad, attended_grad, packed_low, more_sums = backward_attention(
        second_saved, segments, middle_grad, weights[1], small[1]
    )
    second_sums += more_sums
    packed_low = after(packed_low, back_two)
    back_two = to_layer(back_two, 1)
    second_in = first_grad + core_sum(matmul(packed_low, weights[1][0]))
    out_slabs, qkv_slabs = attention_grads(second_saved, attended_grad, packed_low)
    qkv_two, out_two = slabs_along_x(qkv_slabs), slabs_along_x(out_slabs)

    middle_grad, branch_grad, hidden_low, first_sums = backward_hidden(
        first_saved, second_in.astype(LOW), weights[0], small[0]
    )
    middle_grad = after(middle_grad, back_two, in_two, outputs)
    in_two = along_x(in_two)
    back_slabs, inner = feed_forward_grads(first_saved, branch_grad, hidden_low)
    back_one = slabs_along_x(back_slabs)
    in_one = over_z(inner)
    first_grad, attended_grad, packed_low, more_sums = backward_attention(
        first_saved, segments, middle_grad, weights[0], small[0]
    )
    first_sums += more_sums
    packed_low = after(packed_low, qkv_two, out_two, in_two)
    in_two, qkv_two, out_two = to_layer(in_two, 1), to_layer(qkv_two, 1), to_layer(out_two, 1)
    first_in = first_grad + core_sum(matmul(packed_low, weights[0][0]))
    out_slabs, qkv_slabs = attention_grads(first_saved, attended_grad, packed_low)
    back_one = to_layer(back_one, 0)
    qkv_one, out_one = slabs_along_x(qkv_slabs), slabs_along_x(out_slabs)
    input_grads = return_rows(first_in, second_in)
    back_shard = over_z(jnp.where(section == 0, back_one, back_two))
    in_one = to_layer(along_x(in_one), 0)
    in_shard = finish(jnp.where(section == 0, in_one, in_two))
    qkv_one, out_one = to_layer(qkv_one, 0), to_layer(out_one, 0)
    back_shard = finish(back_shard)
    out_shard = finish(over_z(jnp.where(section == 0, out_one, out_two)))
    qkv_shard = finish(over_z(jnp.where(section == 0, qkv_one, qkv_two)))
    qkv_grad = jnp.transpose(qkv_shard.reshape(2, 3, head_half, local), (3, 1, 0, 2)).reshape(local, 3, -1)
    out_grad_w = out_shard.reshape(-1, local)
    in_grad = jnp.transpose(in_shard.reshape(-1, local))
    back_grad = back_shard.reshape(-1, local)

    def spread_columns(row):
        blocks = row.reshape(ranks, 1, -1)
        both = jnp.where(jnp.arange(2)[None, :, None] == core, blocks, 0.0)
        return both.reshape(-1, width)

    tables = []
    for sums in (first_sums, second_sums):
        gain_two, bias_four, bias_five, inner_sum, gain_one, bias_two, bias_three, query_sum, value_sum = sums
        common = jnp.stack([gain_one, gain_two, bias_two, bias_three, bias_four, bias_five])
        common = jnp.where(core == 0, relative(common), 0.0)
        tables.append(
            jnp.concatenate(
                [common[:2], spread_columns(query_sum), spread_columns(value_sum), common[2:], spread_columns(inner_sum)]
            )
        )
    table = jnp.stack(tables)
    table = jnp.where(counted, table, 0.0) if repeats > 1 else table
    table = lax.dynamic_index_in_dim(lax.psum(table, AXES), section, 0, keepdims=False)
    sliced = lax.dynamic_slice_in_dim(table[: gain_count + bias_count], copy_at * local, local, 1)
    inner = lax.dynamic_index_in_dim(
        table[gain_count + bias_count :].reshape(copies, -1), copy_at, 0, keepdims=False
    )
    return (
        outputs,
        input_grads,
        qkv_grad[None],
        out_grad_w[None],
        in_grad[None],
        back_grad[None],
        sliced[None, :gain_count],
        sliced[None, gain_count:],
        inner[None],
    )


def solution(mesh):
    return jax.shard_map(
        on_device,
        mesh=mesh,
        in_specs=(
            P(None, ("dp", "tensor"), None),
            P(None, "dp", None),
            P("section", "dp", None, "tensor"),
            P("section", "tensor", "dp"),
            P("section", "dp", "tensor"),
            P("section", "tensor", "dp"),
            P("section", None, "dp"),
            P("section", None, "dp"),
            P("section", "dp"),
            P(None, ("dp", "tensor"), None),
        ),
        out_specs=(
            P("section", None, ("dp", "tensor"), None),
            P("section", None, ("dp", "tensor"), None),
            P("section", "dp", None, "tensor"),
            P("section", "tensor", "dp"),
            P("section", "dp", "tensor"),
            P("section", "tensor", "dp"),
            P("section", None, "dp"),
            P("section", None, "dp"),
            P("section", "dp"),
        ),
        check_vma=False,
    )
```

```python
import functools

import jax
import jax.numpy as jnp
from jax import lax
from jax.experimental import pallas as pl
from jax.experimental.pallas import tpu as pltpu
from jax.sharding import PartitionSpec as P

HEAD_DIM = 64
AXES = ("section", "dp", "tensor")
LOW = jnp.bfloat16
WIDE = jnp.float32


def move(value, target):
    sections, copies, ranks = (lax.axis_size(axis) for axis in AXES)
    pairs = []
    for s in range(sections):
        for d in range(copies):
            for t in range(ranks):
                goal = target(s, d, t)
                if goal is not None:
                    pairs.append(
                        ((s * copies + d) * ranks + t, (goal[0] * copies + goal[1]) * ranks + goal[2])
                    )
    return lax.ppermute(value, AXES, pairs)


def to_other_core(value):
    return move(value, lambda s, d, t: (s, d ^ 1, t))


def by_core(core, kept, received, axis):
    return jnp.where(
        core == 0,
        jnp.concatenate([kept, received], axis=axis),
        jnp.concatenate([received, kept], axis=axis),
    )


def choose(place, options):
    chosen = options[0]
    for at, option in enumerate(options[1:], 1):
        chosen = jnp.where(place == at, option, chosen)
    return chosen


def after(value, *others):
    return lax.optimization_barrier((value,) + others)[0]


def matmul(lhs_mat, rhs_mat):
    return jnp.dot(lhs_mat, rhs_mat, preferred_element_type=WIDE)


def lhs_inner(lhs_mat, rhs_mat):
    return lax.dot_general(
        lhs_mat, rhs_mat, (((0,), (0,)), ((), ())), preferred_element_type=WIDE
    )


def rhs_inner(lhs_mat, rhs_mat):
    return lax.dot_general(
        lhs_mat, rhs_mat, (((1,), (1,)), ((), ())), preferred_element_type=WIDE
    )


def core_sum(partial):
    low = partial.astype(LOW)
    return low.astype(WIDE) + to_other_core(low).astype(WIDE)


def norm_parts(summed):
    centered = summed - jnp.mean(summed, axis=-1, keepdims=True)
    variance = jnp.mean(centered * centered, axis=-1, keepdims=True)
    scale = lax.rsqrt(variance + 1e-05)
    return centered * scale, scale


def norm_backward(summed, gain_row, grad):
    unit, scale = norm_parts(summed)
    gain_grad = jnp.sum(grad * unit, axis=0)
    bias_grad = jnp.sum(grad, axis=0)
    inner = grad * gain_row
    result = scale * (
        inner
        - jnp.mean(inner, axis=-1, keepdims=True)
        - unit * jnp.mean(inner * unit, axis=-1, keepdims=True)
    )
    return result, gain_grad, bias_grad


def gelu_pair(values):
    below = 0.5 * (1.0 + lax.erf(values * (0.5**0.5)))
    density = jnp.exp(-0.5 * values * values) * (0.3989422804014327)
    return values * below, below + values * density


def segment_ids(seq_lens, row_count):
    seq_ends = jnp.cumsum(seq_lens)
    positions = jnp.arange(row_count, dtype=jnp.int32)
    return jnp.sum((positions[:, None] >= seq_ends[None, :]).astype(jnp.int32), axis=1)


def flash_params(flops, transcendentals, moved):
    return dict(
        cost_estimate=pl.CostEstimate(
            flops=flops, transcendentals=transcendentals, bytes_accessed=moved
        ),
        compiler_params=pltpu.CompilerParams(vmem_limit_bytes=48 * 1024 * 1024),
    )


def head_lanes(values, head):
    lane = lax.broadcasted_iota(jnp.int32, values.shape, 1)
    return jnp.where((lane // HEAD_DIM) == head, values, jnp.zeros_like(values))


def keys_by_queries(keys, queries):
    return lax.dot_general(keys, queries, (((1,), (1,)), ((), ())), preferred_element_type=WIDE)


def key_windows(seq_lens, rows, size):
    widths = tuple(sorted({min(rows, width) for width in (512, 640, 768, rows)}))
    ends = jnp.cumsum(seq_lens)
    first = jnp.arange(rows // size, dtype=jnp.int32)[:, None] * size
    lowest = jnp.max(jnp.where(ends[None, :] <= first, ends[None, :], 0), axis=1)
    highest = jnp.min(jnp.where(ends[None, :] >= first + size, ends[None, :], rows), axis=1)
    start, kind = jnp.zeros_like(lowest), jnp.full_like(lowest, len(widths) - 1)
    for at in range(len(widths) - 2, -1, -1):
        begin = jnp.minimum(lowest // 128 * 128, rows - widths[at])
        fits = highest - begin <= widths[at]
        start = jnp.where(fits, begin, start)
        kind = jnp.where(fits, at, kind)
    return start.astype(jnp.int32), kind.astype(jnp.int32), widths


def each_width(kind, widths, body):
    for at, width in enumerate(widths):
        @pl.when(kind == at)
        def _(width=width):
            body(width)


def forward_kernel(
    widths, start_ref, kind_ref, query_ref, key_ref, value_ref, seg_key_ref, seg_query_ref, out_ref, logsum_ref
):
    block = pl.program_id(1)
    heads = query_ref.shape[1] // HEAD_DIM

    def body(width):
        window = pl.ds(pl.multiple_of(start_ref[block], 128), width)
        allowed = seg_key_ref[window, :] == seg_query_ref[...]
        queries = query_ref[...] * jnp.asarray(HEAD_DIM ** (-0.5), LOW)
        keys, values = key_ref[window, :], value_ref[window, :]
        parts = []
        for head in range(heads):
            scores = keys_by_queries(keys, head_lanes(queries, head))
            scores = jnp.where(allowed, scores, -1000000000.0)
            highest = jnp.max(scores, axis=0, keepdims=True)
            raised = jnp.exp(scores - highest)
            totals = jnp.sum(raised, axis=0, keepdims=True)
            context = lhs_inner(values, raised.astype(LOW))
            rows = slice(head * HEAD_DIM, (head + 1) * HEAD_DIM)
            parts.append(context[rows] / totals)
            logsum_ref[0, head : head + 1, :] = highest + jnp.log(totals)
        out_ref[...] = jnp.concatenate(parts, axis=0).T.astype(LOW)

    each_width(kind_ref[block], widths, body)


def backward_kernel(
    widths, start_ref, kind_ref, query_ref, key_ref, value_ref, seg_key_ref, seg_query_ref, logsum_ref, grad_ref,
    out_ref, sum_ref, key_grad, value_grad,
):
    block = pl.program_id(1)
    size, lanes = query_ref.shape
    heads = lanes // HEAD_DIM
    factor = HEAD_DIM ** (-0.5)

    @pl.when(block == 0)
    def _():
        key_grad[...] = jnp.zeros_like(key_grad)
        value_grad[...] = jnp.zeros_like(value_grad)
        sum_ref[...] = jnp.zeros_like(sum_ref)

    def body(width):
        window = pl.ds(pl.multiple_of(start_ref[block], 128), width)
        allowed = seg_key_ref[window, :] == seg_query_ref[...]
        queries = query_ref[...] * jnp.asarray(factor, LOW)
        grads = grad_ref[...]
        keys, values = key_ref[window, :], value_ref[window, :]
        weight_low, score_low, query_heads, grad_heads, query_parts = [], [], [], [], []
        for head in range(heads):
            query_head, grad_head = head_lanes(queries, head), head_lanes(grads, head)
            scores = jnp.where(allowed, keys_by_queries(keys, query_head), -1000000000.0)
            weights = jnp.exp(scores - logsum_ref[0, head : head + 1, :])
            weight_grad = keys_by_queries(values, grad_head)
            centre = jnp.sum(weight_grad * weights, axis=0, keepdims=True)
            score_grad = (weights * (weight_grad - centre)).astype(LOW)
            rows = slice(head * HEAD_DIM, (head + 1) * HEAD_DIM)
            query_parts.append(lhs_inner(keys, score_grad)[rows] * factor)
            weight_low.append(weights.astype(LOW))
            score_low.append(score_grad)
            query_heads.append(query_head)
            grad_heads.append(grad_head)
        key_grad[window, :] += matmul(
            jnp.concatenate(score_low, axis=1), jnp.concatenate(query_heads, axis=0)
        )
        value_grad[window, :] += matmul(
            jnp.concatenate(weight_low, axis=1), jnp.concatenate(grad_heads, axis=0)
        )
        query_grad = jnp.concatenate(query_parts, axis=0).T
        out_ref[pl.ds(pl.multiple_of(block * size, size), size), :lanes] = query_grad.astype(LOW)
        sum_ref[0, 0:1, :] += jnp.sum(query_grad, axis=0, keepdims=True)

    each_width(kind_ref[block], widths, body)

    @pl.when(block == pl.num_programs(1) - 1)
    def _():
        out_ref[:, lanes : 2 * lanes] = key_grad[...].astype(LOW)
        out_ref[:, 2 * lanes :] = value_grad[...].astype(LOW)
        sum_ref[0, 1:2, :] = jnp.sum(value_grad[...], axis=0, keepdims=True)


def attention_specs(rows, lanes, size):
    return [
        pl.BlockSpec((size, lanes), lambda pair, block, *_: (block, 3 * pair)),
        pl.BlockSpec((rows, lanes), lambda pair, block, *_: (0, 3 * pair + 1)),
        pl.BlockSpec((rows, lanes), lambda pair, block, *_: (0, 3 * pair + 2)),
        pl.BlockSpec((rows, 1), lambda pair, block, *_: (0, 0)),
        pl.BlockSpec((1, size), lambda pair, block, *_: (0, block)),
    ]


def attend_forward(packed, segments, seq_lens, lanes):
    rows = packed.shape[0]
    pairs = packed.shape[1] // (3 * lanes)
    heads = lanes // HEAD_DIM
    size = min(256, rows)
    squares = pairs * heads * rows * rows
    start, kind, widths = key_windows(seq_lens, rows, size)
    return pl.pallas_call(
        functools.partial(forward_kernel, widths),
        grid_spec=pltpu.PrefetchScalarGridSpec(
            num_scalar_prefetch=2,
            grid=(pairs, rows // size),
            in_specs=attention_specs(rows, lanes, size),
            out_specs=[
                pl.BlockSpec((size, lanes), lambda pair, block, *_: (block, pair)),
                pl.BlockSpec((1, heads, size), lambda pair, block, *_: (pair, 0, block)),
            ],
        ),
        out_shape=[
            jax.ShapeDtypeStruct((rows, pairs * lanes), LOW),
            jax.ShapeDtypeStruct((pairs, heads, rows), WIDE),
        ],
        **flash_params(8 * squares * HEAD_DIM, squares, 4 * rows * pairs * lanes * 2),
    )(start, kind, packed, packed, packed, segments[:, None], segments[None, :])


def attend_backward(packed, segments, seq_lens, logsums, context_grad, lanes):
    rows = packed.shape[0]
    pairs = packed.shape[1] // (3 * lanes)
    heads = lanes // HEAD_DIM
    size = min(256, rows)
    squares = pairs * heads * rows * rows
    start, kind, widths = key_windows(seq_lens, rows, size)
    return pl.pallas_call(
        functools.partial(backward_kernel, widths),
        grid_spec=pltpu.PrefetchScalarGridSpec(
            num_scalar_prefetch=2,
            grid=(pairs, rows // size),
            in_specs=attention_specs(rows, lanes, size)
            + [
                pl.BlockSpec((1, heads, size), lambda pair, block, *_: (pair, 0, block)),
                pl.BlockSpec((size, lanes), lambda pair, block, *_: (block, pair)),
            ],
            out_specs=[
                pl.BlockSpec((rows, 3 * lanes), lambda pair, block, *_: (0, pair)),
                pl.BlockSpec((1, 2, lanes), lambda pair, block, *_: (pair, 0, 0)),
            ],
            scratch_shapes=[pltpu.VMEM((rows, lanes), WIDE), pltpu.VMEM((rows, lanes), WIDE)],
        ),
        out_shape=[
            jax.ShapeDtypeStruct((rows, pairs * 3 * lanes), LOW),
            jax.ShapeDtypeStruct((pairs, 2, lanes), WIDE),
        ],
        **flash_params(20 * squares * HEAD_DIM, squares, 8 * rows * pairs * lanes * 2),
    )(start, kind, packed, packed, packed, segments[:, None], segments[None, :], logsums, context_grad)


def pair_columns(packed, head_half, lanes, back=False):
    ranks = lanes // head_half
    if ranks == 1:
        return packed
    order = (3, ranks) if back else (ranks, 3)
    shaped = packed.reshape(packed.shape[0], -1, order[0], order[1], head_half)
    return jnp.swapaxes(shaped, 2, 3).reshape(packed.shape)


def layer_forward(rows, segments, seq_lens, weights, small):
    w_qkv, w_out, w_in, w_back = weights
    gains, biases, offset, inner_bias, head_half = small
    lanes = max(head_half, 128)
    packed = (rhs_inner(rows, w_qkv) + offset).astype(LOW)
    packed = pair_columns(packed, head_half, lanes)
    context, logsums = attend_forward(packed, segments, seq_lens, lanes)
    first_sum = rows.astype(WIDE) + core_sum(matmul(context, w_out)) + biases[2]
    middle = (norm_parts(first_sum)[0] * gains[0] + biases[3]).astype(LOW)
    active, slope = gelu_pair(rhs_inner(middle, w_in) + inner_bias)
    active, slope = active.astype(LOW), slope.astype(LOW)
    second_sum = middle.astype(WIDE) + core_sum(matmul(active, w_back)) + biases[4]
    result = norm_parts(second_sum)[0] * gains[1] + biases[5]
    return result, (rows, packed, logsums, context, first_sum, middle, active, slope, second_sum)


def slab_grads(hidden, features, chips):
    cut = features.shape[1] // chips
    return [lhs_inner(hidden, features[:, k * cut : (k + 1) * cut]).astype(LOW) for k in range(chips)]


def backward_hidden(saved, grad_rows, weights, small):
    _, _, w_in, w_back = weights
    gains = small[0]
    middle, active, slope, second_sum = saved[5:]
    second_grad, gain_two, bias_two = norm_backward(second_sum, gains[1], grad_rows.astype(WIDE))
    branch_grad = second_grad.astype(LOW)
    hidden_grad = rhs_inner(branch_grad, w_back) * slope.astype(WIDE)
    hidden_low = hidden_grad.astype(LOW)
    middle_grad = second_grad + core_sum(matmul(hidden_low, w_in))
    sums = (gain_two, jnp.sum(second_grad, axis=0), bias_two, jnp.sum(hidden_grad, axis=0))
    return middle_grad, branch_grad, hidden_low, sums


def backward_attention(saved, segments, seq_lens, middle_grad, weights, small):
    _, w_out, _, _ = weights
    gains, head_half = small[0], small[4]
    _, packed, logsums, _, first_sum = saved[:5]
    first_grad, gain_one, bias_one = norm_backward(first_sum, gains[0], middle_grad)
    attended_grad = first_grad.astype(LOW)
    context_grad = rhs_inner(attended_grad, w_out).astype(LOW)
    lanes = max(head_half, 128)
    packed_low, column_sums = attend_backward(packed, segments, seq_lens, logsums, context_grad, lanes)
    packed_low = pair_columns(packed_low, head_half, lanes, back=True)
    sums = (gain_one, jnp.sum(first_grad, axis=0), bias_one) + tuple(
        column_sums[:, at].reshape(-1) for at in range(2)
    )
    return first_grad, attended_grad, packed_low, sums


def on_device(
    block_input, seq_lengths, w_qkv, w_out, w_in, w_back, gains, biases, ffn_bias, out_grad
):
    ranks = lax.axis_size("tensor")
    copies = lax.axis_size("dp")
    chips = copies // 2
    section = lax.axis_index("section")
    copy_at = lax.axis_index("dp")
    rank = lax.axis_index("tensor")
    core = copy_at % 2
    chip = copy_at // 2
    micro_count, own_rows, width = block_input.shape
    repeats = ranks // micro_count
    local = gains.shape[-1]
    counted = (rank % repeats) == 0

    def relative(value):
        slabs = jnp.split(value, chips, axis=-1)
        return jnp.concatenate([choose(chip ^ k, slabs) for k in range(chips)], axis=-1)

    def fetch_rows(block, *before):
        parts = block.reshape(micro_count, 2, own_rows // 2, width)
        kept = choose(core, (parts[:, 0], parts[:, 1]))
        given = choose(core, (parts[:, 1], parts[:, 0]))
        received = move(given, lambda s, d, t: (s, d ^ 1, t) if d % 2 == s else None)
        mine = jnp.where(core == section, kept, received)
        mine = jnp.repeat(mine, repeats, axis=0) if repeats > 1 else mine
        mine = after(mine, *before) if before else mine
        mine = lax.all_to_all(mine, "tensor", split_axis=0, concat_axis=0, tiled=True)
        whole = by_core(core, mine, to_other_core(mine), 1)
        return relative(whole.reshape(ranks * own_rows, width)), mine

    def spread_rows(value):
        parts = relative(value.astype(LOW)).reshape(ranks, 2, own_rows // 2, width)
        mine = choose(core, (parts[:, 0], parts[:, 1]))
        spread = lax.all_to_all(mine, "tensor", split_axis=0, concat_axis=0, tiled=True)
        return spread.reshape((micro_count, repeats) + spread.shape[1:])[:, 0]

    def place_rows(spread, layer):
        halves = [
            move(spread, lambda s, d, t: (layer, (d // 2) * 2 + s, t) if d % 2 == half else None)
            for half in range(2)
        ]
        return jnp.concatenate(halves, axis=1)

    def by_section(first, second):
        return jnp.where(section == 0, first, second)

    def own_half(halves):
        kept = choose(core, (halves[0], halves[1]))
        given = choose(core, (halves[1], halves[0]))
        return by_core(core, kept, to_other_core(given), 1)

    def over_ranks(own):
        upward, downward = [own], [own]
        for _ in range(1, ranks):
            upward.append(move(upward[-1], lambda s, d, t: (s, d, t + 1) if t + 1 < ranks else None))
            downward.append(move(downward[-1], lambda s, d, t: (s, d, t - 1) if t > 0 else None))
        item = jnp.zeros((ranks,) + own.shape, LOW)
        item = lax.dynamic_update_index_in_dim(item, own, rank, 0)
        for j in range(1, ranks):
            arrived = jnp.where(rank >= j, upward[j], downward[ranks - j])
            item = lax.dynamic_update_index_in_dim(item, arrived, (rank + ranks - j) % ranks, 0)
        return item

    def over_chips(item):
        part = item.shape[0] // 2
        across = move(item, lambda s, d, t: (1 - s, d, t))
        along = [move(item, lambda s, d, t: (s, d ^ (2 * k), t)) for k in range(1, chips)]
        far = []
        for k in range(1, chips):
            upper = move(across[:part], lambda s, d, t: (s, d ^ (2 * k), t))
            lower = move(along[k - 1][part:], lambda s, d, t: (1 - s, d, t))
            far.append(jnp.concatenate([upper, lower], axis=0))
        mine, other = [item] + along, [across] + far
        result = []
        for layer in range(2):
            slabs = [jnp.where(section == layer, m, o) for m, o in zip(mine, other)]
            result.append(jnp.concatenate(slabs, axis=-1))
        return result

    def gather_weight(own):
        return over_chips(over_ranks(own))

    def gather_weight_late(own):
        both = over_ranks(jnp.stack(over_chips(own)))
        return [both[:, layer] for layer in range(2)]

    def along_x(parts):
        slabs = jnp.split(parts, chips, axis=-1)
        total = slabs[0].astype(WIDE)
        for k in range(1, chips):
            total = total + move(slabs[k], lambda s, d, t: (s, d ^ (2 * k), t)).astype(WIDE)
        return total.astype(LOW)

    def slabs_along_x(slabs):
        total = slabs[0].astype(WIDE)
        for k in range(1, chips):
            total = total + move(slabs[k], lambda s, d, t: (s, d ^ (2 * k), t)).astype(WIDE)
        return total.astype(LOW)

    def to_layer(part, layer):
        sent = move(part, lambda s, d, t: (layer, d, t) if s != layer else None)
        return (part.astype(WIDE) + sent.astype(WIDE)).astype(LOW)

    def over_z(parts):
        parts = parts.reshape((ranks, -1) + parts.shape[1:])
        return lax.psum_scatter(parts, "tensor", scatter_dimension=0, tiled=False).astype(LOW)

    def counted_only(slabs):
        return [jnp.where(counted, slab, jnp.zeros((), LOW)) for slab in slabs] if repeats > 1 else slabs

    def finish(shard):
        parts = jnp.split(shard, 2, axis=1)
        kept = choose(core, parts)
        given = choose(core, parts[::-1])
        return by_core(core, kept[None], to_other_core(given)[None], 0).astype(WIDE)

    head_half = w_qkv.shape[-1] // 2
    hidden_half = w_in.shape[-1] // 2
    in_first = jnp.moveaxis(w_in[0].reshape(local, 2, hidden_half), 0, 2)
    qkv_first = jnp.transpose(w_qkv[0].reshape(local, 3, 2, head_half), (2, 1, 3, 0))
    qkv_first = qkv_first.reshape(2, 3 * head_half, local)
    out_first = w_out[0].reshape(2, head_half, local)
    back_first = w_back[0].reshape(2, hidden_half, local)
    later = hidden_half // 2
    attention_own = own_half(jnp.concatenate([qkv_first, out_first], axis=1))
    back_own = own_half(back_first)
    in_own = own_half(in_first)
    back_two = jnp.stack(over_chips(back_own[later:]))
    attention_item = over_ranks(attention_own)
    attention_all = over_chips(attention_item)
    rows, rows_here = fetch_rows(block_input, attention_item)
    in_item = over_ranks(after(in_own, rows_here))
    in_all = over_chips(in_item)
    back_item = over_ranks(after(back_own[:later], in_item))
    back_one = over_chips(back_item)
    back_two = over_ranks(after(back_two, back_item))
    back_all = [jnp.concatenate([back_one[at], back_two[:, at]], axis=1) for at in range(2)]
    weights = [
        (
            attention_all[layer][:, : 3 * head_half].reshape(-1, width),
            attention_all[layer][:, 3 * head_half :].reshape(-1, width),
            in_all[layer].reshape(-1, width),
            back_all[layer].reshape(-1, width),
        )
        for layer in range(2)
    ]

    gain_count, bias_count = gains.shape[1], biases.shape[1]
    packed_small = jnp.concatenate([gains, biases, ffn_bias.reshape(1, -1, local)], axis=1)
    table_parts = [
        [
            packed_small
            if a == 0 and b == 0
            else move(packed_small, lambda s, d, t: (s ^ a, d ^ b, t))
            for b in range(copies)
        ]
        for a in range(2)
    ]
    table_all = jnp.stack([jnp.stack(row) for row in table_parts])[:, :, 0].astype(WIDE)
    small_all = jnp.stack([choose(section, (table_all[at], table_all[1 - at])) for at in range(2)])
    order = [[at ^ b for b in range(copies)] for at in range(copies)]
    small_all = jnp.stack(
        [choose(copy_at, [small_all[:, order[at][b]] for b in range(copies)]) for at in range(copies)],
        axis=1,
    )

    def head_columns(row):
        halves = row.reshape(ranks, 2, -1)
        return choose(core, (halves[:, 0], halves[:, 1])).reshape(-1)

    small = []
    for layer in range(2):
        table = jnp.moveaxis(small_all[layer, :, : gain_count + bias_count], 0, 1).reshape(-1, width)
        query_bias = head_columns(table[gain_count])
        value_bias = head_columns(table[gain_count + 1])
        query_bias, value_bias = query_bias.reshape(ranks, 1, -1), value_bias.reshape(ranks, 1, -1)
        offset = jnp.concatenate([query_bias, jnp.zeros_like(query_bias), value_bias], axis=1).reshape(-1)
        inner_bias = head_columns(small_all[layer, :, gain_count + bias_count :].reshape(-1))
        table = relative(table)
        small.append((table[:gain_count], table[gain_count:], offset, inner_bias, head_half))

    lengths = jnp.where(core == section, seq_lengths, to_other_core(seq_lengths))[:, 0]
    lengths = lax.dynamic_index_in_dim(lengths, rank // repeats, 0, keepdims=False)
    segments = segment_ids(lengths, ranks * own_rows)
    live = (segments < lengths.shape[0])[:, None]

    first_out, first_saved = layer_forward(rows, segments, lengths, weights[0], small[0])
    first_low = first_out.astype(LOW)
    cotangent, cotangent_here = fetch_rows(out_grad, first_low, back_two)
    cotangent = jnp.where(live, cotangent, jnp.zeros((), LOW))
    second_out, second_saved = layer_forward(first_low, segments, lengths, weights[1], small[1])
    first_spread = spread_rows(after(first_low, cotangent_here))
    second_spread = spread_rows(second_out)

    def matrix_grad(hidden, features):
        return counted_only([lhs_inner(hidden, features).astype(LOW)])[0]

    def attention_grads(saved, attended_grad, packed_low):
        qkv = over_z(matrix_grad(packed_low, saved[0]))
        return qkv, over_z(matrix_grad(saved[3], attended_grad))

    middle_grad, branch_grad, hidden_low, second_sums = backward_hidden(
        second_saved, cotangent, weights[1], small[1]
    )
    middle_grad = after(middle_grad, first_spread)
    first_placed = place_rows(first_spread, 0)
    back_two = slabs_along_x(counted_only(slab_grads(second_saved[6], branch_grad, chips)))
    in_two = over_z(matrix_grad(hidden_low, second_saved[5]))
    first_grad, attended_grad, packed_low, more_sums = backward_attention(
        second_saved, segments, lengths, middle_grad, weights[1], small[1]
    )
    second_sums += more_sums
    packed_low = after(packed_low, back_two, second_spread)
    back_two = to_layer(back_two, 1)
    second_placed = place_rows(second_spread, 1)
    second_in = first_grad + core_sum(matmul(packed_low, weights[1][0]))
    qkv_two, out_two = attention_grads(second_saved, attended_grad, packed_low)
    second_low = second_in.astype(LOW)
    second_in_spread = spread_rows(second_low)

    middle_grad, branch_grad, hidden_low, first_sums = backward_hidden(
        first_saved, second_low, weights[0], small[0]
    )
    middle_grad = after(middle_grad, back_two, in_two, first_placed, second_placed)
    outputs = by_section(first_placed, second_placed).astype(WIDE)[None]
    in_two = along_x(in_two)
    back_one = slabs_along_x(counted_only(slab_grads(first_saved[6], branch_grad, chips)))
    in_one = slabs_along_x(counted_only(slab_grads(hidden_low, first_saved[5], chips)))
    first_grad, attended_grad, packed_low, more_sums = backward_attention(
        first_saved, segments, lengths, middle_grad, weights[0], small[0]
    )
    first_sums += more_sums
    packed_low = after(packed_low, qkv_two, out_two, in_two, back_one)
    in_two, back_one = to_layer(in_two, 1), to_layer(back_one, 0)
    qkv_two, out_two = along_x(qkv_two), along_x(out_two)
    qkv_one, out_one = attention_grads(first_saved, attended_grad, packed_low)
    first_in = first_grad + core_sum(matmul(packed_low, weights[0][0]))
    first_in = after(first_in, in_one, second_in_spread)
    in_one = to_layer(in_one, 0)
    second_in_placed = place_rows(second_in_spread, 1)
    first_in_placed = place_rows(spread_rows(first_in), 0)
    input_grads = by_section(first_in_placed, second_in_placed).astype(WIDE)[None]

    back_shard = finish(over_z(by_section(back_one, back_two)))
    in_shard = finish(by_section(over_z(in_one), in_two))
    qkv_two, out_two = to_layer(qkv_two, 1), to_layer(out_two, 1)
    qkv_one, out_one = to_layer(along_x(qkv_one), 0), to_layer(along_x(out_one), 0)
    out_shard = finish(by_section(out_one, out_two))
    qkv_shard = finish(by_section(qkv_one, qkv_two))
    qkv_grad = jnp.transpose(qkv_shard.reshape(2, 3, head_half, local), (3, 1, 0, 2)).reshape(local, 3, -1)
    out_grad_w = out_shard.reshape(-1, local)
    in_grad = jnp.transpose(in_shard.reshape(-1, local))
    back_grad = back_shard.reshape(-1, local)

    def spread_columns(row):
        blocks = row.reshape(ranks, 1, -1)
        both = jnp.where(jnp.arange(2)[None, :, None] == core, blocks, 0.0)
        return both.reshape(-1, width)

    tables = []
    for sums in (first_sums, second_sums):
        gain_two, bias_four, bias_five, inner_sum, gain_one, bias_two, bias_three, query_sum, value_sum = sums
        common = jnp.stack([gain_one, gain_two, bias_two, bias_three, bias_four, bias_five])
        common = jnp.where(core == 0, relative(common), 0.0)
        tables.append(
            jnp.concatenate(
                [common[:2], spread_columns(query_sum), spread_columns(value_sum), common[2:], spread_columns(inner_sum)]
            )
        )
    table = jnp.stack(tables)
    table = jnp.where(counted, table, 0.0) if repeats > 1 else table
    table = lax.dynamic_index_in_dim(lax.psum(table, AXES), section, 0, keepdims=False)
    sliced = lax.dynamic_slice_in_dim(table[: gain_count + bias_count], copy_at * local, local, 1)
    inner = lax.dynamic_index_in_dim(
        table[gain_count + bias_count :].reshape(copies, -1), copy_at, 0, keepdims=False
    )
    return (
        outputs,
        input_grads,
        qkv_grad[None],
        out_grad_w[None],
        in_grad[None],
        back_grad[None],
        sliced[None, :gain_count],
        sliced[None, gain_count:],
        inner[None],
    )


def solution(mesh):
    return jax.shard_map(
        on_device,
        mesh=mesh,
        in_specs=(
            P(None, ("dp", "tensor"), None),
            P(None, "dp", None),
            P("section", "dp", None, "tensor"),
            P("section", "tensor", "dp"),
            P("section", "dp", "tensor"),
            P("section", "tensor", "dp"),
            P("section", None, "dp"),
            P("section", None, "dp"),
            P("section", "dp"),
            P(None, ("dp", "tensor"), None),
        ),
        out_specs=(
            P("section", None, ("dp", "tensor"), None),
            P("section", None, ("dp", "tensor"), None),
            P("section", "dp", None, "tensor"),
            P("section", "tensor", "dp"),
            P("section", "dp", "tensor"),
            P("section", "tensor", "dp"),
            P("section", None, "dp"),
            P("section", None, "dp"),
            P("section", "dp"),
        ),
        check_vma=False,
    )
```

```python
import functools

import jax
import jax.numpy as jnp
from jax import lax
from jax.experimental import pallas as pl
from jax.experimental.pallas import tpu as pltpu
from jax.sharding import PartitionSpec as P

HEAD_DIM = 64
AXES = ("section", "dp", "tensor")
LOW = jnp.bfloat16
WIDE = jnp.float32


def move(value, target):
    sections, copies, ranks = (lax.axis_size(axis) for axis in AXES)
    pairs = []
    for s in range(sections):
        for d in range(copies):
            for t in range(ranks):
                goal = target(s, d, t)
                if goal is not None:
                    pairs.append(
                        ((s * copies + d) * ranks + t, (goal[0] * copies + goal[1]) * ranks + goal[2])
                    )
    return lax.ppermute(value, AXES, pairs)


def to_other_core(value):
    return move(value, lambda s, d, t: (s, d ^ 1, t))


def by_core(core, kept, received, axis):
    return jnp.where(
        core == 0,
        jnp.concatenate([kept, received], axis=axis),
        jnp.concatenate([received, kept], axis=axis),
    )


def choose(place, options):
    chosen = options[0]
    for at, option in enumerate(options[1:], 1):
        chosen = jnp.where(place == at, option, chosen)
    return chosen


def after(value, *others):
    return lax.optimization_barrier((value,) + others)[0]


def tie(*values):
    return lax.optimization_barrier(values)


def matmul(lhs_mat, rhs_mat):
    return jnp.dot(lhs_mat, rhs_mat, preferred_element_type=WIDE)


def lhs_inner(lhs_mat, rhs_mat):
    return lax.dot_general(
        lhs_mat, rhs_mat, (((0,), (0,)), ((), ())), preferred_element_type=WIDE
    )


def rhs_inner(lhs_mat, rhs_mat):
    return lax.dot_general(
        lhs_mat, rhs_mat, (((1,), (1,)), ((), ())), preferred_element_type=WIDE
    )


def core_sum(partial):
    low = partial.astype(LOW)
    return low.astype(WIDE) + to_other_core(low).astype(WIDE)


def norm_parts(summed):
    centered = summed - jnp.mean(summed, axis=-1, keepdims=True)
    variance = jnp.mean(centered * centered, axis=-1, keepdims=True)
    scale = lax.rsqrt(variance + 1e-05)
    return centered * scale, scale


def norm_backward(summed, gain_row, grad):
    unit, scale = norm_parts(summed)
    gain_grad = jnp.sum(grad * unit, axis=0)
    bias_grad = jnp.sum(grad, axis=0)
    inner = grad * gain_row
    result = scale * (
        inner
        - jnp.mean(inner, axis=-1, keepdims=True)
        - unit * jnp.mean(inner * unit, axis=-1, keepdims=True)
    )
    return result, gain_grad, bias_grad


def gelu_pair(values):
    below = 0.5 * (1.0 + lax.erf(values * (0.5**0.5)))
    density = jnp.exp(-0.5 * values * values) * (0.3989422804014327)
    return values * below, below + values * density


def segment_ids(seq_lens, row_count):
    seq_ends = jnp.cumsum(seq_lens)
    positions = jnp.arange(row_count, dtype=jnp.int32)
    return jnp.sum((positions[:, None] >= seq_ends[None, :]).astype(jnp.int32), axis=1)


def flash_params(flops, transcendentals, moved):
    return dict(
        cost_estimate=pl.CostEstimate(
            flops=flops, transcendentals=transcendentals, bytes_accessed=moved
        ),
        compiler_params=pltpu.CompilerParams(vmem_limit_bytes=48 * 1024 * 1024),
    )


def head_lanes(values, head):
    lane = lax.broadcasted_iota(jnp.int32, values.shape, 1)
    return jnp.where((lane // HEAD_DIM) == head, values, jnp.zeros_like(values))


def keys_by_queries(keys, queries):
    return lax.dot_general(keys, queries, (((1,), (1,)), ((), ())), preferred_element_type=WIDE)


def key_windows(seq_lens, rows, size):
    widths = tuple(sorted({min(rows, width) for width in (512, 640, 768, rows)}))
    ends = jnp.cumsum(seq_lens)
    first = jnp.arange(rows // size, dtype=jnp.int32)[:, None] * size
    lowest = jnp.max(jnp.where(ends[None, :] <= first, ends[None, :], 0), axis=1)
    highest = jnp.min(jnp.where(ends[None, :] >= first + size, ends[None, :], rows), axis=1)
    start, kind = jnp.zeros_like(lowest), jnp.full_like(lowest, len(widths) - 1)
    for at in range(len(widths) - 2, -1, -1):
        begin = jnp.minimum(lowest // 128 * 128, rows - widths[at])
        fits = highest - begin <= widths[at]
        start = jnp.where(fits, begin, start)
        kind = jnp.where(fits, at, kind)
    return start.astype(jnp.int32), kind.astype(jnp.int32), widths


def each_width(kind, widths, body):
    for at, width in enumerate(widths):
        @pl.when(kind == at)
        def _(width=width):
            body(width)


def forward_kernel(
    widths, start_ref, kind_ref, query_ref, key_ref, value_ref, seg_key_ref, seg_query_ref, out_ref, logsum_ref
):
    block = pl.program_id(1)
    heads = query_ref.shape[1] // HEAD_DIM

    def body(width):
        window = pl.ds(pl.multiple_of(start_ref[block], 128), width)
        allowed = seg_key_ref[window, :] == seg_query_ref[...]
        queries = query_ref[...] * jnp.asarray(HEAD_DIM ** (-0.5), LOW)
        keys, values = key_ref[window, :], value_ref[window, :]
        parts = []
        for head in range(heads):
            scores = keys_by_queries(keys, head_lanes(queries, head))
            scores = jnp.where(allowed, scores, -1000000000.0)
            highest = jnp.max(scores, axis=0, keepdims=True)
            raised = jnp.exp(scores - highest)
            totals = jnp.sum(raised, axis=0, keepdims=True)
            context = lhs_inner(values, raised.astype(LOW))
            rows = slice(head * HEAD_DIM, (head + 1) * HEAD_DIM)
            parts.append(context[rows] / totals)
            logsum_ref[0, head : head + 1, :] = highest + jnp.log(totals)
        out_ref[...] = jnp.concatenate(parts, axis=0).T.astype(LOW)

    each_width(kind_ref[block], widths, body)


def backward_kernel(
    widths, start_ref, kind_ref, query_ref, key_ref, value_ref, seg_key_ref, seg_query_ref, logsum_ref, grad_ref,
    out_ref, sum_ref, key_grad, value_grad,
):
    block = pl.program_id(1)
    size, lanes = query_ref.shape
    heads = lanes // HEAD_DIM
    factor = HEAD_DIM ** (-0.5)

    @pl.when(block == 0)
    def _():
        key_grad[...] = jnp.zeros_like(key_grad)
        value_grad[...] = jnp.zeros_like(value_grad)
        sum_ref[...] = jnp.zeros_like(sum_ref)

    def body(width):
        window = pl.ds(pl.multiple_of(start_ref[block], 128), width)
        allowed = seg_key_ref[window, :] == seg_query_ref[...]
        queries = query_ref[...] * jnp.asarray(factor, LOW)
        grads = grad_ref[...]
        keys, values = key_ref[window, :], value_ref[window, :]
        weight_low, score_low, query_heads, grad_heads, query_parts = [], [], [], [], []
        for head in range(heads):
            query_head, grad_head = head_lanes(queries, head), head_lanes(grads, head)
            scores = jnp.where(allowed, keys_by_queries(keys, query_head), -1000000000.0)
            weights = jnp.exp(scores - logsum_ref[0, head : head + 1, :])
            weight_grad = keys_by_queries(values, grad_head)
            centre = jnp.sum(weight_grad * weights, axis=0, keepdims=True)
            score_grad = (weights * (weight_grad - centre)).astype(LOW)
            rows = slice(head * HEAD_DIM, (head + 1) * HEAD_DIM)
            query_parts.append(lhs_inner(keys, score_grad)[rows] * factor)
            weight_low.append(weights.astype(LOW))
            score_low.append(score_grad)
            query_heads.append(query_head)
            grad_heads.append(grad_head)
        key_grad[window, :] += matmul(
            jnp.concatenate(score_low, axis=1), jnp.concatenate(query_heads, axis=0)
        )
        value_grad[window, :] += matmul(
            jnp.concatenate(weight_low, axis=1), jnp.concatenate(grad_heads, axis=0)
        )
        query_grad = jnp.concatenate(query_parts, axis=0).T
        out_ref[pl.ds(pl.multiple_of(block * size, size), size), :lanes] = query_grad.astype(LOW)
        sum_ref[0, 0:1, :] += jnp.sum(query_grad, axis=0, keepdims=True)

    each_width(kind_ref[block], widths, body)

    @pl.when(block == pl.num_programs(1) - 1)
    def _():
        out_ref[:, lanes : 2 * lanes] = key_grad[...].astype(LOW)
        out_ref[:, 2 * lanes :] = value_grad[...].astype(LOW)
        sum_ref[0, 1:2, :] = jnp.sum(value_grad[...], axis=0, keepdims=True)


def attention_specs(rows, lanes, size):
    return [
        pl.BlockSpec((size, lanes), lambda pair, block, *_: (block, 3 * pair)),
        pl.BlockSpec((rows, lanes), lambda pair, block, *_: (0, 3 * pair + 1)),
        pl.BlockSpec((rows, lanes), lambda pair, block, *_: (0, 3 * pair + 2)),
        pl.BlockSpec((rows, 1), lambda pair, block, *_: (0, 0)),
        pl.BlockSpec((1, size), lambda pair, block, *_: (0, block)),
    ]


def attend_forward(packed, segments, seq_lens, lanes):
    rows = packed.shape[0]
    pairs = packed.shape[1] // (3 * lanes)
    heads = lanes // HEAD_DIM
    size = min(256, rows)
    squares = pairs * heads * rows * rows
    start, kind, widths = key_windows(seq_lens, rows, size)
    return pl.pallas_call(
        functools.partial(forward_kernel, widths),
        grid_spec=pltpu.PrefetchScalarGridSpec(
            num_scalar_prefetch=2,
            grid=(pairs, rows // size),
            in_specs=attention_specs(rows, lanes, size),
            out_specs=[
                pl.BlockSpec((size, lanes), lambda pair, block, *_: (block, pair)),
                pl.BlockSpec((1, heads, size), lambda pair, block, *_: (pair, 0, block)),
            ],
        ),
        out_shape=[
            jax.ShapeDtypeStruct((rows, pairs * lanes), LOW),
            jax.ShapeDtypeStruct((pairs, heads, rows), WIDE),
        ],
        **flash_params(8 * squares * HEAD_DIM, squares, 4 * rows * pairs * lanes * 2),
    )(start, kind, packed, packed, packed, segments[:, None], segments[None, :])


def attend_backward(packed, segments, seq_lens, logsums, context_grad, lanes):
    rows = packed.shape[0]
    pairs = packed.shape[1] // (3 * lanes)
    heads = lanes // HEAD_DIM
    size = min(256, rows)
    squares = pairs * heads * rows * rows
    start, kind, widths = key_windows(seq_lens, rows, size)
    return pl.pallas_call(
        functools.partial(backward_kernel, widths),
        grid_spec=pltpu.PrefetchScalarGridSpec(
            num_scalar_prefetch=2,
            grid=(pairs, rows // size),
            in_specs=attention_specs(rows, lanes, size)
            + [
                pl.BlockSpec((1, heads, size), lambda pair, block, *_: (pair, 0, block)),
                pl.BlockSpec((size, lanes), lambda pair, block, *_: (block, pair)),
            ],
            out_specs=[
                pl.BlockSpec((rows, 3 * lanes), lambda pair, block, *_: (0, pair)),
                pl.BlockSpec((1, 2, lanes), lambda pair, block, *_: (pair, 0, 0)),
            ],
            scratch_shapes=[pltpu.VMEM((rows, lanes), WIDE), pltpu.VMEM((rows, lanes), WIDE)],
        ),
        out_shape=[
            jax.ShapeDtypeStruct((rows, pairs * 3 * lanes), LOW),
            jax.ShapeDtypeStruct((pairs, 2, lanes), WIDE),
        ],
        **flash_params(20 * squares * HEAD_DIM, squares, 8 * rows * pairs * lanes * 2),
    )(start, kind, packed, packed, packed, segments[:, None], segments[None, :], logsums, context_grad)


def pair_columns(packed, head_half, lanes, back=False):
    ranks = lanes // head_half
    if ranks == 1:
        return packed
    order = (3, ranks) if back else (ranks, 3)
    shaped = packed.reshape(packed.shape[0], -1, order[0], order[1], head_half)
    return jnp.swapaxes(shaped, 2, 3).reshape(packed.shape)


def layer_forward(rows, segments, seq_lens, weights, small):
    w_qkv, w_out, w_in, w_back = weights
    gains, biases, offset, inner_bias, head_half = small
    lanes = max(head_half, 128)
    packed = (rhs_inner(rows, w_qkv) + offset).astype(LOW)
    packed = pair_columns(packed, head_half, lanes)
    context, logsums = attend_forward(packed, segments, seq_lens, lanes)
    first_sum = rows.astype(WIDE) + core_sum(matmul(context, w_out)) + biases[2]
    middle = (norm_parts(first_sum)[0] * gains[0] + biases[3]).astype(LOW)
    active, slope = gelu_pair(rhs_inner(middle, w_in) + inner_bias)
    active, slope = active.astype(LOW), slope.astype(LOW)
    second_sum = middle.astype(WIDE) + core_sum(matmul(active, w_back)) + biases[4]
    result = norm_parts(second_sum)[0] * gains[1] + biases[5]
    return result, (rows, packed, logsums, context, first_sum, middle, active, slope, second_sum)


def slab_grads(hidden, features, chips):
    cut = features.shape[1] // chips
    return [lhs_inner(hidden, features[:, k * cut : (k + 1) * cut]).astype(LOW) for k in range(chips)]


def backward_hidden(saved, grad_rows, weights, small):
    _, _, w_in, w_back = weights
    gains = small[0]
    middle, active, slope, second_sum = saved[5:]
    second_grad, gain_two, bias_two = norm_backward(second_sum, gains[1], grad_rows.astype(WIDE))
    branch_grad = second_grad.astype(LOW)
    hidden_low = (rhs_inner(branch_grad, w_back) * slope.astype(WIDE)).astype(LOW)
    middle_grad = second_grad + core_sum(matmul(hidden_low, w_in))
    inner_sum = matmul(jnp.ones((8, hidden_low.shape[0]), LOW), hidden_low)[0]
    sums = (gain_two, jnp.sum(second_grad, axis=0), bias_two, inner_sum)
    return middle_grad, branch_grad, hidden_low, sums


def backward_attention(saved, segments, seq_lens, middle_grad, weights, small):
    _, w_out, _, _ = weights
    gains, head_half = small[0], small[4]
    _, packed, logsums, _, first_sum = saved[:5]
    first_grad, gain_one, bias_one = norm_backward(first_sum, gains[0], middle_grad)
    attended_grad = first_grad.astype(LOW)
    context_grad = rhs_inner(attended_grad, w_out).astype(LOW)
    lanes = max(head_half, 128)
    packed_low, column_sums = attend_backward(packed, segments, seq_lens, logsums, context_grad, lanes)
    packed_low = pair_columns(packed_low, head_half, lanes, back=True)
    sums = (gain_one, jnp.sum(first_grad, axis=0), bias_one) + tuple(
        column_sums[:, at].reshape(-1) for at in range(2)
    )
    return first_grad, attended_grad, packed_low, sums


def on_device(
    block_input, seq_lengths, w_qkv, w_out, w_in, w_back, gains, biases, ffn_bias, out_grad
):
    ranks = lax.axis_size("tensor")
    copies = lax.axis_size("dp")
    chips = copies // 2
    section = lax.axis_index("section")
    copy_at = lax.axis_index("dp")
    rank = lax.axis_index("tensor")
    core = copy_at % 2
    chip = copy_at // 2
    micro_count, own_rows, width = block_input.shape
    repeats = ranks // micro_count
    local = gains.shape[-1]
    counted = (rank % repeats) == 0

    def relative(value):
        slabs = jnp.split(value, chips, axis=-1)
        return jnp.concatenate([choose(chip ^ k, slabs) for k in range(chips)], axis=-1)

    def fetch_rows(block, *before):
        half = own_rows // 2
        kept = choose(core, (block[:, :half], block[:, half:]))
        given = choose(core, (block[:, half:], block[:, :half]))
        received = move(given, lambda s, d, t: (s, d ^ 1, t) if d % 2 == s else None)
        mine = jnp.where(core == section, kept, received)
        mine = jnp.repeat(mine, repeats, axis=0) if repeats > 1 else mine
        mine = after(mine, *before) if before else mine
        mine = lax.all_to_all(mine, "tensor", split_axis=0, concat_axis=0, tiled=True)
        whole = by_core(core, mine, to_other_core(mine), 1)
        return relative(whole.reshape(ranks * own_rows, width))

    def spread_both(first, second):
        chosen = relative(jnp.where(core == 0, first, second)).reshape(ranks, own_rows, width)
        spread = lax.all_to_all(chosen, "tensor", split_axis=0, concat_axis=0, tiled=True)
        return spread.reshape(micro_count, repeats, own_rows, width)[:, 0]

    def place_both(spread):
        return move(spread, lambda s, d, t: (d % 2, (d // 2) * 2 + s, t))

    def spread_rows(value):
        parts = relative(value).reshape(ranks, own_rows, width)
        half = own_rows // 2
        mine = choose(core, (parts[:, :half], parts[:, half:]))
        spread = lax.all_to_all(mine, "tensor", split_axis=0, concat_axis=0, tiled=True)
        return spread.reshape((micro_count, repeats) + spread.shape[1:])[:, 0]

    def place_rows(spread, layer):
        halves = [
            move(spread, lambda s, d, t: (layer, (d // 2) * 2 + s, t) if d % 2 == half else None)
            for half in range(2)
        ]
        return jnp.concatenate(halves, axis=1)

    def by_section(first, second):
        return jnp.where(section == 0, first, second)

    def own_half(halves):
        kept = choose(core, (halves[0], halves[1]))
        given = choose(core, (halves[1], halves[0]))
        return by_core(core, kept, to_other_core(given), 1)

    def over_ranks(own):
        upward, downward = [own], [own]
        for _ in range(1, ranks):
            upward.append(move(upward[-1], lambda s, d, t: (s, d, t + 1) if t + 1 < ranks else None))
            downward.append(move(downward[-1], lambda s, d, t: (s, d, t - 1) if t > 0 else None))
        item = jnp.zeros((ranks,) + own.shape, LOW)
        item = lax.dynamic_update_index_in_dim(item, own, rank, 0)
        for j in range(1, ranks):
            arrived = jnp.where(rank >= j, upward[j], downward[ranks - j])
            item = lax.dynamic_update_index_in_dim(item, arrived, (rank + ranks - j) % ranks, 0)
        return item

    def over_chips(item):
        part = item.shape[0] // 2
        across = move(item, lambda s, d, t: (1 - s, d, t))
        along = [move(item, lambda s, d, t: (s, d ^ (2 * k), t)) for k in range(1, chips)]
        far = []
        for k in range(1, chips):
            upper = move(across[:part], lambda s, d, t: (s, d ^ (2 * k), t))
            lower = move(along[k - 1][part:], lambda s, d, t: (1 - s, d, t))
            far.append(jnp.concatenate([upper, lower], axis=0))
        mine, other = [item] + along, [across] + far
        result = []
        for layer in range(2):
            slabs = [jnp.where(section == layer, m, o) for m, o in zip(mine, other)]
            result.append(jnp.concatenate(slabs, axis=-1))
        return result

    def gather_weight(own):
        return over_chips(over_ranks(own))

    def gather_weight_late(own):
        both = over_ranks(jnp.stack(over_chips(own)))
        return [both[:, layer] for layer in range(2)]

    def from_x(slabs):
        return [move(slabs[k], lambda s, d, t: (s, d ^ (2 * k), t)) for k in range(1, chips)]

    def from_section(part, layer):
        return move(part, lambda s, d, t: (layer, d, t) if s != layer else None)

    def add(part, received):
        total = part.astype(WIDE)
        for other in received:
            total = total + other.astype(WIDE)
        return total.astype(LOW)

    def from_z(parts):
        return lax.all_to_all(parts, "tensor", split_axis=0, concat_axis=0, tiled=True)

    def add_ranks(parts):
        return jnp.sum(parts.astype(WIDE), axis=0).astype(LOW)

    def ranked(slab):
        return slab.reshape((ranks, -1) + slab.shape[1:])

    def counted_only(slabs):
        return [jnp.where(counted, slab, jnp.zeros((), LOW)) for slab in slabs] if repeats > 1 else slabs

    def finish(shard):
        parts = jnp.split(shard, 2, axis=1)
        kept = choose(core, parts)
        given = choose(core, parts[::-1])
        return by_core(core, kept[None], to_other_core(given)[None], 0).astype(WIDE)

    head_half = w_qkv.shape[-1] // 2
    hidden_half = w_in.shape[-1] // 2
    in_first = jnp.moveaxis(w_in[0].reshape(local, 2, hidden_half), 0, 2)
    qkv_first = jnp.transpose(w_qkv[0].reshape(local, 3, 2, head_half), (2, 1, 3, 0))
    qkv_first = qkv_first.reshape(2, 3 * head_half, local)
    out_first = w_out[0].reshape(2, head_half, local)
    back_first = w_back[0].reshape(2, hidden_half, local)
    later = hidden_half // 2
    attention_own = own_half(jnp.concatenate([qkv_first, out_first], axis=1))
    back_own = own_half(back_first)
    in_own = own_half(in_first)
    back_two = jnp.stack(over_chips(back_own[later:]))
    attention_item = over_ranks(attention_own)
    attention_item, back_two = tie(attention_item, back_two)
    attention_all = over_chips(attention_item)
    rows = fetch_rows(block_input, attention_item)
    in_item = over_ranks(after(in_own, attention_item))
    in_all = over_chips(in_item)
    back_item = over_ranks(after(back_own[:later], in_item))
    back_one = over_chips(back_item)
    back_two = over_ranks(after(back_two, back_item))
    back_all = [jnp.concatenate([back_one[at], back_two[:, at]], axis=1) for at in range(2)]
    weights = [
        (
            attention_all[layer][:, : 3 * head_half].reshape(-1, width),
            attention_all[layer][:, 3 * head_half :].reshape(-1, width),
            in_all[layer].reshape(-1, width),
            back_all[layer].reshape(-1, width),
        )
        for layer in range(2)
    ]

    gain_count, bias_count = gains.shape[1], biases.shape[1]
    packed_small = jnp.concatenate([gains, biases, ffn_bias.reshape(1, -1, local)], axis=1)
    packed_small, seq_lengths = tie(packed_small, seq_lengths, attention_item)[:2]
    table_parts = [
        [
            packed_small
            if a == 0 and b == 0
            else move(packed_small, lambda s, d, t: (s ^ a, d ^ b, t))
            for b in range(copies)
        ]
        for a in range(2)
    ]
    table_all = jnp.stack([jnp.stack(row) for row in table_parts])[:, :, 0].astype(WIDE)
    small_all = jnp.stack([choose(section, (table_all[at], table_all[1 - at])) for at in range(2)])
    order = [[at ^ b for b in range(copies)] for at in range(copies)]
    small_all = jnp.stack(
        [choose(copy_at, [small_all[:, order[at][b]] for b in range(copies)]) for at in range(copies)],
        axis=1,
    )

    def head_columns(row):
        halves = row.reshape(ranks, 2, -1)
        return choose(core, (halves[:, 0], halves[:, 1])).reshape(-1)

    small = []
    for layer in range(2):
        table = jnp.moveaxis(small_all[layer, :, : gain_count + bias_count], 0, 1).reshape(-1, width)
        query_bias = head_columns(table[gain_count])
        value_bias = head_columns(table[gain_count + 1])
        query_bias, value_bias = query_bias.reshape(ranks, 1, -1), value_bias.reshape(ranks, 1, -1)
        offset = jnp.concatenate([query_bias, jnp.zeros_like(query_bias), value_bias], axis=1).reshape(-1)
        inner_bias = head_columns(small_all[layer, :, gain_count + bias_count :].reshape(-1))
        table = relative(table)
        small.append((table[:gain_count], table[gain_count:], offset, inner_bias, head_half))

    lengths = jnp.where(core == section, seq_lengths, to_other_core(seq_lengths))[:, 0]
    lengths = lax.dynamic_index_in_dim(lengths, rank // repeats, 0, keepdims=False)
    segments = segment_ids(lengths, ranks * own_rows)
    live = (segments < lengths.shape[0])[:, None]

    first_out, first_saved = layer_forward(rows, segments, lengths, weights[0], small[0])
    first_low = first_out.astype(LOW)
    cotangent = fetch_rows(out_grad, back_two)
    cotangent = jnp.where(live, cotangent, jnp.zeros((), LOW))
    second_out, second_saved = layer_forward(first_low, segments, lengths, weights[1], small[1])
    spread = spread_both(first_low, second_out.astype(LOW))

    def hidden_grads(hidden, features):
        return [ranked(slab) for slab in counted_only(slab_grads(hidden, features, chips))]

    def attention_grads(saved, attended_grad, packed_low):
        qkv = hidden_grads(packed_low, saved[0])
        out = hidden_grads(saved[3], attended_grad)
        return [jnp.concatenate(pair, axis=1) for pair in zip(qkv, out)]

    middle_grad, branch_grad, hidden_low, second_sums = backward_hidden(
        second_saved, cotangent, weights[1], small[1]
    )
    back_slabs = hidden_grads(second_saved[6], branch_grad)
    back_here = from_x(back_slabs)
    inner = counted_only([lhs_inner(hidden_low, second_saved[5]).astype(LOW)])[0]
    in_here = from_z(ranked(inner))
    first_grad, attended_grad, packed_low, more_sums = backward_attention(
        second_saved, segments, lengths, middle_grad, weights[1], small[1]
    )
    second_sums += more_sums
    packed_low, spread, *back_here = tie(packed_low, spread, *back_here)
    back_two = add(back_slabs[0], back_here)
    back_sent = from_section(back_two, 1)
    placed = place_both(spread)
    second_in = first_grad + core_sum(matmul(packed_low, weights[1][0]))
    attention_slabs = attention_grads(second_saved, attended_grad, packed_low)
    attention_here = from_x(attention_slabs)
    second_low = second_in.astype(LOW)

    middle_grad, branch_grad, hidden_low, first_sums = backward_hidden(
        first_saved, second_low, weights[0], small[0]
    )
    middle_grad, back_sent, placed = tie(middle_grad, back_sent, placed)
    back_two = add(back_two, [back_sent])
    outputs = placed.astype(WIDE)[None]
    second_in_spread = spread_rows(second_low)
    back_slabs = hidden_grads(first_saved[6], branch_grad)
    back_here = from_x(back_slabs)
    in_slabs = hidden_grads(hidden_low, first_saved[5])
    in_one_here = from_x(in_slabs)
    first_grad, attended_grad, packed_low, more_sums = backward_attention(
        first_saved, segments, lengths, middle_grad, weights[0], small[0]
    )
    first_sums += more_sums
    packed_low, in_here, *attention_here = tie(packed_low, in_here, *attention_here)
    attention_two = add(attention_slabs[0], attention_here)
    attention_sent = from_section(attention_two, 1)
    in_two_slabs = jnp.split(add_ranks(in_here), chips, axis=-1)
    in_two_here = from_x(in_two_slabs)
    first_in = first_grad + core_sum(matmul(packed_low, weights[0][0]))
    attention_slabs = attention_grads(first_saved, attended_grad, packed_low)
    attention_here = from_x(attention_slabs)
    first_in, second_in_spread, *back_here = tie(first_in, second_in_spread, *back_here)
    back_one = add(back_slabs[0], back_here)
    back_sent = from_section(back_one, 0)
    first_in_spread = spread_rows(first_in.astype(LOW))
    second_placed = place_rows(second_in_spread, 1)

    back_sent, *in_one_here = tie(back_sent, *in_one_here)
    in_one = add(in_slabs[0], in_one_here)
    in_one_sent = from_section(in_one, 0)
    back_here = from_z(by_section(add(back_one, [back_sent]), back_two))
    in_two = add(in_two_slabs[0], in_two_here)
    in_two_sent = from_section(in_two, 1)
    attention_two = add(attention_two, [attention_sent])
    in_one_sent, *attention_here = tie(in_one_sent, *attention_here)
    attention_one = add(attention_slabs[0], attention_here)
    attention_one_sent = from_section(attention_one, 0)
    in_one_here = from_z(add(in_one, [in_one_sent]))
    in_two = add(in_two, [in_two_sent])
    back_shard = finish(add_ranks(back_here))
    first_placed = place_rows(first_in_spread, 0)
    attention_one = add(attention_one, [attention_one_sent])
    attention_here = from_z(by_section(attention_one, attention_two))
    input_grads = by_section(first_placed, second_placed).astype(WIDE)[None]
    in_shard = finish(by_section(add_ranks(in_one_here), in_two))
    attention_shard = finish(add_ranks(attention_here))
    qkv_shard, out_shard = attention_shard[:, : 3 * head_half], attention_shard[:, 3 * head_half :]
    qkv_grad = jnp.transpose(qkv_shard.reshape(2, 3, head_half, local), (3, 1, 0, 2)).reshape(local, 3, -1)
    out_grad_w = out_shard.reshape(-1, local)
    in_grad = jnp.transpose(in_shard.reshape(-1, local))
    back_grad = back_shard.reshape(-1, local)

    def spread_columns(row):
        blocks = row.reshape(ranks, 1, -1)
        both = jnp.where(jnp.arange(2)[None, :, None] == core, blocks, 0.0)
        return both.reshape(-1, width)

    tables = []
    for sums in (first_sums, second_sums):
        gain_two, bias_four, bias_five, inner_sum, gain_one, bias_two, bias_three, query_sum, value_sum = sums
        common = jnp.stack([gain_one, gain_two, bias_two, bias_three, bias_four, bias_five])
        common = jnp.where(core == 0, relative(common), 0.0)
        tables.append(
            jnp.concatenate(
                [common[:2], spread_columns(query_sum), spread_columns(value_sum), common[2:], spread_columns(inner_sum)]
            )
        )
    table = jnp.stack(tables)
    table = jnp.where(counted, table, 0.0) if repeats > 1 else table
    table = lax.dynamic_index_in_dim(lax.psum(table, AXES), section, 0, keepdims=False)
    sliced = lax.dynamic_slice_in_dim(table[: gain_count + bias_count], copy_at * local, local, 1)
    inner = lax.dynamic_index_in_dim(
        table[gain_count + bias_count :].reshape(copies, -1), copy_at, 0, keepdims=False
    )
    return (
        outputs,
        input_grads,
        qkv_grad[None],
        out_grad_w[None],
        in_grad[None],
        back_grad[None],
        sliced[None, :gain_count],
        sliced[None, gain_count:],
        inner[None],
    )


def solution(mesh):
    return jax.shard_map(
        on_device,
        mesh=mesh,
        in_specs=(
            P(None, ("dp", "tensor"), None),
            P(None, "dp", None),
            P("section", "dp", None, "tensor"),
            P("section", "tensor", "dp"),
            P("section", "dp", "tensor"),
            P("section", "tensor", "dp"),
            P("section", None, "dp"),
            P("section", None, "dp"),
            P("section", "dp"),
            P(None, ("dp", "tensor"), None),
        ),
        out_specs=(
            P("section", None, ("dp", "tensor"), None),
            P("section", None, ("dp", "tensor"), None),
            P("section", "dp", None, "tensor"),
            P("section", "tensor", "dp"),
            P("section", "dp", "tensor"),
            P("section", "tensor", "dp"),
            P("section", None, "dp"),
            P("section", None, "dp"),
            P("section", "dp"),
        ),
        check_vma=False,
    )
```

```python
import functools

import jax
import jax.numpy as jnp
from jax import lax
from jax.experimental import pallas as pl
from jax.experimental.pallas import tpu as pltpu
from jax.sharding import PartitionSpec as P

HEAD_DIM = 64
AXES = ("section", "dp", "tensor")
LOW = jnp.bfloat16
WIDE = jnp.float32


def move(value, target):
    sections, copies, ranks = (lax.axis_size(axis) for axis in AXES)
    pairs = []
    for s in range(sections):
        for d in range(copies):
            for t in range(ranks):
                goal = target(s, d, t)
                if goal is not None:
                    pairs.append(
                        ((s * copies + d) * ranks + t, (goal[0] * copies + goal[1]) * ranks + goal[2])
                    )
    return lax.ppermute(value, AXES, pairs)


def to_other_core(value):
    return move(value, lambda s, d, t: (s, d ^ 1, t))


def by_core(core, kept, received, axis):
    return jnp.where(
        core == 0,
        jnp.concatenate([kept, received], axis=axis),
        jnp.concatenate([received, kept], axis=axis),
    )


def choose(place, options):
    chosen = options[0]
    for at, option in enumerate(options[1:], 1):
        chosen = jnp.where(place == at, option, chosen)
    return chosen


def after(value, *others):
    return lax.optimization_barrier((value,) + others)[0]


def tie(*values):
    return lax.optimization_barrier(values)


def matmul(lhs_mat, rhs_mat):
    return jnp.dot(lhs_mat, rhs_mat, preferred_element_type=WIDE)


def lhs_inner(lhs_mat, rhs_mat):
    return lax.dot_general(
        lhs_mat, rhs_mat, (((0,), (0,)), ((), ())), preferred_element_type=WIDE
    )


def rhs_inner(lhs_mat, rhs_mat):
    return lax.dot_general(
        lhs_mat, rhs_mat, (((1,), (1,)), ((), ())), preferred_element_type=WIDE
    )


def core_sum(partial):
    low = partial.astype(LOW)
    return low.astype(WIDE) + to_other_core(low).astype(WIDE)


def norm_parts(summed):
    centered = summed - jnp.mean(summed, axis=-1, keepdims=True)
    variance = jnp.mean(centered * centered, axis=-1, keepdims=True)
    scale = lax.rsqrt(variance + 1e-05)
    return centered * scale, scale


def norm_backward(summed, gain_row, grad):
    unit, scale = norm_parts(summed)
    gain_grad = jnp.sum(grad * unit, axis=0)
    bias_grad = jnp.sum(grad, axis=0)
    inner = grad * gain_row
    result = scale * (
        inner
        - jnp.mean(inner, axis=-1, keepdims=True)
        - unit * jnp.mean(inner * unit, axis=-1, keepdims=True)
    )
    return result, gain_grad, bias_grad


def gelu_pair(values):
    below = 0.5 * (1.0 + lax.erf(values * (0.5**0.5)))
    density = jnp.exp(-0.5 * values * values) * (0.3989422804014327)
    return values * below, below + values * density


def segment_ids(seq_lens, row_count):
    seq_ends = jnp.cumsum(seq_lens)
    positions = jnp.arange(row_count, dtype=jnp.int32)
    return jnp.sum((positions[:, None] >= seq_ends[None, :]).astype(jnp.int32), axis=1)


def flash_params():
    return dict(
        cost_estimate=pl.CostEstimate(flops=0, transcendentals=0, bytes_accessed=0),
        compiler_params=pltpu.CompilerParams(vmem_limit_bytes=48 * 1024 * 1024),
    )


def head_lanes(values, head):
    lane = lax.broadcasted_iota(jnp.int32, values.shape, 1)
    return jnp.where((lane // HEAD_DIM) == head, values, jnp.zeros_like(values))


def keys_by_queries(keys, queries):
    return lax.dot_general(keys, queries, (((1,), (1,)), ((), ())), preferred_element_type=WIDE)


def key_windows(seq_lens, rows, size):
    widths = tuple(sorted({min(rows, width) for width in (512, 640, 768, rows)}))
    ends = jnp.cumsum(seq_lens)
    first = jnp.arange(rows // size, dtype=jnp.int32)[:, None] * size
    lowest = jnp.max(jnp.where(ends[None, :] <= first, ends[None, :], 0), axis=1)
    highest = jnp.min(jnp.where(ends[None, :] >= first + size, ends[None, :], rows), axis=1)
    start, kind = jnp.zeros_like(lowest), jnp.full_like(lowest, len(widths) - 1)
    for at in range(len(widths) - 2, -1, -1):
        begin = jnp.minimum(lowest // 128 * 128, rows - widths[at])
        fits = highest - begin <= widths[at]
        start = jnp.where(fits, begin, start)
        kind = jnp.where(fits, at, kind)
    return start.astype(jnp.int32), kind.astype(jnp.int32), widths


def each_width(kind, widths, body):
    for at, width in enumerate(widths):
        @pl.when(kind == at)
        def _(width=width):
            body(width)


def forward_kernel(
    widths, start_ref, kind_ref, query_ref, key_ref, value_ref, seg_key_ref, seg_query_ref, out_ref, logsum_ref
):
    block = pl.program_id(1)
    heads = query_ref.shape[1] // HEAD_DIM

    def body(width):
        window = pl.ds(pl.multiple_of(start_ref[block], 128), width)
        allowed = seg_key_ref[window, :] == seg_query_ref[...]
        queries = query_ref[...] * jnp.asarray(HEAD_DIM ** (-0.5), LOW)
        keys, values = key_ref[window, :], value_ref[window, :]
        parts = []
        for head in range(heads):
            scores = keys_by_queries(keys, head_lanes(queries, head))
            scores = jnp.where(allowed, scores, -1000000000.0)
            highest = jnp.max(scores, axis=0, keepdims=True)
            raised = jnp.exp(scores - highest)
            totals = jnp.sum(raised, axis=0, keepdims=True)
            context = lhs_inner(values, raised.astype(LOW))
            rows = slice(head * HEAD_DIM, (head + 1) * HEAD_DIM)
            parts.append(context[rows] / totals)
            logsum_ref[0, head : head + 1, :] = highest + jnp.log(totals)
        out_ref[...] = jnp.concatenate(parts, axis=0).T.astype(LOW)

    each_width(kind_ref[block], widths, body)


def backward_kernel(
    widths, start_ref, kind_ref, query_ref, key_ref, value_ref, seg_key_ref, seg_query_ref, logsum_ref, grad_ref,
    out_ref, sum_ref, key_grad, value_grad,
):
    block = pl.program_id(1)
    size, lanes = query_ref.shape
    heads = lanes // HEAD_DIM
    factor = HEAD_DIM ** (-0.5)

    @pl.when(block == 0)
    def _():
        key_grad[...] = jnp.zeros_like(key_grad)
        value_grad[...] = jnp.zeros_like(value_grad)
        sum_ref[...] = jnp.zeros_like(sum_ref)

    def body(width):
        window = pl.ds(pl.multiple_of(start_ref[block], 128), width)
        allowed = seg_key_ref[window, :] == seg_query_ref[...]
        queries = query_ref[...] * jnp.asarray(factor, LOW)
        grads = grad_ref[...]
        keys, values = key_ref[window, :], value_ref[window, :]
        weight_low, score_low, query_heads, grad_heads, query_parts = [], [], [], [], []
        for head in range(heads):
            query_head, grad_head = head_lanes(queries, head), head_lanes(grads, head)
            scores = jnp.where(allowed, keys_by_queries(keys, query_head), -1000000000.0)
            weights = jnp.exp(scores - logsum_ref[0, head : head + 1, :])
            weight_grad = keys_by_queries(values, grad_head)
            centre = jnp.sum(weight_grad * weights, axis=0, keepdims=True)
            score_grad = (weights * (weight_grad - centre)).astype(LOW)
            rows = slice(head * HEAD_DIM, (head + 1) * HEAD_DIM)
            query_parts.append(lhs_inner(keys, score_grad)[rows] * factor)
            weight_low.append(weights.astype(LOW))
            score_low.append(score_grad)
            query_heads.append(query_head)
            grad_heads.append(grad_head)
        key_grad[window, :] += matmul(
            jnp.concatenate(score_low, axis=1), jnp.concatenate(query_heads, axis=0)
        )
        value_grad[window, :] += matmul(
            jnp.concatenate(weight_low, axis=1), jnp.concatenate(grad_heads, axis=0)
        )
        query_grad = jnp.concatenate(query_parts, axis=0).T
        out_ref[pl.ds(pl.multiple_of(block * size, size), size), :lanes] = query_grad.astype(LOW)
        sum_ref[0, 0:1, :] += jnp.sum(query_grad, axis=0, keepdims=True)

    each_width(kind_ref[block], widths, body)

    @pl.when(block == pl.num_programs(1) - 1)
    def _():
        out_ref[:, lanes : 2 * lanes] = key_grad[...].astype(LOW)
        out_ref[:, 2 * lanes :] = value_grad[...].astype(LOW)
        sum_ref[0, 1:2, :] = jnp.sum(value_grad[...], axis=0, keepdims=True)


def attention_specs(rows, lanes, size):
    return [
        pl.BlockSpec((size, lanes), lambda pair, block, *_: (block, 3 * pair)),
        pl.BlockSpec((rows, lanes), lambda pair, block, *_: (0, 3 * pair + 1)),
        pl.BlockSpec((rows, lanes), lambda pair, block, *_: (0, 3 * pair + 2)),
        pl.BlockSpec((rows, 1), lambda pair, block, *_: (0, 0)),
        pl.BlockSpec((1, size), lambda pair, block, *_: (0, block)),
    ]


def attend_forward(packed, segments, seq_lens, lanes):
    rows = packed.shape[0]
    pairs = packed.shape[1] // (3 * lanes)
    heads = lanes // HEAD_DIM
    size = min(256, rows)
    start, kind, widths = key_windows(seq_lens, rows, size)
    return pl.pallas_call(
        functools.partial(forward_kernel, widths),
        grid_spec=pltpu.PrefetchScalarGridSpec(
            num_scalar_prefetch=2,
            grid=(pairs, rows // size),
            in_specs=attention_specs(rows, lanes, size),
            out_specs=[
                pl.BlockSpec((size, lanes), lambda pair, block, *_: (block, pair)),
                pl.BlockSpec((1, heads, size), lambda pair, block, *_: (pair, 0, block)),
            ],
        ),
        out_shape=[
            jax.ShapeDtypeStruct((rows, pairs * lanes), LOW),
            jax.ShapeDtypeStruct((pairs, heads, rows), WIDE),
        ],
        **flash_params(),
    )(start, kind, packed, packed, packed, segments[:, None], segments[None, :])


def attend_backward(packed, segments, seq_lens, logsums, context_grad, lanes):
    rows = packed.shape[0]
    pairs = packed.shape[1] // (3 * lanes)
    heads = lanes // HEAD_DIM
    size = min(256, rows)
    start, kind, widths = key_windows(seq_lens, rows, size)
    return pl.pallas_call(
        functools.partial(backward_kernel, widths),
        grid_spec=pltpu.PrefetchScalarGridSpec(
            num_scalar_prefetch=2,
            grid=(pairs, rows // size),
            in_specs=attention_specs(rows, lanes, size)
            + [
                pl.BlockSpec((1, heads, size), lambda pair, block, *_: (pair, 0, block)),
                pl.BlockSpec((size, lanes), lambda pair, block, *_: (block, pair)),
            ],
            out_specs=[
                pl.BlockSpec((rows, 3 * lanes), lambda pair, block, *_: (0, pair)),
                pl.BlockSpec((1, 2, lanes), lambda pair, block, *_: (pair, 0, 0)),
            ],
            scratch_shapes=[pltpu.VMEM((rows, lanes), WIDE), pltpu.VMEM((rows, lanes), WIDE)],
        ),
        out_shape=[
            jax.ShapeDtypeStruct((rows, pairs * 3 * lanes), LOW),
            jax.ShapeDtypeStruct((pairs, 2, lanes), WIDE),
        ],
        **flash_params(),
    )(start, kind, packed, packed, packed, segments[:, None], segments[None, :], logsums, context_grad)


def pair_columns(packed, head_half, lanes, back=False):
    ranks = lanes // head_half
    if ranks == 1:
        return packed
    order = (3, ranks) if back else (ranks, 3)
    shaped = packed.reshape(packed.shape[0], -1, order[0], order[1], head_half)
    return jnp.swapaxes(shaped, 2, 3).reshape(packed.shape)


def layer_forward(rows, segments, seq_lens, weights, small, late_weights=None):
    w_qkv, w_out, w_in = weights[:3]
    gains, biases, offset, inner_bias, head_half = small
    lanes = max(head_half, 128)
    packed = (rhs_inner(rows, w_qkv) + offset).astype(LOW)
    packed = pair_columns(packed, head_half, lanes)
    context, logsums = attend_forward(packed, segments, seq_lens, lanes)
    first_sum = rows.astype(WIDE) + core_sum(matmul(context, w_out)) + biases[2]
    middle = (norm_parts(first_sum)[0] * gains[0] + biases[3]).astype(LOW)
    active, slope = gelu_pair(rhs_inner(middle, w_in) + inner_bias)
    active, slope = active.astype(LOW), slope.astype(LOW)
    if late_weights is None:
        w_back = weights[3]
    else:
        active, late = late_weights(active)
        w_back = late[0]
    second_sum = middle.astype(WIDE) + core_sum(matmul(active, w_back)) + biases[4]
    result = norm_parts(second_sum)[0] * gains[1] + biases[5]
    saved = (rows, packed, logsums, context, first_sum, middle, active, slope, second_sum)
    return result, saved, late if late_weights is not None else None


def slab_grads(hidden, features, chips):
    cut = features.shape[1] // chips
    return [lhs_inner(hidden, features[:, k * cut : (k + 1) * cut]).astype(LOW) for k in range(chips)]


def backward_hidden(saved, grad_rows, weights, small):
    _, _, w_in, w_back = weights
    gains = small[0]
    middle, active, slope, second_sum = saved[5:]
    second_grad, gain_two, bias_two = norm_backward(second_sum, gains[1], grad_rows.astype(WIDE))
    branch_grad = second_grad.astype(LOW)
    hidden_low = (rhs_inner(branch_grad, w_back) * slope.astype(WIDE)).astype(LOW)
    middle_grad = second_grad + core_sum(matmul(hidden_low, w_in))
    inner_sum = matmul(jnp.ones((8, hidden_low.shape[0]), LOW), hidden_low)[0]
    sums = (gain_two, jnp.sum(second_grad, axis=0), bias_two, inner_sum)
    return middle_grad, branch_grad, hidden_low, sums


def backward_attention(saved, segments, seq_lens, middle_grad, weights, small):
    _, w_out, _, _ = weights
    gains, head_half = small[0], small[4]
    _, packed, logsums, _, first_sum = saved[:5]
    first_grad, gain_one, bias_one = norm_backward(first_sum, gains[0], middle_grad)
    attended_grad = first_grad.astype(LOW)
    context_grad = rhs_inner(attended_grad, w_out).astype(LOW)
    lanes = max(head_half, 128)
    packed_low, column_sums = attend_backward(packed, segments, seq_lens, logsums, context_grad, lanes)
    packed_low = pair_columns(packed_low, head_half, lanes, back=True)
    sums = (gain_one, jnp.sum(first_grad, axis=0), bias_one) + tuple(
        column_sums[:, at].reshape(-1) for at in range(2)
    )
    return first_grad, attended_grad, packed_low, sums


def on_device(
    block_input, seq_lengths, w_qkv, w_out, w_in, w_back, gains, biases, ffn_bias, out_grad
):
    ranks = lax.axis_size("tensor")
    copies = lax.axis_size("dp")
    chips = copies // 2
    section = lax.axis_index("section")
    copy_at = lax.axis_index("dp")
    rank = lax.axis_index("tensor")
    core = copy_at % 2
    chip = copy_at // 2
    micro_count, own_rows, width = block_input.shape
    repeats = ranks // micro_count
    local = gains.shape[-1]
    counted = (rank % repeats) == 0

    def relative(value):
        slabs = jnp.split(value, chips, axis=-1)
        return jnp.concatenate([choose(chip ^ k, slabs) for k in range(chips)], axis=-1)

    def fetch_rows(block, *before):
        half = own_rows // 2
        kept = choose(core, (block[:, :half], block[:, half:]))
        given = choose(core, (block[:, half:], block[:, :half]))
        received = move(given, lambda s, d, t: (s, d ^ 1, t) if d % 2 == s else None)
        mine = jnp.where(core == section, kept, received)
        mine = jnp.repeat(mine, repeats, axis=0) if repeats > 1 else mine
        mine = after(mine, *before) if before else mine
        mine = lax.all_to_all(mine, "tensor", split_axis=0, concat_axis=0, tiled=True)
        whole = by_core(core, mine, to_other_core(mine), 1)
        return relative(whole.reshape(ranks * own_rows, width))

    def spread_both(first, second):
        chosen = relative(jnp.where(core == 0, first, second)).reshape(ranks, own_rows, width)
        spread = lax.all_to_all(chosen, "tensor", split_axis=0, concat_axis=0, tiled=True)
        return spread.reshape(micro_count, repeats, own_rows, width)[:, 0]

    def place_both(spread):
        return move(spread, lambda s, d, t: (d % 2, (d // 2) * 2 + s, t))

    def spread_rows(value):
        parts = relative(value).reshape(ranks, own_rows, width)
        half = own_rows // 2
        mine = choose(core, (parts[:, :half], parts[:, half:]))
        spread = lax.all_to_all(mine, "tensor", split_axis=0, concat_axis=0, tiled=True)
        return spread.reshape((micro_count, repeats) + spread.shape[1:])[:, 0]

    def place_rows(spread, layer):
        halves = [
            move(spread, lambda s, d, t: (layer, (d // 2) * 2 + s, t) if d % 2 == half else None)
            for half in range(2)
        ]
        return jnp.concatenate(halves, axis=1)

    def by_section(first, second):
        return jnp.where(section == 0, first, second)

    def own_half(halves):
        kept = choose(core, (halves[0], halves[1]))
        given = choose(core, (halves[1], halves[0]))
        return by_core(core, kept, to_other_core(given), 1)

    def relay(upward, downward):
        upward.append(move(upward[-1], lambda s, d, t: (s, d, t + 1) if t + 1 < ranks else None))
        downward.append(move(downward[-1], lambda s, d, t: (s, d, t - 1) if t > 0 else None))

    def assemble(upward, downward):
        own = upward[0]
        item = jnp.zeros((ranks,) + own.shape, LOW)
        item = lax.dynamic_update_index_in_dim(item, own, rank, 0)
        for j in range(1, ranks):
            arrived = jnp.where(rank >= j, upward[j], downward[ranks - j])
            item = lax.dynamic_update_index_in_dim(item, arrived, (rank + ranks - j) % ranks, 0)
        return item

    def over_ranks(own):
        upward, downward = [own], [own]
        for _ in range(1, ranks):
            relay(upward, downward)
        return assemble(upward, downward)

    def chips_once(item):
        across = move(item, lambda s, d, t: (1 - s, d, t))
        along = [move(item, lambda s, d, t: (s, d ^ (2 * k), t)) for k in range(1, chips)]
        return across, along

    def chips_twice(item, across, along):
        part = item.shape[0] // 2
        far = []
        for k in range(1, chips):
            upper = move(across[:part], lambda s, d, t: (s, d ^ (2 * k), t))
            lower = move(along[k - 1][part:], lambda s, d, t: (1 - s, d, t))
            far.append(jnp.concatenate([upper, lower], axis=0))
        mine, other = [item] + along, [across] + far
        result = []
        for layer in range(2):
            slabs = [jnp.where(section == layer, m, o) for m, o in zip(mine, other)]
            result.append(jnp.concatenate(slabs, axis=-1))
        return result

    def over_chips(item):
        return chips_twice(item, *chips_once(item))

    def from_x(slabs):
        return [move(slabs[k], lambda s, d, t: (s, d ^ (2 * k), t)) for k in range(1, chips)]

    def from_section(part, layer):
        return move(part, lambda s, d, t: (layer, d, t) if s != layer else None)

    def add(part, received):
        total = part.astype(WIDE)
        for other in received:
            total = total + other.astype(WIDE)
        return total.astype(LOW)

    def from_z(parts):
        return lax.all_to_all(parts, "tensor", split_axis=0, concat_axis=0, tiled=True)

    def add_ranks(parts):
        return jnp.sum(parts.astype(WIDE), axis=0).astype(LOW)

    def ranked(slab):
        return slab.reshape((ranks, -1) + slab.shape[1:])

    def counted_only(slabs):
        return [jnp.where(counted, slab, jnp.zeros((), LOW)) for slab in slabs] if repeats > 1 else slabs

    def finish(shard):
        parts = jnp.split(shard, 2, axis=1)
        kept = choose(core, parts)
        given = choose(core, parts[::-1])
        return by_core(core, kept[None], to_other_core(given)[None], 0).astype(WIDE)

    head_half = w_qkv.shape[-1] // 2
    hidden_half = w_in.shape[-1] // 2
    in_first = jnp.moveaxis(w_in[0].reshape(local, 2, hidden_half), 0, 2)
    qkv_first = jnp.transpose(w_qkv[0].reshape(local, 3, 2, head_half), (2, 1, 3, 0))
    qkv_first = qkv_first.reshape(2, 3 * head_half, local)
    out_first = w_out[0].reshape(2, head_half, local)
    back_first = w_back[0].reshape(2, hidden_half, local)
    later = hidden_half // 2
    attention_own = own_half(jnp.concatenate([qkv_first, out_first], axis=1))
    back_own = own_half(back_first)
    in_own = own_half(in_first)
    back_two = jnp.stack(over_chips(back_own[later:]))
    attention_item = over_ranks(attention_own)
    attention_item, back_two = tie(attention_item, back_two)
    across, along = chips_once(attention_item)
    rows = fetch_rows(block_input, attention_item)
    in_own = after(in_own, attention_item)
    upward, downward = [in_own], [in_own]
    for at in range(1, ranks):
        relay(upward, downward)
        if at == ranks // 2:
            upward[-1], downward[-1], across, *along = tie(upward[-1], downward[-1], across, *along)
            attention_all = chips_twice(attention_item, across, along)
    upward[-1], downward[-1], gains, seq_lengths = tie(upward[-1], downward[-1], gains, seq_lengths)
    in_item = assemble(upward, downward)
    in_all = over_chips(in_item)
    back_item = over_ranks(after(back_own[:later], in_item))
    across, along = chips_once(back_item)
    back_two = after(back_two, back_item)
    upward, downward = [back_two], [back_two]
    for _ in range(1, ranks):
        relay(upward, downward)

    def late_weights(active):
        tied = tie(active, across, upward[-1], downward[-1], *along)
        halves = zip(
            chips_twice(back_item, tied[1], list(tied[4:])),
            jnp.moveaxis(assemble(upward[:-1] + [tied[2]], downward[:-1] + [tied[3]]), 1, 0),
        )
        return tied[0], [jnp.concatenate(pair, axis=1).reshape(-1, width) for pair in halves]

    weights = [
        (
            attention_all[layer][:, : 3 * head_half].reshape(-1, width),
            attention_all[layer][:, 3 * head_half :].reshape(-1, width),
            in_all[layer].reshape(-1, width),
        )
        for layer in range(2)
    ]

    gain_count, bias_count = gains.shape[1], biases.shape[1]
    packed_small = jnp.concatenate([gains, biases, ffn_bias.reshape(1, -1, local)], axis=1)
    table_parts = [
        [
            packed_small
            if a == 0 and b == 0
            else move(packed_small, lambda s, d, t: (s ^ a, d ^ b, t))
            for b in range(copies)
        ]
        for a in range(2)
    ]
    table_all = jnp.stack([jnp.stack(row) for row in table_parts])[:, :, 0].astype(WIDE)
    small_all = jnp.stack([choose(section, (table_all[at], table_all[1 - at])) for at in range(2)])
    order = [[at ^ b for b in range(copies)] for at in range(copies)]
    small_all = jnp.stack(
        [choose(copy_at, [small_all[:, order[at][b]] for b in range(copies)]) for at in range(copies)],
        axis=1,
    )

    def head_columns(row):
        halves = row.reshape(ranks, 2, -1)
        return choose(core, (halves[:, 0], halves[:, 1])).reshape(-1)

    small = []
    for layer in range(2):
        table = jnp.moveaxis(small_all[layer, :, : gain_count + bias_count], 0, 1).reshape(-1, width)
        query_bias = head_columns(table[gain_count])
        value_bias = head_columns(table[gain_count + 1])
        query_bias, value_bias = query_bias.reshape(ranks, 1, -1), value_bias.reshape(ranks, 1, -1)
        offset = jnp.concatenate([query_bias, jnp.zeros_like(query_bias), value_bias], axis=1).reshape(-1)
        inner_bias = head_columns(small_all[layer, :, gain_count + bias_count :].reshape(-1))
        table = relative(table)
        small.append((table[:gain_count], table[gain_count:], offset, inner_bias, head_half))

    lengths = jnp.where(core == section, seq_lengths, to_other_core(seq_lengths))[:, 0]
    lengths = lax.dynamic_index_in_dim(lengths, rank // repeats, 0, keepdims=False)
    segments = segment_ids(lengths, ranks * own_rows)
    live = (segments < lengths.shape[0])[:, None]

    first_out, first_saved, late = layer_forward(rows, segments, lengths, weights[0], small[0], late_weights)
    weights = [weights[layer] + (late[layer],) for layer in range(2)]
    first_low = first_out.astype(LOW)
    cotangent = fetch_rows(out_grad, back_two)
    cotangent = jnp.where(live, cotangent, jnp.zeros((), LOW))
    second_out, second_saved, _ = layer_forward(first_low, segments, lengths, weights[1], small[1])
    spread = spread_both(first_low, second_out.astype(LOW))

    def hidden_grads(hidden, features):
        return [ranked(slab) for slab in counted_only(slab_grads(hidden, features, chips))]

    def attention_grads(saved, attended_grad, packed_low):
        qkv = hidden_grads(packed_low, saved[0])
        out = hidden_grads(saved[3], attended_grad)
        return [jnp.concatenate(pair, axis=1) for pair in zip(qkv, out)]

    middle_grad, branch_grad, hidden_low, second_sums = backward_hidden(
        second_saved, cotangent, weights[1], small[1]
    )
    back_slabs = hidden_grads(second_saved[6], branch_grad)
    back_here = from_x(back_slabs)
    in_slabs = hidden_grads(hidden_low, second_saved[5])
    in_here = from_x(in_slabs)
    first_grad, attended_grad, packed_low, more_sums = backward_attention(
        second_saved, segments, lengths, middle_grad, weights[1], small[1]
    )
    second_sums += more_sums
    packed_low, spread, *back_here = tie(packed_low, spread, *back_here)
    back_two = add(back_slabs[0], back_here)
    back_sent = from_section(back_two, 1)
    placed = place_both(spread)
    second_in = first_grad + core_sum(matmul(packed_low, weights[1][0]))
    qkv, out = [
        ranked(counted_only([lhs_inner(hidden, features).astype(LOW)])[0])
        for hidden, features in ((packed_low, second_saved[0]), (second_saved[3], attended_grad))
    ]
    attention_here = from_z(jnp.concatenate([qkv, out], axis=1))
    second_low = second_in.astype(LOW)

    middle_grad, branch_grad, hidden_low, first_sums = backward_hidden(
        first_saved, second_low, weights[0], small[0]
    )
    middle_grad, back_sent, placed, *in_here = tie(middle_grad, back_sent, placed, *in_here)
    back_two = add(back_two, [back_sent])
    in_two = add(in_slabs[0], in_here)
    in_sent = from_section(in_two, 1)
    outputs = placed.astype(WIDE)[None]
    second_in_spread = spread_rows(second_low)
    back_slabs = hidden_grads(first_saved[6], branch_grad)
    back_here = from_x(back_slabs)
    in_slabs = hidden_grads(hidden_low, first_saved[5])
    in_here = from_x(in_slabs)
    first_grad, attended_grad, packed_low, more_sums = backward_attention(
        first_saved, segments, lengths, middle_grad, weights[0], small[0]
    )
    first_sums += more_sums
    packed_low, in_sent, second_in_spread, *back_here = tie(packed_low, in_sent, second_in_spread, *back_here)
    in_two = add(in_two, [in_sent])
    back_one = add(back_slabs[0], back_here)
    back_sent = from_section(back_one, 0)
    second_placed = place_rows(second_in_spread, 1)
    first_in = first_grad + core_sum(matmul(packed_low, weights[0][0]))
    attention_slabs = attention_grads(first_saved, attended_grad, packed_low)
    attention_one_here = from_x(attention_slabs)
    first_in, attention_here, *in_here = tie(first_in, attention_here, *in_here)
    first_in_spread = spread_rows(first_in.astype(LOW))
    in_one = add(in_slabs[0], in_here)
    in_sent = from_section(in_one, 0)
    attention_two_slabs = jnp.split(add_ranks(attention_here), chips, axis=-1)
    attention_two_here = from_x(attention_two_slabs)

    back_sent, *attention_one_here = tie(back_sent, *attention_one_here)
    back_here = from_z(by_section(add(back_one, [back_sent]), back_two))
    attention_one = add(attention_slabs[0], attention_one_here)
    attention_one_sent = from_section(attention_one, 0)
    attention_two = add(attention_two_slabs[0], attention_two_here)
    attention_two_sent = from_section(attention_two, 1)
    in_here = from_z(by_section(add(in_one, [in_sent]), in_two))
    first_placed = place_rows(first_in_spread, 0)
    attention_one_sent, attention_two_sent, back_here = tie(attention_one_sent, attention_two_sent, back_here)
    attention_one = add(attention_one, [attention_one_sent])
    attention_two = add(attention_two, [attention_two_sent])
    back_shard = finish(add_ranks(back_here))
    input_grads = by_section(first_placed, second_placed).astype(WIDE)[None]
    attention_here = from_z(attention_one)
    in_shard = finish(add_ranks(in_here))

    def spread_columns(row):
        blocks = row.reshape(ranks, 1, -1)
        both = jnp.where(jnp.arange(2)[None, :, None] == core, blocks, 0.0)
        return both.reshape(-1, width)

    tables = []
    for sums in (first_sums, second_sums):
        gain_two, bias_four, bias_five, inner_sum, gain_one, bias_two, bias_three, query_sum, value_sum = sums
        common = jnp.stack([gain_one, gain_two, bias_two, bias_three, bias_four, bias_five])
        common = jnp.where(core == 0, relative(common), 0.0)
        tables.append(
            jnp.concatenate(
                [common[:2], spread_columns(query_sum), spread_columns(value_sum), common[2:], spread_columns(inner_sum)]
            )
        )
    table = jnp.stack(tables)
    table = jnp.where(counted, table, 0.0) if repeats > 1 else table
    table = lax.psum(table, AXES)
    attention_here, table = tie(attention_here, table)
    attention_shard = finish(by_section(add_ranks(attention_here), attention_two))
    qkv_shard, out_shard = attention_shard[:, : 3 * head_half], attention_shard[:, 3 * head_half :]
    qkv_grad = jnp.transpose(qkv_shard.reshape(2, 3, head_half, local), (3, 1, 0, 2)).reshape(local, 3, -1)
    out_grad_w = out_shard.reshape(-1, local)
    in_grad = jnp.transpose(in_shard.reshape(-1, local))
    back_grad = back_shard.reshape(-1, local)
    table = choose(section, (table[0], table[1]))
    sliced = lax.dynamic_slice_in_dim(table[: gain_count + bias_count], copy_at * local, local, 1)
    inner = lax.dynamic_index_in_dim(
        table[gain_count + bias_count :].reshape(copies, -1), copy_at, 0, keepdims=False
    )
    return (
        outputs,
        input_grads,
        qkv_grad[None],
        out_grad_w[None],
        in_grad[None],
        back_grad[None],
        sliced[None, :gain_count],
        sliced[None, gain_count:],
        inner[None],
    )


def solution(mesh):
    return jax.shard_map(
        on_device,
        mesh=mesh,
        in_specs=(
            P(None, ("dp", "tensor"), None),
            P(None, "dp", None),
            P("section", "dp", None, "tensor"),
            P("section", "tensor", "dp"),
            P("section", "dp", "tensor"),
            P("section", "tensor", "dp"),
            P("section", None, "dp"),
            P("section", None, "dp"),
            P("section", "dp"),
            P(None, ("dp", "tensor"), None),
        ),
        out_specs=(
            P("section", None, ("dp", "tensor"), None),
            P("section", None, ("dp", "tensor"), None),
            P("section", "dp", None, "tensor"),
            P("section", "tensor", "dp"),
            P("section", "dp", "tensor"),
            P("section", "tensor", "dp"),
            P("section", None, "dp"),
            P("section", None, "dp"),
            P("section", "dp"),
        ),
        check_vma=False,
    )
```

```python
import functools

import jax
import jax.numpy as jnp
from jax import lax
from jax.experimental import pallas as pl
from jax.experimental.pallas import tpu as pltpu
from jax.sharding import PartitionSpec as P

HEAD_DIM = 64
AXES = ("section", "dp", "tensor")
LOW = jnp.bfloat16
WIDE = jnp.float32


def move(value, target):
    sections, copies, ranks = (lax.axis_size(axis) for axis in AXES)
    pairs = []
    for s in range(sections):
        for d in range(copies):
            for t in range(ranks):
                goal = target(s, d, t)
                if goal is not None:
                    pairs.append(
                        ((s * copies + d) * ranks + t, (goal[0] * copies + goal[1]) * ranks + goal[2])
                    )
    return lax.ppermute(value, AXES, pairs)


def to_other_core(value):
    return move(value, lambda s, d, t: (s, d ^ 1, t))


def by_core(core, kept, received, axis):
    return jnp.where(
        core == 0,
        jnp.concatenate([kept, received], axis=axis),
        jnp.concatenate([received, kept], axis=axis),
    )


def choose(place, options):
    chosen = options[0]
    for at, option in enumerate(options[1:], 1):
        chosen = jnp.where(place == at, option, chosen)
    return chosen


def after(value, *others):
    return lax.optimization_barrier((value,) + others)[0]


def tie(*values):
    return lax.optimization_barrier(values)


def matmul(lhs_mat, rhs_mat):
    return jnp.dot(lhs_mat, rhs_mat, preferred_element_type=WIDE)


def lhs_inner(lhs_mat, rhs_mat):
    return lax.dot_general(
        lhs_mat, rhs_mat, (((0,), (0,)), ((), ())), preferred_element_type=WIDE
    )


def rhs_inner(lhs_mat, rhs_mat):
    return lax.dot_general(
        lhs_mat, rhs_mat, (((1,), (1,)), ((), ())), preferred_element_type=WIDE
    )


def core_sum(partial):
    low = partial.astype(LOW)
    return low.astype(WIDE) + to_other_core(low).astype(WIDE)


def norm_parts(summed):
    centered = summed - jnp.mean(summed, axis=-1, keepdims=True)
    variance = jnp.mean(centered * centered, axis=-1, keepdims=True)
    scale = lax.rsqrt(variance + 1e-05)
    return centered * scale, scale


def norm_backward(summed, gain_row, grad):
    unit, scale = norm_parts(summed)
    gain_grad = jnp.sum(grad * unit, axis=0)
    bias_grad = jnp.sum(grad, axis=0)
    inner = grad * gain_row
    result = scale * (
        inner
        - jnp.mean(inner, axis=-1, keepdims=True)
        - unit * jnp.mean(inner * unit, axis=-1, keepdims=True)
    )
    return result, gain_grad, bias_grad


def gelu_pair(values):
    below = 0.5 * (1.0 + lax.erf(values * (0.5**0.5)))
    density = jnp.exp(-0.5 * values * values) * (0.3989422804014327)
    return values * below, below + values * density


def segment_ids(seq_lens, row_count):
    seq_ends = jnp.cumsum(seq_lens)
    positions = jnp.arange(row_count, dtype=jnp.int32)
    return jnp.sum((positions[:, None] >= seq_ends[None, :]).astype(jnp.int32), axis=1)


def flash_params():
    return dict(
        cost_estimate=pl.CostEstimate(flops=0, transcendentals=0, bytes_accessed=0),
        compiler_params=pltpu.CompilerParams(vmem_limit_bytes=48 * 1024 * 1024),
    )


def head_lanes(values, head):
    lane = lax.broadcasted_iota(jnp.int32, values.shape, 1)
    return jnp.where((lane // HEAD_DIM) == head, values, jnp.zeros_like(values))


def keys_by_queries(keys, queries):
    return lax.dot_general(keys, queries, (((1,), (1,)), ((), ())), preferred_element_type=WIDE)


def key_windows(seq_lens, rows, size):
    widths = tuple(sorted({min(rows, width) for width in (512, 640, 768, rows)}))
    ends = jnp.cumsum(seq_lens)
    first = jnp.arange(rows // size, dtype=jnp.int32)[:, None] * size
    lowest = jnp.max(jnp.where(ends[None, :] <= first, ends[None, :], 0), axis=1)
    highest = jnp.min(jnp.where(ends[None, :] >= first + size, ends[None, :], rows), axis=1)
    start, kind = jnp.zeros_like(lowest), jnp.full_like(lowest, len(widths) - 1)
    for at in range(len(widths) - 2, -1, -1):
        begin = jnp.minimum(lowest // 128 * 128, rows - widths[at])
        fits = highest - begin <= widths[at]
        start = jnp.where(fits, begin, start)
        kind = jnp.where(fits, at, kind)
    return start.astype(jnp.int32), kind.astype(jnp.int32), widths


def each_width(kind, widths, body):
    for at, width in enumerate(widths):
        @pl.when(kind == at)
        def _(width=width):
            body(width)


def forward_kernel(
    widths, start_ref, kind_ref, query_ref, key_ref, value_ref, seg_key_ref, seg_query_ref, out_ref, logsum_ref
):
    block = pl.program_id(1)
    heads = query_ref.shape[1] // HEAD_DIM

    def body(width):
        window = pl.ds(pl.multiple_of(start_ref[block], 128), width)
        allowed = seg_key_ref[window, :] == seg_query_ref[...]
        queries = query_ref[...] * jnp.asarray(HEAD_DIM ** (-0.5), LOW)
        keys, values = key_ref[window, :], value_ref[window, :]
        parts = []
        for head in range(heads):
            scores = keys_by_queries(keys, head_lanes(queries, head))
            scores = jnp.where(allowed, scores, -1000000000.0)
            highest = jnp.max(scores, axis=0, keepdims=True)
            raised = jnp.exp(scores - highest)
            totals = jnp.sum(raised, axis=0, keepdims=True)
            context = lhs_inner(values, raised.astype(LOW))
            rows = slice(head * HEAD_DIM, (head + 1) * HEAD_DIM)
            parts.append(context[rows] / totals)
            logsum_ref[0, head : head + 1, :] = highest + jnp.log(totals)
        out_ref[...] = jnp.concatenate(parts, axis=0).T.astype(LOW)

    each_width(kind_ref[block], widths, body)


def backward_kernel(
    widths, start_ref, kind_ref, query_ref, key_ref, value_ref, seg_key_ref, seg_query_ref, logsum_ref, grad_ref,
    out_ref, sum_ref, key_grad, value_grad,
):
    block = pl.program_id(1)
    size, lanes = query_ref.shape
    heads = lanes // HEAD_DIM
    factor = HEAD_DIM ** (-0.5)

    @pl.when(block == 0)
    def _():
        key_grad[...] = jnp.zeros_like(key_grad)
        value_grad[...] = jnp.zeros_like(value_grad)
        sum_ref[...] = jnp.zeros_like(sum_ref)

    def body(width):
        window = pl.ds(pl.multiple_of(start_ref[block], 128), width)
        allowed = seg_key_ref[window, :] == seg_query_ref[...]
        queries = query_ref[...] * jnp.asarray(factor, LOW)
        grads = grad_ref[...]
        keys, values = key_ref[window, :], value_ref[window, :]
        weight_low, score_low, query_heads, grad_heads, query_parts = [], [], [], [], []
        for head in range(heads):
            query_head, grad_head = head_lanes(queries, head), head_lanes(grads, head)
            scores = jnp.where(allowed, keys_by_queries(keys, query_head), -1000000000.0)
            weights = jnp.exp(scores - logsum_ref[0, head : head + 1, :])
            weight_grad = keys_by_queries(values, grad_head)
            centre = jnp.sum(weight_grad * weights, axis=0, keepdims=True)
            score_grad = (weights * (weight_grad - centre)).astype(LOW)
            rows = slice(head * HEAD_DIM, (head + 1) * HEAD_DIM)
            query_parts.append(lhs_inner(keys, score_grad)[rows] * factor)
            weight_low.append(weights.astype(LOW))
            score_low.append(score_grad)
            query_heads.append(query_head)
            grad_heads.append(grad_head)
        key_grad[window, :] += matmul(
            jnp.concatenate(score_low, axis=1), jnp.concatenate(query_heads, axis=0)
        )
        value_grad[window, :] += matmul(
            jnp.concatenate(weight_low, axis=1), jnp.concatenate(grad_heads, axis=0)
        )
        query_grad = jnp.concatenate(query_parts, axis=0).T
        out_ref[pl.ds(pl.multiple_of(block * size, size), size), :lanes] = query_grad.astype(LOW)
        sum_ref[0, 0:1, :] += jnp.sum(query_grad, axis=0, keepdims=True)

    each_width(kind_ref[block], widths, body)

    @pl.when(block == pl.num_programs(1) - 1)
    def _():
        out_ref[:, lanes : 2 * lanes] = key_grad[...].astype(LOW)
        out_ref[:, 2 * lanes :] = value_grad[...].astype(LOW)
        sum_ref[0, 1:2, :] = jnp.sum(value_grad[...], axis=0, keepdims=True)


def attention_specs(rows, lanes, size):
    return [
        pl.BlockSpec((size, lanes), lambda pair, block, *_: (block, 3 * pair)),
        pl.BlockSpec((rows, lanes), lambda pair, block, *_: (0, 3 * pair + 1)),
        pl.BlockSpec((rows, lanes), lambda pair, block, *_: (0, 3 * pair + 2)),
        pl.BlockSpec((rows, 1), lambda pair, block, *_: (0, 0)),
        pl.BlockSpec((1, size), lambda pair, block, *_: (0, block)),
    ]


def attend_forward(packed, segments, seq_lens, lanes):
    rows = packed.shape[0]
    pairs = packed.shape[1] // (3 * lanes)
    heads = lanes // HEAD_DIM
    size = min(256, rows)
    start, kind, widths = key_windows(seq_lens, rows, size)
    return pl.pallas_call(
        functools.partial(forward_kernel, widths),
        grid_spec=pltpu.PrefetchScalarGridSpec(
            num_scalar_prefetch=2,
            grid=(pairs, rows // size),
            in_specs=attention_specs(rows, lanes, size),
            out_specs=[
                pl.BlockSpec((size, lanes), lambda pair, block, *_: (block, pair)),
                pl.BlockSpec((1, heads, size), lambda pair, block, *_: (pair, 0, block)),
            ],
        ),
        out_shape=[
            jax.ShapeDtypeStruct((rows, pairs * lanes), LOW),
            jax.ShapeDtypeStruct((pairs, heads, rows), WIDE),
        ],
        **flash_params(),
    )(start, kind, packed, packed, packed, segments[:, None], segments[None, :])


def attend_backward(packed, segments, seq_lens, logsums, context_grad, lanes):
    rows = packed.shape[0]
    pairs = packed.shape[1] // (3 * lanes)
    heads = lanes // HEAD_DIM
    size = min(256, rows)
    start, kind, widths = key_windows(seq_lens, rows, size)
    return pl.pallas_call(
        functools.partial(backward_kernel, widths),
        grid_spec=pltpu.PrefetchScalarGridSpec(
            num_scalar_prefetch=2,
            grid=(pairs, rows // size),
            in_specs=attention_specs(rows, lanes, size)
            + [
                pl.BlockSpec((1, heads, size), lambda pair, block, *_: (pair, 0, block)),
                pl.BlockSpec((size, lanes), lambda pair, block, *_: (block, pair)),
            ],
            out_specs=[
                pl.BlockSpec((rows, 3 * lanes), lambda pair, block, *_: (0, pair)),
                pl.BlockSpec((1, 2, lanes), lambda pair, block, *_: (pair, 0, 0)),
            ],
            scratch_shapes=[pltpu.VMEM((rows, lanes), WIDE), pltpu.VMEM((rows, lanes), WIDE)],
        ),
        out_shape=[
            jax.ShapeDtypeStruct((rows, pairs * 3 * lanes), LOW),
            jax.ShapeDtypeStruct((pairs, 2, lanes), WIDE),
        ],
        **flash_params(),
    )(start, kind, packed, packed, packed, segments[:, None], segments[None, :], logsums, context_grad)


def pair_columns(packed, head_half, lanes, back=False):
    ranks = lanes // head_half
    if ranks == 1:
        return packed
    order = (3, ranks) if back else (ranks, 3)
    shaped = packed.reshape(packed.shape[0], -1, order[0], order[1], head_half)
    return jnp.swapaxes(shaped, 2, 3).reshape(packed.shape)


def layer_forward(rows, segments, seq_lens, weights, small, late_weights=None):
    w_qkv, w_out, w_in = weights[:3]
    gains, biases, offset, inner_bias, head_half = small
    lanes = max(head_half, 128)
    packed = (rhs_inner(rows, w_qkv) + offset).astype(LOW)
    packed = pair_columns(packed, head_half, lanes)
    context, logsums = attend_forward(packed, segments, seq_lens, lanes)
    first_sum = rows.astype(WIDE) + core_sum(matmul(context, w_out)) + biases[2]
    middle = (norm_parts(first_sum)[0] * gains[0] + biases[3]).astype(LOW)
    active, slope = gelu_pair(rhs_inner(middle, w_in) + inner_bias)
    active, slope = active.astype(LOW), slope.astype(LOW)
    if late_weights is None:
        w_back = weights[3]
    else:
        active, late = late_weights(active)
        w_back = late[0]
    second_sum = middle.astype(WIDE) + core_sum(matmul(active, w_back)) + biases[4]
    result = norm_parts(second_sum)[0] * gains[1] + biases[5]
    saved = (rows, packed, logsums, context, first_sum, middle, active, slope, second_sum)
    return result, saved, late if late_weights is not None else None


def slab_grads(hidden, features, chips):
    cut = features.shape[1] // chips
    return [lhs_inner(hidden, features[:, k * cut : (k + 1) * cut]).astype(LOW) for k in range(chips)]


def backward_hidden(saved, grad_rows, weights, small):
    _, _, w_in, w_back = weights
    gains = small[0]
    middle, active, slope, second_sum = saved[5:]
    second_grad, gain_two, bias_two = norm_backward(second_sum, gains[1], grad_rows.astype(WIDE))
    branch_grad = second_grad.astype(LOW)
    hidden_low = (rhs_inner(branch_grad, w_back) * slope.astype(WIDE)).astype(LOW)
    middle_grad = second_grad + core_sum(matmul(hidden_low, w_in))
    inner_sum = matmul(jnp.ones((8, hidden_low.shape[0]), LOW), hidden_low)[0]
    sums = (gain_two, jnp.sum(second_grad, axis=0), bias_two, inner_sum)
    return middle_grad, branch_grad, hidden_low, sums


def backward_attention(saved, segments, seq_lens, middle_grad, weights, small):
    _, w_out, _, _ = weights
    gains, head_half = small[0], small[4]
    _, packed, logsums, _, first_sum = saved[:5]
    first_grad, gain_one, bias_one = norm_backward(first_sum, gains[0], middle_grad)
    attended_grad = first_grad.astype(LOW)
    context_grad = rhs_inner(attended_grad, w_out).astype(LOW)
    lanes = max(head_half, 128)
    packed_low, column_sums = attend_backward(packed, segments, seq_lens, logsums, context_grad, lanes)
    packed_low = pair_columns(packed_low, head_half, lanes, back=True)
    sums = (gain_one, jnp.sum(first_grad, axis=0), bias_one) + tuple(
        column_sums[:, at].reshape(-1) for at in range(2)
    )
    return first_grad, attended_grad, packed_low, sums


def on_device(
    block_input, seq_lengths, w_qkv, w_out, w_in, w_back, gains, biases, ffn_bias, out_grad
):
    ranks = lax.axis_size("tensor")
    copies = lax.axis_size("dp")
    chips = copies // 2
    section = lax.axis_index("section")
    copy_at = lax.axis_index("dp")
    rank = lax.axis_index("tensor")
    core = copy_at % 2
    chip = copy_at // 2
    micro_count, own_rows, width = block_input.shape
    repeats = ranks // micro_count
    local = gains.shape[-1]
    counted = (rank % repeats) == 0

    def relative(value):
        slabs = jnp.split(value, chips, axis=-1)
        return jnp.concatenate([choose(chip ^ k, slabs) for k in range(chips)], axis=-1)

    def fetch_rows(block, *before):
        half = own_rows // 2
        kept = choose(core, (block[:, :half], block[:, half:]))
        given = choose(core, (block[:, half:], block[:, :half]))
        received = move(given, lambda s, d, t: (s, d ^ 1, t) if d % 2 == s else None)
        mine = jnp.where(core == section, kept, received)
        mine = jnp.repeat(mine, repeats, axis=0) if repeats > 1 else mine
        mine = after(mine, *before) if before else mine
        mine = lax.all_to_all(mine, "tensor", split_axis=0, concat_axis=0, tiled=True)
        whole = by_core(core, mine, to_other_core(mine), 1)
        return relative(whole.reshape(ranks * own_rows, width))

    def spread_both(first, second):
        chosen = relative(jnp.where(core == 0, first, second)).reshape(ranks, own_rows, width)
        spread = lax.all_to_all(chosen, "tensor", split_axis=0, concat_axis=0, tiled=True)
        return spread.reshape(micro_count, repeats, own_rows, width)[:, 0]

    def place_both(spread):
        return move(spread, lambda s, d, t: (d % 2, (d // 2) * 2 + s, t))

    def spread_rows(value):
        parts = relative(value).reshape(ranks, own_rows, width)
        half = own_rows // 2
        mine = choose(core, (parts[:, :half], parts[:, half:]))
        spread = lax.all_to_all(mine, "tensor", split_axis=0, concat_axis=0, tiled=True)
        return spread.reshape((micro_count, repeats) + spread.shape[1:])[:, 0]

    def place_rows(spread, layer):
        halves = [
            move(spread, lambda s, d, t: (layer, (d // 2) * 2 + s, t) if d % 2 == half else None)
            for half in range(2)
        ]
        return jnp.concatenate(halves, axis=1)

    def by_section(first, second):
        return jnp.where(section == 0, first, second)

    def own_half(halves):
        kept = choose(core, (halves[0], halves[1]))
        given = choose(core, (halves[1], halves[0]))
        return by_core(core, kept, to_other_core(given), 1)

    def relay(upward, downward):
        upward.append(move(upward[-1], lambda s, d, t: (s, d, t + 1) if t + 1 < ranks else None))
        downward.append(move(downward[-1], lambda s, d, t: (s, d, t - 1) if t > 0 else None))

    def assemble(upward, downward):
        own = upward[0]
        item = jnp.zeros((ranks,) + own.shape, LOW)
        item = lax.dynamic_update_index_in_dim(item, own, rank, 0)
        for j in range(1, ranks):
            arrived = jnp.where(rank >= j, upward[j], downward[ranks - j])
            item = lax.dynamic_update_index_in_dim(item, arrived, (rank + ranks - j) % ranks, 0)
        return item

    def over_ranks(own):
        upward, downward = [own], [own]
        for _ in range(1, ranks):
            relay(upward, downward)
        return assemble(upward, downward)

    def chips_once(item):
        across = move(item, lambda s, d, t: (1 - s, d, t))
        along = [move(item, lambda s, d, t: (s, d ^ (2 * k), t)) for k in range(1, chips)]
        return across, along

    def chips_twice(item, across, along):
        part = item.shape[0] // 2
        uppers = [move(across[:part], lambda s, d, t: (s, d ^ (2 * k), t)) for k in range(1, chips)]
        lowers = [move(along[k - 1][part:], lambda s, d, t: (1 - s, d, t)) for k in range(1, chips)]
        return uppers, lowers

    def both_layers(item, across, along, uppers, lowers):
        far = [jnp.concatenate(pair, axis=0) for pair in zip(uppers, lowers)]
        mine, other = [item] + along, [across] + far
        result = []
        for layer in range(2):
            slabs = [jnp.where(section == layer, m, o) for m, o in zip(mine, other)]
            result.append(jnp.concatenate(slabs, axis=-1))
        return result

    def over_chips(item):
        across, along = chips_once(item)
        return both_layers(item, across, along, *chips_twice(item, across, along))

    def from_x(slabs):
        return [move(slabs[k], lambda s, d, t: (s, d ^ (2 * k), t)) for k in range(1, chips)]

    def from_section(part, layer):
        return move(part, lambda s, d, t: (layer, d, t) if s != layer else None)

    def add(part, received):
        total = part.astype(WIDE)
        for other in received:
            total = total + other.astype(WIDE)
        return total.astype(LOW)

    def from_z(parts):
        return lax.all_to_all(parts, "tensor", split_axis=0, concat_axis=0, tiled=True)

    def add_ranks(parts):
        return jnp.sum(parts.astype(WIDE), axis=0).astype(LOW)

    def ranked(slab):
        return slab.reshape((ranks, -1) + slab.shape[1:])

    def counted_only(slabs):
        return [jnp.where(counted, slab, jnp.zeros((), LOW)) for slab in slabs] if repeats > 1 else slabs

    def finish(shard):
        parts = jnp.split(shard, 2, axis=1)
        kept = choose(core, parts)
        given = choose(core, parts[::-1])
        return by_core(core, kept[None], to_other_core(given)[None], 0).astype(WIDE)

    head_half = w_qkv.shape[-1] // 2
    hidden_half = w_in.shape[-1] // 2
    in_first = jnp.moveaxis(w_in[0].reshape(local, 2, hidden_half), 0, 2)
    qkv_first = jnp.transpose(w_qkv[0].reshape(local, 3, 2, head_half), (2, 1, 3, 0))
    qkv_first = qkv_first.reshape(2, 3 * head_half, local)
    out_first = w_out[0].reshape(2, head_half, local)
    back_first = w_back[0].reshape(2, hidden_half, local)
    later = hidden_half // 2
    gain_count, bias_count = gains.shape[1], biases.shape[1]
    table = jnp.concatenate([gains[0], biases[0], ffn_bias.reshape(-1, local)], axis=0)
    table_rows = table.shape[0]
    table = jnp.pad(table, ((0, -table_rows % 16), (0, 0)))
    table = jnp.broadcast_to(table, (2,) + table.shape)
    attention_own = own_half(jnp.concatenate([qkv_first, out_first, table], axis=1))
    back_own = own_half(back_first)
    in_own = own_half(in_first)
    back_two = jnp.stack(over_chips(back_own[later:]))
    attention_item = over_ranks(attention_own)
    attention_item, back_two = tie(attention_item, back_two)
    across, along = chips_once(attention_item)
    rows = fetch_rows(block_input, attention_item)
    in_own = after(in_own, attention_item)
    upward, downward = [in_own], [in_own]
    for at in range(1, ranks):
        relay(upward, downward)
        if at == 1:
            upward[-1], downward[-1], seq_lengths = tie(upward[-1], downward[-1], seq_lengths)
        if at == ranks // 2:
            upward[-1], downward[-1], across, *along = tie(upward[-1], downward[-1], across, *along)
            uppers, lowers = chips_twice(attention_item, across, along)
    upward[-1], downward[-1], *far = tie(upward[-1], downward[-1], *uppers, *lowers)
    attention_all = both_layers(attention_item, across, along, far[: chips - 1], far[chips - 1 :])
    in_item = assemble(upward, downward)
    in_across, in_along = chips_once(in_item)
    back_item = over_ranks(after(back_own[:later], in_item))
    back_item, back_two, in_across, *in_along = tie(back_item, back_two, in_across, *in_along)
    in_all = both_layers(in_item, in_across, in_along, *chips_twice(in_item, in_across, in_along))
    across, along = chips_once(back_item)
    upward, downward = [back_two], [back_two]
    for _ in range(1, ranks):
        relay(upward, downward)

    def late_weights(active):
        tied = tie(active, across, upward[-1], downward[-1], *along)
        here = (back_item, tied[1], list(tied[4:]))
        halves = zip(
            both_layers(*here, *chips_twice(*here)),
            jnp.moveaxis(assemble(upward[:-1] + [tied[2]], downward[:-1] + [tied[3]]), 1, 0),
        )
        return tied[0], [jnp.concatenate(pair, axis=1).reshape(-1, width) for pair in halves]

    weights = [
        (
            attention_all[layer][:, : 3 * head_half].reshape(-1, width),
            attention_all[layer][:, 3 * head_half : 4 * head_half].reshape(-1, width),
            in_all[layer].reshape(-1, width),
        )
        for layer in range(2)
    ]

    def head_columns(row):
        halves = row.reshape(ranks, 2, -1)
        return choose(core, (halves[:, 0], halves[:, 1])).reshape(-1)

    small = []
    for layer in range(2):
        table = attention_all[layer][0, 4 * head_half : 4 * head_half + table_rows].astype(WIDE)
        whole = relative(table)
        query_bias = head_columns(whole[gain_count])
        value_bias = head_columns(whole[gain_count + 1])
        query_bias, value_bias = query_bias.reshape(ranks, 1, -1), value_bias.reshape(ranks, 1, -1)
        offset = jnp.concatenate([query_bias, jnp.zeros_like(query_bias), value_bias], axis=1).reshape(-1)
        inner_bias = whole[gain_count + bias_count :].reshape(-1, copies, local)
        inner_bias = head_columns(jnp.swapaxes(inner_bias, 0, 1).reshape(-1))
        small.append((table[:gain_count], table[gain_count : gain_count + bias_count], offset, inner_bias, head_half))

    lengths = jnp.where(core == section, seq_lengths, to_other_core(seq_lengths))[:, 0]
    lengths = lax.dynamic_index_in_dim(lengths, rank // repeats, 0, keepdims=False)
    segments = segment_ids(lengths, ranks * own_rows)
    live = (segments < lengths.shape[0])[:, None]

    first_out, first_saved, late = layer_forward(rows, segments, lengths, weights[0], small[0], late_weights)
    weights = [weights[layer] + (late[layer],) for layer in range(2)]
    first_low = first_out.astype(LOW)
    cotangent = fetch_rows(out_grad, back_two)
    cotangent = jnp.where(live, cotangent, jnp.zeros((), LOW))
    second_out, second_saved, _ = layer_forward(first_low, segments, lengths, weights[1], small[1])
    spread = spread_both(first_low, second_out.astype(LOW))

    def hidden_grads(hidden, features):
        return [ranked(slab) for slab in counted_only(slab_grads(hidden, features, chips))]

    def attention_grads(saved, attended_grad, packed_low):
        qkv = hidden_grads(packed_low, saved[0])
        out = hidden_grads(saved[3], attended_grad)
        return [jnp.concatenate(pair, axis=1) for pair in zip(qkv, out)]

    middle_grad, branch_grad, hidden_low, second_sums = backward_hidden(
        second_saved, cotangent, weights[1], small[1]
    )
    back_slabs = hidden_grads(second_saved[6], branch_grad)
    back_here = from_x(back_slabs)
    in_slabs = hidden_grads(hidden_low, second_saved[5])
    in_here = from_x(in_slabs)
    first_grad, attended_grad, packed_low, more_sums = backward_attention(
        second_saved, segments, lengths, middle_grad, weights[1], small[1]
    )
    second_sums += more_sums
    packed_low, spread, *back_here = tie(packed_low, spread, *back_here)
    back_two = add(back_slabs[0], back_here)
    back_sent = from_section(back_two, 1)
    placed = place_both(spread)
    second_in = first_grad + core_sum(matmul(packed_low, weights[1][0]))
    qkv, out = [
        ranked(counted_only([lhs_inner(hidden, features).astype(LOW)])[0])
        for hidden, features in ((packed_low, second_saved[0]), (second_saved[3], attended_grad))
    ]
    attention_here = from_z(jnp.concatenate([qkv, out], axis=1))
    second_low = second_in.astype(LOW)

    middle_grad, branch_grad, hidden_low, first_sums = backward_hidden(
        first_saved, second_low, weights[0], small[0]
    )
    middle_grad, back_sent, placed, *in_here = tie(middle_grad, back_sent, placed, *in_here)
    back_two = add(back_two, [back_sent])
    in_two = add(in_slabs[0], in_here)
    in_sent = from_section(in_two, 1)
    outputs = placed.astype(WIDE)[None]
    second_in_spread = spread_rows(second_low)
    back_slabs = hidden_grads(first_saved[6], branch_grad)
    back_here = from_x(back_slabs)
    in_slabs = hidden_grads(hidden_low, first_saved[5])
    in_here = from_x(in_slabs)
    first_grad, attended_grad, packed_low, more_sums = backward_attention(
        first_saved, segments, lengths, middle_grad, weights[0], small[0]
    )
    first_sums += more_sums
    packed_low, in_sent, second_in_spread, *back_here = tie(packed_low, in_sent, second_in_spread, *back_here)
    in_two = add(in_two, [in_sent])
    back_one = add(back_slabs[0], back_here)
    back_sent = from_section(back_one, 0)
    second_placed = place_rows(second_in_spread, 1)
    first_in = first_grad + core_sum(matmul(packed_low, weights[0][0]))
    attention_slabs = attention_grads(first_saved, attended_grad, packed_low)
    attention_one_here = from_x(attention_slabs)
    first_in, attention_here, back_sent, *in_here = tie(first_in, attention_here, back_sent, *in_here)
    in_one = add(in_slabs[0], in_here)
    in_sent = from_section(in_one, 0)
    first_in_spread = spread_rows(first_in.astype(LOW))
    back_here = from_z(by_section(add(back_one, [back_sent]), back_two))
    attention_two_slabs = jnp.split(add_ranks(attention_here), chips, axis=-1)
    attention_two_here = from_x(attention_two_slabs)

    in_sent, back_here, first_in_spread, *attention_one_here = tie(
        in_sent, back_here, first_in_spread, *attention_one_here
    )
    attention_one = add(attention_slabs[0], attention_one_here)
    attention_one_sent = from_section(attention_one, 0)
    in_here = from_z(by_section(add(in_one, [in_sent]), in_two))
    attention_two = add(attention_two_slabs[0], attention_two_here)
    attention_two_sent = from_section(attention_two, 1)
    first_placed = place_rows(first_in_spread, 0)
    back_shard = finish(add_ranks(back_here))

    def spread_columns(row):
        blocks = row.reshape(ranks, 1, -1)
        both = jnp.where(jnp.arange(2)[None, :, None] == core, blocks, 0.0)
        return both.reshape(-1, width)

    tables = []
    for sums in (first_sums, second_sums):
        gain_two, bias_four, bias_five, inner_sum, gain_one, bias_two, bias_three, query_sum, value_sum = sums
        common = jnp.stack([gain_one, gain_two, bias_two, bias_three, bias_four, bias_five])
        common = jnp.where(core == 0, relative(common), 0.0)
        tables.append(
            jnp.concatenate(
                [common[:2], spread_columns(query_sum), spread_columns(value_sum), common[2:], spread_columns(inner_sum)]
            )
        )
    table = jnp.stack(tables)
    table = jnp.where(counted, table, 0.0) if repeats > 1 else table
    table = table + to_other_core(table)
    table = choose(section, (table[0], table[1])) + move(
        choose(section, (table[1], table[0])), lambda s, d, t: (1 - s, d, t)
    )
    attention_one_sent, attention_two_sent, in_here, table = tie(
        attention_one_sent, attention_two_sent, in_here, table
    )
    attention_here = from_z(add(attention_one, [attention_one_sent]))
    table = sum([move(table, lambda s, d, t: (s, d ^ (2 * k), t)) for k in range(1, chips)], table)
    table = sum([move(table, lambda s, d, t: (s, d, (t + j) % ranks)) for j in range(1, ranks)], table)
    attention_two = add(attention_two, [attention_two_sent])
    in_shard = finish(add_ranks(in_here))
    input_grads = by_section(first_placed, second_placed).astype(WIDE)[None]
    attention_shard = finish(by_section(add_ranks(attention_here), attention_two))
    qkv_shard, out_shard = attention_shard[:, : 3 * head_half], attention_shard[:, 3 * head_half :]
    qkv_grad = jnp.transpose(qkv_shard.reshape(2, 3, head_half, local), (3, 1, 0, 2)).reshape(local, 3, -1)
    out_grad_w = out_shard.reshape(-1, local)
    in_grad = jnp.transpose(in_shard.reshape(-1, local))
    back_grad = back_shard.reshape(-1, local)
    sliced = lax.dynamic_slice_in_dim(table[: gain_count + bias_count], copy_at * local, local, 1)
    inner = lax.dynamic_index_in_dim(
        table[gain_count + bias_count :].reshape(copies, -1), copy_at, 0, keepdims=False
    )
    return (
        outputs,
        input_grads,
        qkv_grad[None],
        out_grad_w[None],
        in_grad[None],
        back_grad[None],
        sliced[None, :gain_count],
        sliced[None, gain_count:],
        inner[None],
    )


def solution(mesh):
    return jax.shard_map(
        on_device,
        mesh=mesh,
        in_specs=(
            P(None, ("dp", "tensor"), None),
            P(None, "dp", None),
            P("section", "dp", None, "tensor"),
            P("section", "tensor", "dp"),
            P("section", "dp", "tensor"),
            P("section", "tensor", "dp"),
            P("section", None, "dp"),
            P("section", None, "dp"),
            P("section", "dp"),
            P(None, ("dp", "tensor"), None),
        ),
        out_specs=(
            P("section", None, ("dp", "tensor"), None),
            P("section", None, ("dp", "tensor"), None),
            P("section", "dp", None, "tensor"),
            P("section", "tensor", "dp"),
            P("section", "dp", "tensor"),
            P("section", "tensor", "dp"),
            P("section", None, "dp"),
            P("section", None, "dp"),
            P("section", "dp"),
        ),
        check_vma=False,
    )
```

```python
import functools

import jax
import jax.numpy as jnp
from jax import lax
from jax.experimental import pallas as pl
from jax.experimental.pallas import tpu as pltpu
from jax.sharding import PartitionSpec as P

HEAD_DIM = 64
AXES = ("section", "dp", "tensor")
LOW = jnp.bfloat16
WIDE = jnp.float32


def move(value, target):
    sections, copies, ranks = (lax.axis_size(axis) for axis in AXES)
    pairs = []
    for s in range(sections):
        for d in range(copies):
            for t in range(ranks):
                goal = target(s, d, t)
                if goal is not None:
                    pairs.append(
                        ((s * copies + d) * ranks + t, (goal[0] * copies + goal[1]) * ranks + goal[2])
                    )
    return lax.ppermute(value, AXES, pairs)


def to_other_core(value):
    return move(value, lambda s, d, t: (s, d ^ 1, t))


def by_core(core, kept, received, axis):
    return jnp.where(
        core == 0,
        jnp.concatenate([kept, received], axis=axis),
        jnp.concatenate([received, kept], axis=axis),
    )


def choose(place, options):
    chosen = options[0]
    for at, option in enumerate(options[1:], 1):
        chosen = jnp.where(place == at, option, chosen)
    return chosen


def after(value, *others):
    return lax.optimization_barrier((value,) + others)[0]


def tie(*values):
    return lax.optimization_barrier(values)


def matmul(lhs_mat, rhs_mat):
    return jnp.dot(lhs_mat, rhs_mat, preferred_element_type=WIDE)


def lhs_inner(lhs_mat, rhs_mat):
    return lax.dot_general(
        lhs_mat, rhs_mat, (((0,), (0,)), ((), ())), preferred_element_type=WIDE
    )


def rhs_inner(lhs_mat, rhs_mat):
    return lax.dot_general(
        lhs_mat, rhs_mat, (((1,), (1,)), ((), ())), preferred_element_type=WIDE
    )


def core_sum(partial):
    low = partial.astype(LOW)
    return low.astype(WIDE) + to_other_core(low).astype(WIDE)


def norm_parts(summed):
    centered = summed - jnp.mean(summed, axis=-1, keepdims=True)
    variance = jnp.mean(centered * centered, axis=-1, keepdims=True)
    scale = lax.rsqrt(variance + 1e-05)
    return centered * scale, scale


def norm_backward(summed, gain_row, grad):
    unit, scale = norm_parts(summed)
    gain_grad = jnp.sum(grad * unit, axis=0)
    bias_grad = jnp.sum(grad, axis=0)
    inner = grad * gain_row
    result = scale * (
        inner
        - jnp.mean(inner, axis=-1, keepdims=True)
        - unit * jnp.mean(inner * unit, axis=-1, keepdims=True)
    )
    return result, gain_grad, bias_grad


def gelu_pair(values):
    below = 0.5 * (1.0 + lax.erf(values * (0.5**0.5)))
    density = jnp.exp(-0.5 * values * values) * (0.3989422804014327)
    return values * below, below + values * density


def segment_ids(seq_lens, row_count):
    seq_ends = jnp.cumsum(seq_lens)
    positions = jnp.arange(row_count, dtype=jnp.int32)
    return jnp.sum((positions[:, None] >= seq_ends[None, :]).astype(jnp.int32), axis=1)


def flash_params():
    return dict(
        cost_estimate=pl.CostEstimate(flops=0, transcendentals=0, bytes_accessed=0),
        compiler_params=pltpu.CompilerParams(vmem_limit_bytes=48 * 1024 * 1024),
    )


def head_lanes(values, head):
    lane = lax.broadcasted_iota(jnp.int32, values.shape, 1)
    return jnp.where((lane // HEAD_DIM) == head, values, jnp.zeros_like(values))


def keys_by_queries(keys, queries):
    return lax.dot_general(keys, queries, (((1,), (1,)), ((), ())), preferred_element_type=WIDE)


def key_windows(seq_lens, rows, size):
    widths = tuple(sorted({min(rows, width) for width in (512, 640, 768, rows)}))
    ends = jnp.cumsum(seq_lens)
    first = jnp.arange(rows // size, dtype=jnp.int32)[:, None] * size
    lowest = jnp.max(jnp.where(ends[None, :] <= first, ends[None, :], 0), axis=1)
    highest = jnp.min(jnp.where(ends[None, :] >= first + size, ends[None, :], rows), axis=1)
    start, kind = jnp.zeros_like(lowest), jnp.full_like(lowest, len(widths) - 1)
    for at in range(len(widths) - 2, -1, -1):
        begin = jnp.minimum(lowest // 128 * 128, rows - widths[at])
        fits = highest - begin <= widths[at]
        start = jnp.where(fits, begin, start)
        kind = jnp.where(fits, at, kind)
    return start.astype(jnp.int32), kind.astype(jnp.int32), widths


def each_width(kind, widths, body):
    for at, width in enumerate(widths):
        @pl.when(kind == at)
        def _(width=width):
            body(width)


def forward_kernel(
    widths, start_ref, kind_ref, query_ref, key_ref, value_ref, seg_key_ref, seg_query_ref, out_ref, logsum_ref
):
    block = pl.program_id(1)
    heads = query_ref.shape[1] // HEAD_DIM

    def body(width):
        window = pl.ds(pl.multiple_of(start_ref[block], 128), width)
        allowed = seg_key_ref[window, :] == seg_query_ref[...]
        queries = query_ref[...] * jnp.asarray(HEAD_DIM ** (-0.5), LOW)
        keys, values = key_ref[window, :], value_ref[window, :]
        parts = []
        for head in range(heads):
            scores = keys_by_queries(keys, head_lanes(queries, head))
            scores = jnp.where(allowed, scores, -1000000000.0)
            highest = jnp.max(scores, axis=0, keepdims=True)
            raised = jnp.exp(scores - highest)
            totals = jnp.sum(raised, axis=0, keepdims=True)
            context = lhs_inner(values, raised.astype(LOW))
            rows = slice(head * HEAD_DIM, (head + 1) * HEAD_DIM)
            parts.append(context[rows] / totals)
            logsum_ref[0, head : head + 1, :] = highest + jnp.log(totals)
        out_ref[...] = jnp.concatenate(parts, axis=0).T.astype(LOW)

    each_width(kind_ref[block], widths, body)


def backward_kernel(
    widths, start_ref, kind_ref, query_ref, key_ref, value_ref, seg_key_ref, seg_query_ref, logsum_ref, grad_ref,
    out_ref, sum_ref, key_grad, value_grad,
):
    block = pl.program_id(1)
    size, lanes = query_ref.shape
    heads = lanes // HEAD_DIM
    factor = HEAD_DIM ** (-0.5)

    @pl.when(block == 0)
    def _():
        key_grad[...] = jnp.zeros_like(key_grad)
        value_grad[...] = jnp.zeros_like(value_grad)
        sum_ref[...] = jnp.zeros_like(sum_ref)

    def body(width):
        window = pl.ds(pl.multiple_of(start_ref[block], 128), width)
        allowed = seg_key_ref[window, :] == seg_query_ref[...]
        queries = query_ref[...] * jnp.asarray(factor, LOW)
        grads = grad_ref[...]
        keys, values = key_ref[window, :], value_ref[window, :]
        weight_low, score_low, query_heads, grad_heads, query_parts = [], [], [], [], []
        for head in range(heads):
            query_head, grad_head = head_lanes(queries, head), head_lanes(grads, head)
            scores = jnp.where(allowed, keys_by_queries(keys, query_head), -1000000000.0)
            weights = jnp.exp(scores - logsum_ref[0, head : head + 1, :])
            weight_grad = keys_by_queries(values, grad_head)
            centre = jnp.sum(weight_grad * weights, axis=0, keepdims=True)
            score_grad = (weights * (weight_grad - centre)).astype(LOW)
            rows = slice(head * HEAD_DIM, (head + 1) * HEAD_DIM)
            query_parts.append(lhs_inner(keys, score_grad)[rows] * factor)
            weight_low.append(weights.astype(LOW))
            score_low.append(score_grad)
            query_heads.append(query_head)
            grad_heads.append(grad_head)
        key_grad[window, :] += matmul(
            jnp.concatenate(score_low, axis=1), jnp.concatenate(query_heads, axis=0)
        )
        value_grad[window, :] += matmul(
            jnp.concatenate(weight_low, axis=1), jnp.concatenate(grad_heads, axis=0)
        )
        query_grad = jnp.concatenate(query_parts, axis=0).T
        out_ref[pl.ds(pl.multiple_of(block * size, size), size), :lanes] = query_grad.astype(LOW)
        sum_ref[0, 0:1, :] += jnp.sum(query_grad, axis=0, keepdims=True)

    each_width(kind_ref[block], widths, body)

    @pl.when(block == pl.num_programs(1) - 1)
    def _():
        out_ref[:, lanes : 2 * lanes] = key_grad[...].astype(LOW)
        out_ref[:, 2 * lanes :] = value_grad[...].astype(LOW)
        sum_ref[0, 1:2, :] = jnp.sum(value_grad[...], axis=0, keepdims=True)


def attention_specs(rows, lanes, size):
    return [
        pl.BlockSpec((size, lanes), lambda pair, block, *_: (block, 3 * pair)),
        pl.BlockSpec((rows, lanes), lambda pair, block, *_: (0, 3 * pair + 1)),
        pl.BlockSpec((rows, lanes), lambda pair, block, *_: (0, 3 * pair + 2)),
        pl.BlockSpec((rows, 1), lambda pair, block, *_: (0, 0)),
        pl.BlockSpec((1, size), lambda pair, block, *_: (0, block)),
    ]


def attend_forward(packed, segments, seq_lens, lanes):
    rows = packed.shape[0]
    pairs = packed.shape[1] // (3 * lanes)
    heads = lanes // HEAD_DIM
    size = min(256, rows)
    start, kind, widths = key_windows(seq_lens, rows, size)
    return pl.pallas_call(
        functools.partial(forward_kernel, widths),
        grid_spec=pltpu.PrefetchScalarGridSpec(
            num_scalar_prefetch=2,
            grid=(pairs, rows // size),
            in_specs=attention_specs(rows, lanes, size),
            out_specs=[
                pl.BlockSpec((size, lanes), lambda pair, block, *_: (block, pair)),
                pl.BlockSpec((1, heads, size), lambda pair, block, *_: (pair, 0, block)),
            ],
        ),
        out_shape=[
            jax.ShapeDtypeStruct((rows, pairs * lanes), LOW),
            jax.ShapeDtypeStruct((pairs, heads, rows), WIDE),
        ],
        **flash_params(),
    )(start, kind, packed, packed, packed, segments[:, None], segments[None, :])


def attend_backward(packed, segments, seq_lens, logsums, context_grad, lanes):
    rows = packed.shape[0]
    pairs = packed.shape[1] // (3 * lanes)
    heads = lanes // HEAD_DIM
    size = min(256, rows)
    start, kind, widths = key_windows(seq_lens, rows, size)
    return pl.pallas_call(
        functools.partial(backward_kernel, widths),
        grid_spec=pltpu.PrefetchScalarGridSpec(
            num_scalar_prefetch=2,
            grid=(pairs, rows // size),
            in_specs=attention_specs(rows, lanes, size)
            + [
                pl.BlockSpec((1, heads, size), lambda pair, block, *_: (pair, 0, block)),
                pl.BlockSpec((size, lanes), lambda pair, block, *_: (block, pair)),
            ],
            out_specs=[
                pl.BlockSpec((rows, 3 * lanes), lambda pair, block, *_: (0, pair)),
                pl.BlockSpec((1, 2, lanes), lambda pair, block, *_: (pair, 0, 0)),
            ],
            scratch_shapes=[pltpu.VMEM((rows, lanes), WIDE), pltpu.VMEM((rows, lanes), WIDE)],
        ),
        out_shape=[
            jax.ShapeDtypeStruct((rows, pairs * 3 * lanes), LOW),
            jax.ShapeDtypeStruct((pairs, 2, lanes), WIDE),
        ],
        **flash_params(),
    )(start, kind, packed, packed, packed, segments[:, None], segments[None, :], logsums, context_grad)


def pair_columns(packed, head_half, lanes, back=False):
    ranks = lanes // head_half
    if ranks == 1:
        return packed
    order = (3, ranks) if back else (ranks, 3)
    shaped = packed.reshape(packed.shape[0], -1, order[0], order[1], head_half)
    return jnp.swapaxes(shaped, 2, 3).reshape(packed.shape)


def layer_forward(rows, segments, seq_lens, weights, small, late_weights=None):
    w_qkv, w_out, w_in = weights[:3]
    gains, biases, offset, inner_bias, head_half = small
    lanes = max(head_half, 128)
    packed = (rhs_inner(rows, w_qkv) + offset).astype(LOW)
    packed = pair_columns(packed, head_half, lanes)
    context, logsums = attend_forward(packed, segments, seq_lens, lanes)
    first_sum = rows.astype(WIDE) + core_sum(matmul(context, w_out)) + biases[2]
    middle = (norm_parts(first_sum)[0] * gains[0] + biases[3]).astype(LOW)
    active, slope = gelu_pair(rhs_inner(middle, w_in) + inner_bias)
    active, slope = active.astype(LOW), slope.astype(LOW)
    if late_weights is None:
        w_back = weights[3]
    else:
        active, late = late_weights(active)
        w_back = late[0]
    second_sum = middle.astype(WIDE) + core_sum(matmul(active, w_back)) + biases[4]
    result = norm_parts(second_sum)[0] * gains[1] + biases[5]
    saved = (rows, packed, logsums, context, first_sum, middle, active, slope, second_sum)
    return result, saved, late if late_weights is not None else None


def slab_grads(hidden, features, chips):
    cut = features.shape[1] // chips
    return [lhs_inner(hidden, features[:, k * cut : (k + 1) * cut]).astype(LOW) for k in range(chips)]


def backward_hidden(saved, grad_rows, weights, small):
    _, _, w_in, w_back = weights
    gains = small[0]
    middle, active, slope, second_sum = saved[5:]
    second_grad, gain_two, bias_two = norm_backward(second_sum, gains[1], grad_rows.astype(WIDE))
    branch_grad = second_grad.astype(LOW)
    hidden_low = (rhs_inner(branch_grad, w_back) * slope.astype(WIDE)).astype(LOW)
    middle_grad = second_grad + core_sum(matmul(hidden_low, w_in))
    inner_sum = matmul(jnp.ones((8, hidden_low.shape[0]), LOW), hidden_low)[0]
    sums = (gain_two, jnp.sum(second_grad, axis=0), bias_two, inner_sum)
    return middle_grad, branch_grad, hidden_low, sums


def backward_attention(saved, segments, seq_lens, middle_grad, weights, small):
    _, w_out, _, _ = weights
    gains, head_half = small[0], small[4]
    _, packed, logsums, _, first_sum = saved[:5]
    first_grad, gain_one, bias_one = norm_backward(first_sum, gains[0], middle_grad)
    attended_grad = first_grad.astype(LOW)
    context_grad = rhs_inner(attended_grad, w_out).astype(LOW)
    lanes = max(head_half, 128)
    packed_low, column_sums = attend_backward(packed, segments, seq_lens, logsums, context_grad, lanes)
    packed_low = pair_columns(packed_low, head_half, lanes, back=True)
    sums = (gain_one, jnp.sum(first_grad, axis=0), bias_one) + tuple(
        column_sums[:, at].reshape(-1) for at in range(2)
    )
    return first_grad, attended_grad, packed_low, sums


def on_device(
    block_input, seq_lengths, w_qkv, w_out, w_in, w_back, gains, biases, ffn_bias, out_grad
):
    ranks = lax.axis_size("tensor")
    copies = lax.axis_size("dp")
    chips = copies // 2
    section = lax.axis_index("section")
    copy_at = lax.axis_index("dp")
    rank = lax.axis_index("tensor")
    core = copy_at % 2
    chip = copy_at // 2
    micro_count, own_rows, width = block_input.shape
    repeats = ranks // micro_count
    local = gains.shape[-1]
    counted = (rank % repeats) == 0

    def relative(value):
        slabs = jnp.split(value, chips, axis=-1)
        return jnp.concatenate([choose(chip ^ k, slabs) for k in range(chips)], axis=-1)

    def fetch_rows(block, *before):
        half = own_rows // 2
        kept = choose(core, (block[:, :half], block[:, half:]))
        given = choose(core, (block[:, half:], block[:, :half]))
        received = move(given, lambda s, d, t: (s, d ^ 1, t) if d % 2 == s else None)
        mine = jnp.where(core == section, kept, received)
        mine = jnp.repeat(mine, repeats, axis=0) if repeats > 1 else mine
        mine = after(mine, *before) if before else mine
        mine = lax.all_to_all(mine, "tensor", split_axis=0, concat_axis=0, tiled=True)
        whole = by_core(core, mine, to_other_core(mine), 1)
        return relative(whole.reshape(ranks * own_rows, width))

    def spread_both(first, second):
        chosen = relative(jnp.where(core == 0, first, second)).reshape(ranks, own_rows, width)
        spread = lax.all_to_all(chosen, "tensor", split_axis=0, concat_axis=0, tiled=True)
        return spread.reshape(micro_count, repeats, own_rows, width)[:, 0]

    def place_both(spread):
        moved = move(spread, lambda s, d, t: (d % 2, (d // 2) * 2 + s, t) if d % 2 != s else None)
        return jnp.where(core == section, spread, moved)

    def spread_rows(value):
        parts = relative(value).reshape(ranks, own_rows, width)
        half = own_rows // 2
        mine = choose(core, (parts[:, :half], parts[:, half:]))
        spread = lax.all_to_all(mine, "tensor", split_axis=0, concat_axis=0, tiled=True)
        return spread.reshape((micro_count, repeats) + spread.shape[1:])[:, 0]

    def place_rows(spread, layer):
        halves = []
        for half in range(2):
            own = lambda s, d: half == layer and s == layer and d % 2 == layer
            moved = move(
                spread,
                lambda s, d, t: (layer, (d // 2) * 2 + s, t) if d % 2 == half and not own(s, d) else None,
            )
            if half == layer:
                moved = jnp.where((section == layer) & (core == layer), spread, moved)
            halves.append(moved)
        return jnp.concatenate(halves, axis=1)

    def by_section(first, second):
        return jnp.where(section == 0, first, second)

    def own_half(halves):
        kept = choose(core, (halves[0], halves[1]))
        given = choose(core, (halves[1], halves[0]))
        return by_core(core, kept, to_other_core(given), 1)

    def relay(upward, downward):
        upward.append(move(upward[-1], lambda s, d, t: (s, d, t + 1) if t + 1 < ranks else None))
        downward.append(move(downward[-1], lambda s, d, t: (s, d, t - 1) if t > 0 else None))

    def assemble(upward, downward):
        own = upward[0]
        item = jnp.zeros((ranks,) + own.shape, LOW)
        item = lax.dynamic_update_index_in_dim(item, own, rank, 0)
        for j in range(1, ranks):
            arrived = jnp.where(rank >= j, upward[j], downward[ranks - j])
            item = lax.dynamic_update_index_in_dim(item, arrived, (rank + ranks - j) % ranks, 0)
        return item

    def over_ranks(own):
        upward, downward = [own], [own]
        for _ in range(1, ranks):
            relay(upward, downward)
        return assemble(upward, downward)

    def chips_once(item):
        across = move(item, lambda s, d, t: (1 - s, d, t))
        along = [move(item, lambda s, d, t: (s, d ^ (2 * k), t)) for k in range(1, chips)]
        return across, along

    def chips_twice(item, across, along):
        part = item.shape[0] // 2
        uppers = [move(across[:part], lambda s, d, t: (s, d ^ (2 * k), t)) for k in range(1, chips)]
        lowers = [move(along[k - 1][part:], lambda s, d, t: (1 - s, d, t)) for k in range(1, chips)]
        return uppers, lowers

    def both_layers(item, across, along, uppers, lowers):
        far = [jnp.concatenate(pair, axis=0) for pair in zip(uppers, lowers)]
        mine, other = [item] + along, [across] + far
        result = []
        for layer in range(2):
            slabs = [jnp.where(section == layer, m, o) for m, o in zip(mine, other)]
            result.append(jnp.concatenate(slabs, axis=-1))
        return result

    def over_chips(item):
        across, along = chips_once(item)
        return both_layers(item, across, along, *chips_twice(item, across, along))

    def from_x(slabs):
        return [move(slabs[k], lambda s, d, t: (s, d ^ (2 * k), t)) for k in range(1, chips)]

    def from_section(part, layer):
        return move(part, lambda s, d, t: (layer, d, t) if s != layer else None)

    def add(part, received):
        total = part.astype(WIDE)
        for other in received:
            total = total + other.astype(WIDE)
        return total.astype(LOW)

    def from_z(parts):
        return lax.all_to_all(parts, "tensor", split_axis=0, concat_axis=0, tiled=True)

    def add_ranks(parts):
        return jnp.sum(parts.astype(WIDE), axis=0).astype(LOW)

    def hops_z(parts):
        own = lax.dynamic_index_in_dim(parts, rank, 0, keepdims=False)
        received = [
            move(
                lax.dynamic_index_in_dim(parts, (rank + j) % ranks, 0, keepdims=False),
                lambda s, d, t: (s, d, (t + j) % ranks),
            )
            for j in range(1, ranks)
        ]
        return own, received

    def ranked(slab):
        return slab.reshape((ranks, -1) + slab.shape[1:])

    def counted_only(slabs):
        return [jnp.where(counted, slab, jnp.zeros((), LOW)) for slab in slabs] if repeats > 1 else slabs

    def finish(shard):
        parts = jnp.split(shard, 2, axis=1)
        kept = choose(core, parts)
        given = choose(core, parts[::-1])
        return by_core(core, kept[None], to_other_core(given)[None], 0).astype(WIDE)

    head_half = w_qkv.shape[-1] // 2
    hidden_half = w_in.shape[-1] // 2
    in_first = jnp.moveaxis(w_in[0].reshape(local, 2, hidden_half), 0, 2)
    qkv_first = jnp.transpose(w_qkv[0].reshape(local, 3, 2, head_half), (2, 1, 3, 0))
    qkv_first = qkv_first.reshape(2, 3 * head_half, local)
    out_first = w_out[0].reshape(2, head_half, local)
    back_first = w_back[0].reshape(2, hidden_half, local)
    later = hidden_half // 2
    gain_count, bias_count = gains.shape[1], biases.shape[1]
    table = jnp.concatenate([gains[0], biases[0], ffn_bias.reshape(-1, local)], axis=0)
    table_rows = table.shape[0]
    table = jnp.pad(table, ((0, -table_rows % 16), (0, 0)))
    table = jnp.broadcast_to(table, (2,) + table.shape)
    attention_own = own_half(jnp.concatenate([qkv_first, out_first, table], axis=1))
    back_own = own_half(back_first)
    in_own = own_half(in_first)
    back_two = jnp.stack(over_chips(back_own[later:]))
    attention_item = over_ranks(attention_own)
    attention_item, back_two = tie(attention_item, back_two)
    across, along = chips_once(attention_item)
    rows = fetch_rows(block_input, attention_item)
    in_own = after(in_own, attention_item)
    upward, downward = [in_own], [in_own]
    for at in range(1, ranks):
        relay(upward, downward)
        if at == 1:
            upward[-1], downward[-1], seq_lengths = tie(upward[-1], downward[-1], seq_lengths)
        if at == ranks // 2:
            upward[-1], downward[-1], across, *along = tie(upward[-1], downward[-1], across, *along)
            uppers, lowers = chips_twice(attention_item, across, along)
    upward[-1], downward[-1], *far = tie(upward[-1], downward[-1], *uppers, *lowers)
    attention_all = both_layers(attention_item, across, along, far[: chips - 1], far[chips - 1 :])
    in_item = assemble(upward, downward)
    in_across, in_along = chips_once(in_item)
    back_one = after(back_own[:later], in_item)
    back_up, back_down = [back_one], [back_one]
    for at in range(1, ranks):
        relay(back_up, back_down)
        if at == 1:
            rows, back_up[-1], back_down[-1] = tie(rows, back_up[-1], back_down[-1])
    back_item = assemble(back_up, back_down)
    back_item, back_two, in_across, *in_along = tie(back_item, back_two, in_across, *in_along)
    in_all = both_layers(in_item, in_across, in_along, *chips_twice(in_item, in_across, in_along))
    across, along = chips_once(back_item)
    upward, downward = [back_two], [back_two]
    for _ in range(1, ranks):
        relay(upward, downward)

    def late_weights(active):
        tied = tie(active, across, upward[-1], downward[-1], *along)
        here = (back_item, tied[1], list(tied[4:]))
        halves = zip(
            both_layers(*here, *chips_twice(*here)),
            jnp.moveaxis(assemble(upward[:-1] + [tied[2]], downward[:-1] + [tied[3]]), 1, 0),
        )
        return tied[0], [jnp.concatenate(pair, axis=1).reshape(-1, width) for pair in halves]

    weights = [
        (
            attention_all[layer][:, : 3 * head_half].reshape(-1, width),
            attention_all[layer][:, 3 * head_half : 4 * head_half].reshape(-1, width),
            in_all[layer].reshape(-1, width),
        )
        for layer in range(2)
    ]

    def head_columns(row):
        halves = row.reshape(ranks, 2, -1)
        return choose(core, (halves[:, 0], halves[:, 1])).reshape(-1)

    small = []
    for layer in range(2):
        table = attention_all[layer][0, 4 * head_half : 4 * head_half + table_rows].astype(WIDE)
        whole = relative(table)
        query_bias = head_columns(whole[gain_count])
        value_bias = head_columns(whole[gain_count + 1])
        query_bias, value_bias = query_bias.reshape(ranks, 1, -1), value_bias.reshape(ranks, 1, -1)
        offset = jnp.concatenate([query_bias, jnp.zeros_like(query_bias), value_bias], axis=1).reshape(-1)
        inner_bias = whole[gain_count + bias_count :].reshape(-1, copies, local)
        inner_bias = head_columns(jnp.swapaxes(inner_bias, 0, 1).reshape(-1))
        small.append((table[:gain_count], table[gain_count : gain_count + bias_count], offset, inner_bias, head_half))

    lengths = jnp.where(core == section, seq_lengths, to_other_core(seq_lengths))[:, 0]
    lengths = lax.dynamic_index_in_dim(lengths, rank // repeats, 0, keepdims=False)
    segments = segment_ids(lengths, ranks * own_rows)
    live = (segments < lengths.shape[0])[:, None]

    first_out, first_saved, late = layer_forward(rows, segments, lengths, weights[0], small[0], late_weights)
    weights = [weights[layer] + (late[layer],) for layer in range(2)]
    first_low = first_out.astype(LOW)
    cotangent = fetch_rows(out_grad, back_two)
    cotangent = jnp.where(live, cotangent, jnp.zeros((), LOW))
    second_out, second_saved, _ = layer_forward(first_low, segments, lengths, weights[1], small[1])
    spread = spread_both(first_low, second_out.astype(LOW))

    def hidden_grads(hidden, features):
        return [ranked(slab) for slab in counted_only(slab_grads(hidden, features, chips))]

    def attention_grads(saved, attended_grad, packed_low):
        qkv = hidden_grads(packed_low, saved[0])
        out = hidden_grads(saved[3], attended_grad)
        return [jnp.concatenate(pair, axis=1) for pair in zip(qkv, out)]

    middle_grad, branch_grad, hidden_low, second_sums = backward_hidden(
        second_saved, cotangent, weights[1], small[1]
    )
    back_slabs = hidden_grads(second_saved[6], branch_grad)
    back_here = from_x(back_slabs)
    in_slabs = hidden_grads(hidden_low, second_saved[5])
    in_here = from_x(in_slabs)
    first_grad, attended_grad, packed_low, more_sums = backward_attention(
        second_saved, segments, lengths, middle_grad, weights[1], small[1]
    )
    second_sums += more_sums
    packed_low, spread, *back_here = tie(packed_low, spread, *back_here)
    back_two = add(back_slabs[0], back_here)
    back_sent = from_section(back_two, 1)
    placed = place_both(spread)
    second_in = first_grad + core_sum(matmul(packed_low, weights[1][0]))
    qkv, out = [
        ranked(counted_only([lhs_inner(hidden, features).astype(LOW)])[0])
        for hidden, features in ((packed_low, second_saved[0]), (second_saved[3], attended_grad))
    ]
    attention_here = from_z(jnp.concatenate([qkv, out], axis=1))
    second_low = second_in.astype(LOW)

    middle_grad, branch_grad, hidden_low, first_sums = backward_hidden(
        first_saved, second_low, weights[0], small[0]
    )
    middle_grad, back_sent, placed, *in_here = tie(middle_grad, back_sent, placed, *in_here)
    back_two = add(back_two, [back_sent])
    in_two = add(in_slabs[0], in_here)
    in_sent = from_section(in_two, 1)
    outputs = placed.astype(WIDE)[None]
    second_in_spread = spread_rows(second_low)
    back_slabs = hidden_grads(first_saved[6], branch_grad)
    back_here = from_x(back_slabs)
    in_slabs = hidden_grads(hidden_low, first_saved[5])
    in_here = from_x(in_slabs)
    first_grad, attended_grad, packed_low, more_sums = backward_attention(
        first_saved, segments, lengths, middle_grad, weights[0], small[0]
    )
    first_sums += more_sums
    packed_low, in_sent, second_in_spread, *back_here = tie(packed_low, in_sent, second_in_spread, *back_here)
    in_two = add(in_two, [in_sent])
    back_one = add(back_slabs[0], back_here)
    back_sent = from_section(back_one, 0)
    second_placed = place_rows(second_in_spread, 1)
    first_in = first_grad + core_sum(matmul(packed_low, weights[0][0]))
    attention_slabs = attention_grads(first_saved, attended_grad, packed_low)
    attention_one_here = from_x(attention_slabs)
    first_in, attention_here, back_sent, *held = tie(
        first_in, attention_here, back_sent, *in_here, *attention_slabs
    )
    in_one = add(in_slabs[0], held[: chips - 1])
    attention_slabs = held[chips - 1 :]
    in_sent = from_section(in_one, 0)
    back_own, back_here = hops_z(by_section(add(back_one, [back_sent]), back_two))
    first_in_spread = spread_rows(first_in.astype(LOW))
    attention_two_slabs = jnp.split(add_ranks(attention_here), chips, axis=-1)
    attention_two_here = from_x(attention_two_slabs)

    def spread_columns(row):
        blocks = row.reshape(ranks, 1, -1)
        both = jnp.where(jnp.arange(2)[None, :, None] == core, blocks, 0.0)
        return both.reshape(-1, width)

    tables = []
    for sums in (first_sums, second_sums):
        gain_two, bias_four, bias_five, inner_sum, gain_one, bias_two, bias_three, query_sum, value_sum = sums
        common = jnp.stack([gain_one, gain_two, bias_two, bias_three, bias_four, bias_five])
        common = jnp.where(core == 0, relative(common), 0.0)
        tables.append(
            jnp.concatenate(
                [common[:2], spread_columns(query_sum), spread_columns(value_sum), common[2:], spread_columns(inner_sum)]
            )
        )
    table = jnp.stack(tables)
    table = jnp.where(counted, table, 0.0) if repeats > 1 else table
    table = table + to_other_core(table)
    table = choose(section, (table[0], table[1])) + move(
        choose(section, (table[1], table[0])), lambda s, d, t: (1 - s, d, t)
    )
    beside = [move(table, lambda s, d, t: (s, d ^ (2 * k), t)) for k in range(1, chips)]
    in_sent, table, *held = tie(in_sent, table, *beside, *attention_one_here, *attention_two_here)
    table, held = sum(held[: chips - 1], table), held[chips - 1 :]
    attention_one = add(attention_slabs[0], held[: chips - 1])
    attention_one_sent = from_section(attention_one, 0)
    attention_two = add(attention_two_slabs[0], held[chips - 1 :])
    attention_two_sent = from_section(attention_two, 1)
    in_own, in_here = hops_z(by_section(add(in_one, [in_sent]), in_two))

    beside = [move(table, lambda s, d, t: (s, d, (t + j) % ranks)) for j in range(1, ranks)]
    attention_one_sent, attention_two_sent, first_in_spread, table, *held = tie(
        attention_one_sent, attention_two_sent, first_in_spread, table, *beside, *back_here
    )
    table, back_here = sum(held[: ranks - 1], table), held[ranks - 1 :]
    attention_own, attention_here = hops_z(add(attention_one, [attention_one_sent]))
    first_placed = place_rows(first_in_spread, 0)
    back_shard = finish(add(back_own, back_here))
    table, *in_here = tie(table, *in_here)
    attention_two = add(attention_two, [attention_two_sent])
    in_shard = finish(add(in_own, in_here))
    input_grads = by_section(first_placed, second_placed).astype(WIDE)[None]
    attention_shard = finish(by_section(add(attention_own, attention_here), attention_two))
    qkv_shard, out_shard = attention_shard[:, : 3 * head_half], attention_shard[:, 3 * head_half :]
    qkv_grad = jnp.transpose(qkv_shard.reshape(2, 3, head_half, local), (3, 1, 0, 2)).reshape(local, 3, -1)
    out_grad_w = out_shard.reshape(-1, local)
    in_grad = jnp.transpose(in_shard.reshape(-1, local))
    back_grad = back_shard.reshape(-1, local)
    sliced = lax.dynamic_slice_in_dim(table[: gain_count + bias_count], copy_at * local, local, 1)
    inner = lax.dynamic_index_in_dim(
        table[gain_count + bias_count :].reshape(copies, -1), copy_at, 0, keepdims=False
    )
    return (
        outputs,
        input_grads,
        qkv_grad[None],
        out_grad_w[None],
        in_grad[None],
        back_grad[None],
        sliced[None, :gain_count],
        sliced[None, gain_count:],
        inner[None],
    )


def solution(mesh):
    return jax.shard_map(
        on_device,
        mesh=mesh,
        in_specs=(
            P(None, ("dp", "tensor"), None),
            P(None, "dp", None),
            P("section", "dp", None, "tensor"),
            P("section", "tensor", "dp"),
            P("section", "dp", "tensor"),
            P("section", "tensor", "dp"),
            P("section", None, "dp"),
            P("section", None, "dp"),
            P("section", "dp"),
            P(None, ("dp", "tensor"), None),
        ),
        out_specs=(
            P("section", None, ("dp", "tensor"), None),
            P("section", None, ("dp", "tensor"), None),
            P("section", "dp", None, "tensor"),
            P("section", "tensor", "dp"),
            P("section", "dp", "tensor"),
            P("section", "tensor", "dp"),
            P("section", None, "dp"),
            P("section", None, "dp"),
            P("section", "dp"),
        ),
        check_vma=False,
    )
```

```python
import functools

import jax
import jax.numpy as jnp
from jax import lax
from jax.experimental import pallas as pl
from jax.experimental.pallas import tpu as pltpu
from jax.sharding import PartitionSpec as P

HEAD_DIM = 64
AXES = ("section", "dp", "tensor")
LOW = jnp.bfloat16
WIDE = jnp.float32


def move(value, target):
    sections, copies, ranks = (lax.axis_size(axis) for axis in AXES)
    pairs = []
    for s in range(sections):
        for d in range(copies):
            for t in range(ranks):
                goal = target(s, d, t)
                if goal is not None:
                    pairs.append(
                        ((s * copies + d) * ranks + t, (goal[0] * copies + goal[1]) * ranks + goal[2])
                    )
    return lax.ppermute(value, AXES, pairs)


def to_other_core(value):
    return move(value, lambda s, d, t: (s, d ^ 1, t))


def by_core(core, kept, received, axis):
    return jnp.where(
        core == 0,
        jnp.concatenate([kept, received], axis=axis),
        jnp.concatenate([received, kept], axis=axis),
    )


def choose(place, options):
    chosen = options[0]
    for at, option in enumerate(options[1:], 1):
        chosen = jnp.where(place == at, option, chosen)
    return chosen


def after(value, *others):
    return lax.optimization_barrier((value,) + others)[0]


def tie(*values):
    return lax.optimization_barrier(values)


def matmul(lhs_mat, rhs_mat):
    return jnp.dot(lhs_mat, rhs_mat, preferred_element_type=WIDE)


def lhs_inner(lhs_mat, rhs_mat):
    return lax.dot_general(
        lhs_mat, rhs_mat, (((0,), (0,)), ((), ())), preferred_element_type=WIDE
    )


def rhs_inner(lhs_mat, rhs_mat):
    return lax.dot_general(
        lhs_mat, rhs_mat, (((1,), (1,)), ((), ())), preferred_element_type=WIDE
    )


def core_sum(partial):
    low = partial.astype(LOW)
    return low.astype(WIDE) + to_other_core(low).astype(WIDE)


def norm_parts(summed):
    centered = summed - jnp.mean(summed, axis=-1, keepdims=True)
    variance = jnp.mean(centered * centered, axis=-1, keepdims=True)
    scale = lax.rsqrt(variance + 1e-05)
    return centered * scale, scale


def norm_backward(summed, gain_row, grad):
    unit, scale = norm_parts(summed)
    gain_grad = jnp.sum(grad * unit, axis=0)
    bias_grad = jnp.sum(grad, axis=0)
    inner = grad * gain_row
    result = scale * (
        inner
        - jnp.mean(inner, axis=-1, keepdims=True)
        - unit * jnp.mean(inner * unit, axis=-1, keepdims=True)
    )
    return result, gain_grad, bias_grad


def gelu_pair(values):
    below = 0.5 * (1.0 + lax.erf(values * (0.5**0.5)))
    density = jnp.exp(-0.5 * values * values) * (0.3989422804014327)
    return values * below, below + values * density


def segment_ids(seq_lens, row_count):
    seq_ends = jnp.cumsum(seq_lens)
    positions = jnp.arange(row_count, dtype=jnp.int32)
    return jnp.sum((positions[:, None] >= seq_ends[None, :]).astype(jnp.int32), axis=1)


def flash_params():
    return dict(
        cost_estimate=pl.CostEstimate(flops=0, transcendentals=0, bytes_accessed=0),
        compiler_params=pltpu.CompilerParams(vmem_limit_bytes=48 * 1024 * 1024),
    )


def head_lanes(values, head):
    lane = lax.broadcasted_iota(jnp.int32, values.shape, 1)
    return jnp.where((lane // HEAD_DIM) == head, values, jnp.zeros_like(values))


def keys_by_queries(keys, queries):
    return lax.dot_general(keys, queries, (((1,), (1,)), ((), ())), preferred_element_type=WIDE)


def key_windows(seq_lens, rows, size):
    widths = tuple(sorted({min(rows, width) for width in (512, 640, 768, rows)}))
    ends = jnp.cumsum(seq_lens)
    first = jnp.arange(rows // size, dtype=jnp.int32)[:, None] * size
    lowest = jnp.max(jnp.where(ends[None, :] <= first, ends[None, :], 0), axis=1)
    highest = jnp.min(jnp.where(ends[None, :] >= first + size, ends[None, :], rows), axis=1)
    start, kind = jnp.zeros_like(lowest), jnp.full_like(lowest, len(widths) - 1)
    for at in range(len(widths) - 2, -1, -1):
        begin = jnp.minimum(lowest // 128 * 128, rows - widths[at])
        fits = highest - begin <= widths[at]
        start = jnp.where(fits, begin, start)
        kind = jnp.where(fits, at, kind)
    return start.astype(jnp.int32), kind.astype(jnp.int32), widths


def each_width(kind, widths, body):
    for at, width in enumerate(widths):
        @pl.when(kind == at)
        def _(width=width):
            body(width)


def forward_kernel(
    widths, start_ref, kind_ref, query_ref, key_ref, value_ref, seg_key_ref, seg_query_ref, out_ref, logsum_ref
):
    block = pl.program_id(1)
    heads = query_ref.shape[1] // HEAD_DIM

    def body(width):
        window = pl.ds(pl.multiple_of(start_ref[block], 128), width)
        allowed = seg_key_ref[window, :] == seg_query_ref[...]
        queries = query_ref[...] * jnp.asarray(HEAD_DIM ** (-0.5), LOW)
        keys, values = key_ref[window, :], value_ref[window, :]
        parts = []
        for head in range(heads):
            scores = keys_by_queries(keys, head_lanes(queries, head))
            scores = jnp.where(allowed, scores, -1000000000.0)
            highest = jnp.max(scores, axis=0, keepdims=True)
            raised = jnp.exp(scores - highest)
            totals = jnp.sum(raised, axis=0, keepdims=True)
            context = lhs_inner(values, raised.astype(LOW))
            rows = slice(head * HEAD_DIM, (head + 1) * HEAD_DIM)
            parts.append(context[rows] / totals)
            logsum_ref[0, head : head + 1, :] = highest + jnp.log(totals)
        out_ref[...] = jnp.concatenate(parts, axis=0).T.astype(LOW)

    each_width(kind_ref[block], widths, body)


def backward_kernel(
    widths, start_ref, kind_ref, query_ref, key_ref, value_ref, seg_key_ref, seg_query_ref, logsum_ref, grad_ref,
    out_ref, sum_ref, key_grad, value_grad,
):
    block = pl.program_id(1)
    size, lanes = query_ref.shape
    heads = lanes // HEAD_DIM
    factor = HEAD_DIM ** (-0.5)

    @pl.when(block == 0)
    def _():
        key_grad[...] = jnp.zeros_like(key_grad)
        value_grad[...] = jnp.zeros_like(value_grad)
        sum_ref[...] = jnp.zeros_like(sum_ref)

    def body(width):
        window = pl.ds(pl.multiple_of(start_ref[block], 128), width)
        allowed = seg_key_ref[window, :] == seg_query_ref[...]
        queries = query_ref[...] * jnp.asarray(factor, LOW)
        grads = grad_ref[...]
        keys, values = key_ref[window, :], value_ref[window, :]
        weight_low, score_low, query_heads, grad_heads, query_parts = [], [], [], [], []
        for head in range(heads):
            query_head, grad_head = head_lanes(queries, head), head_lanes(grads, head)
            scores = jnp.where(allowed, keys_by_queries(keys, query_head), -1000000000.0)
            weights = jnp.exp(scores - logsum_ref[0, head : head + 1, :])
            weight_grad = keys_by_queries(values, grad_head)
            centre = jnp.sum(weight_grad * weights, axis=0, keepdims=True)
            score_grad = (weights * (weight_grad - centre)).astype(LOW)
            rows = slice(head * HEAD_DIM, (head + 1) * HEAD_DIM)
            query_parts.append(lhs_inner(keys, score_grad)[rows] * factor)
            weight_low.append(weights.astype(LOW))
            score_low.append(score_grad)
            query_heads.append(query_head)
            grad_heads.append(grad_head)
        key_grad[window, :] += matmul(
            jnp.concatenate(score_low, axis=1), jnp.concatenate(query_heads, axis=0)
        )
        value_grad[window, :] += matmul(
            jnp.concatenate(weight_low, axis=1), jnp.concatenate(grad_heads, axis=0)
        )
        query_grad = jnp.concatenate(query_parts, axis=0).T
        out_ref[pl.ds(pl.multiple_of(block * size, size), size), :lanes] = query_grad.astype(LOW)
        sum_ref[0, 0:1, :] += jnp.sum(query_grad, axis=0, keepdims=True)

    each_width(kind_ref[block], widths, body)

    @pl.when(block == pl.num_programs(1) - 1)
    def _():
        out_ref[:, lanes : 2 * lanes] = key_grad[...].astype(LOW)
        out_ref[:, 2 * lanes :] = value_grad[...].astype(LOW)
        sum_ref[0, 1:2, :] = jnp.sum(value_grad[...], axis=0, keepdims=True)


def attention_specs(rows, lanes, size):
    return [
        pl.BlockSpec((size, lanes), lambda pair, block, *_: (block, 3 * pair)),
        pl.BlockSpec((rows, lanes), lambda pair, block, *_: (0, 3 * pair + 1)),
        pl.BlockSpec((rows, lanes), lambda pair, block, *_: (0, 3 * pair + 2)),
        pl.BlockSpec((rows, 1), lambda pair, block, *_: (0, 0)),
        pl.BlockSpec((1, size), lambda pair, block, *_: (0, block)),
    ]


def attend_forward(packed, segments, seq_lens, lanes):
    rows = packed.shape[0]
    pairs = packed.shape[1] // (3 * lanes)
    heads = lanes // HEAD_DIM
    size = min(256, rows)
    start, kind, widths = key_windows(seq_lens, rows, size)
    return pl.pallas_call(
        functools.partial(forward_kernel, widths),
        grid_spec=pltpu.PrefetchScalarGridSpec(
            num_scalar_prefetch=2,
            grid=(pairs, rows // size),
            in_specs=attention_specs(rows, lanes, size),
            out_specs=[
                pl.BlockSpec((size, lanes), lambda pair, block, *_: (block, pair)),
                pl.BlockSpec((1, heads, size), lambda pair, block, *_: (pair, 0, block)),
            ],
        ),
        out_shape=[
            jax.ShapeDtypeStruct((rows, pairs * lanes), LOW),
            jax.ShapeDtypeStruct((pairs, heads, rows), WIDE),
        ],
        **flash_params(),
    )(start, kind, packed, packed, packed, segments[:, None], segments[None, :])


def attend_backward(packed, segments, seq_lens, logsums, context_grad, lanes):
    rows = packed.shape[0]
    pairs = packed.shape[1] // (3 * lanes)
    heads = lanes // HEAD_DIM
    size = min(256, rows)
    start, kind, widths = key_windows(seq_lens, rows, size)
    return pl.pallas_call(
        functools.partial(backward_kernel, widths),
        grid_spec=pltpu.PrefetchScalarGridSpec(
            num_scalar_prefetch=2,
            grid=(pairs, rows // size),
            in_specs=attention_specs(rows, lanes, size)
            + [
                pl.BlockSpec((1, heads, size), lambda pair, block, *_: (pair, 0, block)),
                pl.BlockSpec((size, lanes), lambda pair, block, *_: (block, pair)),
            ],
            out_specs=[
                pl.BlockSpec((rows, 3 * lanes), lambda pair, block, *_: (0, pair)),
                pl.BlockSpec((1, 2, lanes), lambda pair, block, *_: (pair, 0, 0)),
            ],
            scratch_shapes=[pltpu.VMEM((rows, lanes), WIDE), pltpu.VMEM((rows, lanes), WIDE)],
        ),
        out_shape=[
            jax.ShapeDtypeStruct((rows, pairs * 3 * lanes), LOW),
            jax.ShapeDtypeStruct((pairs, 2, lanes), WIDE),
        ],
        **flash_params(),
    )(start, kind, packed, packed, packed, segments[:, None], segments[None, :], logsums, context_grad)


def pair_columns(packed, head_half, lanes, back=False):
    ranks = lanes // head_half
    if ranks == 1:
        return packed
    order = (3, ranks) if back else (ranks, 3)
    shaped = packed.reshape(packed.shape[0], -1, order[0], order[1], head_half)
    return jnp.swapaxes(shaped, 2, 3).reshape(packed.shape)


def layer_forward(rows, segments, seq_lens, weights, small, late_weights=None):
    w_qkv, w_out, w_in = weights[:3]
    gains, biases, offset, inner_bias, head_half = small
    lanes = max(head_half, 128)
    packed = (rhs_inner(rows, w_qkv) + offset).astype(LOW)
    packed = pair_columns(packed, head_half, lanes)
    context, logsums = attend_forward(packed, segments, seq_lens, lanes)
    first_sum = rows.astype(WIDE) + core_sum(matmul(context, w_out)) + biases[2]
    middle = (norm_parts(first_sum)[0] * gains[0] + biases[3]).astype(LOW)
    active, slope = gelu_pair(rhs_inner(middle, w_in) + inner_bias)
    active, slope = active.astype(LOW), slope.astype(LOW)
    if late_weights is None:
        w_back = weights[3]
    else:
        active, late = late_weights(active)
        w_back = late[0]
    second_sum = middle.astype(WIDE) + core_sum(matmul(active, w_back)) + biases[4]
    result = norm_parts(second_sum)[0] * gains[1] + biases[5]
    saved = (rows, packed, logsums, context, first_sum, middle, active, slope, second_sum)
    return result, saved, late if late_weights is not None else None


def slab_grads(hidden, features, chips):
    cut = features.shape[1] // chips
    return [lhs_inner(hidden, features[:, k * cut : (k + 1) * cut]).astype(LOW) for k in range(chips)]


def backward_hidden(saved, grad_rows, weights, small):
    _, _, w_in, w_back = weights
    gains = small[0]
    middle, active, slope, second_sum = saved[5:]
    second_grad, gain_two, bias_two = norm_backward(second_sum, gains[1], grad_rows.astype(WIDE))
    branch_grad = second_grad.astype(LOW)
    hidden_low = (rhs_inner(branch_grad, w_back) * slope.astype(WIDE)).astype(LOW)
    middle_grad = second_grad + core_sum(matmul(hidden_low, w_in))
    inner_sum = matmul(jnp.ones((8, hidden_low.shape[0]), LOW), hidden_low)[0]
    sums = (gain_two, jnp.sum(second_grad, axis=0), bias_two, inner_sum)
    return middle_grad, branch_grad, hidden_low, sums


def backward_attention(saved, segments, seq_lens, middle_grad, weights, small):
    _, w_out, _, _ = weights
    gains, head_half = small[0], small[4]
    _, packed, logsums, _, first_sum = saved[:5]
    first_grad, gain_one, bias_one = norm_backward(first_sum, gains[0], middle_grad)
    attended_grad = first_grad.astype(LOW)
    context_grad = rhs_inner(attended_grad, w_out).astype(LOW)
    lanes = max(head_half, 128)
    packed_low, column_sums = attend_backward(packed, segments, seq_lens, logsums, context_grad, lanes)
    packed_low = pair_columns(packed_low, head_half, lanes, back=True)
    sums = (gain_one, jnp.sum(first_grad, axis=0), bias_one) + tuple(
        column_sums[:, at].reshape(-1) for at in range(2)
    )
    return first_grad, attended_grad, packed_low, sums


def on_device(
    block_input, seq_lengths, w_qkv, w_out, w_in, w_back, gains, biases, ffn_bias, out_grad
):
    ranks = lax.axis_size("tensor")
    copies = lax.axis_size("dp")
    chips = copies // 2
    section = lax.axis_index("section")
    copy_at = lax.axis_index("dp")
    rank = lax.axis_index("tensor")
    core = copy_at % 2
    chip = copy_at // 2
    micro_count, own_rows, width = block_input.shape
    repeats = ranks // micro_count
    local = gains.shape[-1]
    counted = (rank % repeats) == 0

    def relative(value):
        slabs = jnp.split(value, chips, axis=-1)
        return jnp.concatenate([choose(chip ^ k, slabs) for k in range(chips)], axis=-1)

    def fetch_rows(block, *before):
        half = own_rows // 2
        kept = choose(core, (block[:, :half], block[:, half:]))
        given = choose(core, (block[:, half:], block[:, :half]))
        received = move(given, lambda s, d, t: (s, d ^ 1, t) if d % 2 == s else None)
        mine = jnp.where(core == section, kept, received)
        mine = jnp.repeat(mine, repeats, axis=0) if repeats > 1 else mine
        mine = after(mine, *before) if before else mine
        mine = lax.all_to_all(mine, "tensor", split_axis=0, concat_axis=0, tiled=True)
        whole = by_core(core, mine, to_other_core(mine), 1)
        return relative(whole.reshape(ranks * own_rows, width))

    def spread_both(first, second):
        chosen = relative(jnp.where(core == 0, first, second)).reshape(ranks, own_rows, width)
        spread = lax.all_to_all(chosen, "tensor", split_axis=0, concat_axis=0, tiled=True)
        return spread.reshape(micro_count, repeats, own_rows, width)[:, 0]

    def place_both(spread):
        moved = move(spread, lambda s, d, t: (d % 2, (d // 2) * 2 + s, t) if d % 2 != s else None)
        return jnp.where(core == section, spread, moved)

    def spread_rows(value):
        parts = relative(value).reshape(ranks, own_rows, width)
        half = own_rows // 2
        mine = choose(core, (parts[:, :half], parts[:, half:]))
        spread = lax.all_to_all(mine, "tensor", split_axis=0, concat_axis=0, tiled=True)
        return spread.reshape((micro_count, repeats) + spread.shape[1:])[:, 0]

    def place_rows(spread, layer):
        halves = []
        for half in range(2):
            own = lambda s, d: half == layer and s == layer and d % 2 == layer
            moved = move(
                spread,
                lambda s, d, t: (layer, (d // 2) * 2 + s, t) if d % 2 == half and not own(s, d) else None,
            )
            if half == layer:
                moved = jnp.where((section == layer) & (core == layer), spread, moved)
            halves.append(moved)
        return jnp.concatenate(halves, axis=1)

    def by_section(first, second):
        return jnp.where(section == 0, first, second)

    def own_half(halves):
        kept = choose(core, (halves[0], halves[1]))
        given = choose(core, (halves[1], halves[0]))
        return by_core(core, kept, to_other_core(given), 1)

    def relay(upward, downward):
        upward.append(move(upward[-1], lambda s, d, t: (s, d, t + 1) if t + 1 < ranks else None))
        downward.append(move(downward[-1], lambda s, d, t: (s, d, t - 1) if t > 0 else None))

    def assemble(upward, downward):
        own = upward[0]
        item = jnp.zeros((ranks,) + own.shape, LOW)
        item = lax.dynamic_update_index_in_dim(item, own, rank, 0)
        for j in range(1, ranks):
            arrived = jnp.where(rank >= j, upward[j], downward[ranks - j])
            item = lax.dynamic_update_index_in_dim(item, arrived, (rank + ranks - j) % ranks, 0)
        return item

    def over_ranks(own):
        upward, downward = [own], [own]
        for _ in range(1, ranks):
            relay(upward, downward)
        return assemble(upward, downward)

    def chips_once(item):
        across = move(item, lambda s, d, t: (1 - s, d, t))
        along = [move(item, lambda s, d, t: (s, d ^ (2 * k), t)) for k in range(1, chips)]
        return across, along

    def chips_twice(item, across, along):
        part = item.shape[0] // 2
        uppers = [move(across[:part], lambda s, d, t: (s, d ^ (2 * k), t)) for k in range(1, chips)]
        lowers = [move(along[k - 1][part:], lambda s, d, t: (1 - s, d, t)) for k in range(1, chips)]
        return uppers, lowers

    def both_layers(item, across, along, uppers, lowers):
        far = [jnp.concatenate(pair, axis=0) for pair in zip(uppers, lowers)]
        mine, other = [item] + along, [across] + far
        result = []
        for layer in range(2):
            slabs = [jnp.where(section == layer, m, o) for m, o in zip(mine, other)]
            result.append(jnp.concatenate(slabs, axis=-1))
        return result

    def over_chips(item):
        across, along = chips_once(item)
        return both_layers(item, across, along, *chips_twice(item, across, along))

    def from_x(slabs):
        return [move(slabs[k], lambda s, d, t: (s, d ^ (2 * k), t)) for k in range(1, chips)]

    def from_section(part, layer):
        return move(part, lambda s, d, t: (layer, d, t) if s != layer else None)

    def add(part, received):
        total = part.astype(WIDE)
        for other in received:
            total = total + other.astype(WIDE)
        return total.astype(LOW)

    def from_z(parts):
        return lax.all_to_all(parts, "tensor", split_axis=0, concat_axis=0, tiled=True)

    def add_ranks(parts):
        return jnp.sum(parts.astype(WIDE), axis=0).astype(LOW)

    def hops_z(parts):
        own = lax.dynamic_index_in_dim(parts, rank, 0, keepdims=False)
        received = [
            move(
                lax.dynamic_index_in_dim(parts, (rank + j) % ranks, 0, keepdims=False),
                lambda s, d, t: (s, d, (t + j) % ranks),
            )
            for j in range(1, ranks)
        ]
        return own, received

    def ranked(slab):
        return slab.reshape((ranks, -1) + slab.shape[1:])

    def counted_only(slabs):
        return [jnp.where(counted, slab, jnp.zeros((), LOW)) for slab in slabs] if repeats > 1 else slabs

    def finish(shard):
        parts = jnp.split(shard, 2, axis=1)
        kept = choose(core, parts)
        given = choose(core, parts[::-1])
        return by_core(core, kept[None], to_other_core(given)[None], 0).astype(WIDE)

    head_half = w_qkv.shape[-1] // 2
    hidden_half = w_in.shape[-1] // 2
    in_first = jnp.moveaxis(w_in[0].reshape(local, 2, hidden_half), 0, 2)
    qkv_first = jnp.transpose(w_qkv[0].reshape(local, 3, 2, head_half), (2, 1, 3, 0))
    qkv_first = qkv_first.reshape(2, 3 * head_half, local)
    out_first = w_out[0].reshape(2, head_half, local)
    back_first = w_back[0].reshape(2, hidden_half, local)
    later = hidden_half // 2
    gain_count, bias_count = gains.shape[1], biases.shape[1]
    table = jnp.concatenate([gains[0], biases[0], ffn_bias.reshape(-1, local)], axis=0)
    table_rows = table.shape[0]
    table = jnp.pad(table, ((0, -table_rows % 16), (0, 0)))
    table = jnp.broadcast_to(table, (2,) + table.shape)
    attention_own = own_half(jnp.concatenate([qkv_first, out_first, table], axis=1))
    back_own = own_half(back_first)
    in_own = own_half(in_first)
    back_two = jnp.stack(over_chips(back_own[later:]))
    attention_item = over_ranks(attention_own)
    attention_item, back_two = tie(attention_item, back_two)
    across, along = chips_once(attention_item)
    rows = fetch_rows(block_input, attention_item)
    in_own = after(in_own, attention_item)
    upward, downward = [in_own], [in_own]
    for at in range(1, ranks):
        relay(upward, downward)
        if at == 1:
            upward[-1], downward[-1], seq_lengths = tie(upward[-1], downward[-1], seq_lengths)
        if at == ranks // 2:
            upward[-1], downward[-1], across, *along = tie(upward[-1], downward[-1], across, *along)
            uppers, lowers = chips_twice(attention_item, across, along)
    upward[-1], downward[-1], *far = tie(upward[-1], downward[-1], *uppers, *lowers)
    attention_all = both_layers(attention_item, across, along, far[: chips - 1], far[chips - 1 :])
    in_item = assemble(upward, downward)
    in_across, in_along = chips_once(in_item)
    back_one = after(back_own[:later], in_item)
    back_up, back_down = [back_one], [back_one]
    for at in range(1, ranks):
        relay(back_up, back_down)
        if at == 1:
            rows, back_up[-1], back_down[-1] = tie(rows, back_up[-1], back_down[-1])
    back_item = assemble(back_up, back_down)
    back_item, back_two, in_across, *in_along = tie(back_item, back_two, in_across, *in_along)
    in_all = both_layers(in_item, in_across, in_along, *chips_twice(in_item, in_across, in_along))
    across, along = chips_once(back_item)
    upward, downward = [back_two], [back_two]
    for _ in range(1, ranks):
        relay(upward, downward)

    def late_weights(active):
        tied = tie(active, across, upward[-1], downward[-1], *along)
        here = (back_item, tied[1], list(tied[4:]))
        halves = zip(
            both_layers(*here, *chips_twice(*here)),
            jnp.moveaxis(assemble(upward[:-1] + [tied[2]], downward[:-1] + [tied[3]]), 1, 0),
        )
        return tied[0], [jnp.concatenate(pair, axis=1).reshape(-1, width) for pair in halves]

    weights = [
        (
            attention_all[layer][:, : 3 * head_half].reshape(-1, width),
            attention_all[layer][:, 3 * head_half : 4 * head_half].reshape(-1, width),
            in_all[layer].reshape(-1, width),
        )
        for layer in range(2)
    ]

    def head_columns(row):
        halves = row.reshape(ranks, 2, -1)
        return choose(core, (halves[:, 0], halves[:, 1])).reshape(-1)

    small = []
    for layer in range(2):
        table = attention_all[layer][0, 4 * head_half : 4 * head_half + table_rows].astype(WIDE)
        whole = relative(table)
        query_bias = head_columns(whole[gain_count])
        value_bias = head_columns(whole[gain_count + 1])
        query_bias, value_bias = query_bias.reshape(ranks, 1, -1), value_bias.reshape(ranks, 1, -1)
        offset = jnp.concatenate([query_bias, jnp.zeros_like(query_bias), value_bias], axis=1).reshape(-1)
        inner_bias = whole[gain_count + bias_count :].reshape(-1, copies, local)
        inner_bias = head_columns(jnp.swapaxes(inner_bias, 0, 1).reshape(-1))
        small.append((table[:gain_count], table[gain_count : gain_count + bias_count], offset, inner_bias, head_half))

    lengths = jnp.where(core == section, seq_lengths, to_other_core(seq_lengths))[:, 0]
    lengths = lax.dynamic_index_in_dim(lengths, rank // repeats, 0, keepdims=False)
    segments = segment_ids(lengths, ranks * own_rows)
    live = (segments < lengths.shape[0])[:, None]

    first_out, first_saved, late = layer_forward(rows, segments, lengths, weights[0], small[0], late_weights)
    weights = [weights[layer] + (late[layer],) for layer in range(2)]
    first_low = first_out.astype(LOW)
    cotangent = fetch_rows(out_grad, back_two)
    cotangent = jnp.where(live, cotangent, jnp.zeros((), LOW))
    second_out, second_saved, _ = layer_forward(first_low, segments, lengths, weights[1], small[1])
    spread = spread_both(first_low, second_out.astype(LOW))

    def hidden_grads(hidden, features):
        return [ranked(slab) for slab in counted_only(slab_grads(hidden, features, chips))]

    def attention_grads(saved, attended_grad, packed_low):
        qkv = hidden_grads(packed_low, saved[0])
        out = hidden_grads(saved[3], attended_grad)
        return [jnp.concatenate(pair, axis=1) for pair in zip(qkv, out)]

    middle_grad, branch_grad, hidden_low, second_sums = backward_hidden(
        second_saved, cotangent, weights[1], small[1]
    )
    back_slabs = hidden_grads(second_saved[6], branch_grad)
    back_here = from_x(back_slabs)
    in_slabs = hidden_grads(hidden_low, second_saved[5])
    in_here = from_x(in_slabs)
    first_grad, attended_grad, packed_low, more_sums = backward_attention(
        second_saved, segments, lengths, middle_grad, weights[1], small[1]
    )
    second_sums += more_sums
    packed_low, spread, *back_here = tie(packed_low, spread, *back_here)
    back_two = add(back_slabs[0], back_here)
    back_sent = from_section(back_two, 1)
    placed = place_both(spread)
    second_in = first_grad + core_sum(matmul(packed_low, weights[1][0]))
    qkv, out = [
        ranked(counted_only([lhs_inner(hidden, features).astype(LOW)])[0])
        for hidden, features in ((packed_low, second_saved[0]), (second_saved[3], attended_grad))
    ]
    attention_here = from_z(jnp.concatenate([qkv, out], axis=1))
    second_low = second_in.astype(LOW)

    middle_grad, branch_grad, hidden_low, first_sums = backward_hidden(
        first_saved, second_low, weights[0], small[0]
    )
    middle_grad, back_sent, placed, *in_here = tie(middle_grad, back_sent, placed, *in_here)
    back_two = add(back_two, [back_sent])
    in_two = add(in_slabs[0], in_here)
    in_sent = from_section(in_two, 1)
    outputs = placed.astype(WIDE)[None]
    second_in_spread = spread_rows(second_low)
    back_slabs = hidden_grads(first_saved[6], branch_grad)
    back_here = from_x(back_slabs)
    in_slabs = hidden_grads(hidden_low, first_saved[5])
    in_here = from_x(in_slabs)
    first_grad, attended_grad, packed_low, more_sums = backward_attention(
        first_saved, segments, lengths, middle_grad, weights[0], small[0]
    )
    first_sums += more_sums
    packed_low, in_sent, second_in_spread, *back_here = tie(packed_low, in_sent, second_in_spread, *back_here)
    in_two = add(in_two, [in_sent])
    back_one = add(back_slabs[0], back_here)
    back_sent = from_section(back_one, 0)
    second_placed = place_rows(second_in_spread, 1)
    first_in = first_grad + core_sum(matmul(packed_low, weights[0][0]))
    attention_slabs = attention_grads(first_saved, attended_grad, packed_low)
    attention_one_here = from_x(attention_slabs)
    first_in, attention_here, back_sent, *held = tie(
        first_in, attention_here, back_sent, *in_here, *attention_one_here, *attention_slabs
    )
    in_one = add(in_slabs[0], held[: chips - 1])
    attention_one_here, attention_slabs = held[chips - 1 : 2 * chips - 2], held[2 * chips - 2 :]
    attention_one = add(attention_slabs[0], attention_one_here)
    in_sent = from_section(in_one, 0)
    attention_one_sent = from_section(attention_one, 0)
    back_own, back_here = hops_z(by_section(add(back_one, [back_sent]), back_two))
    first_in_spread = spread_rows(first_in.astype(LOW))
    attention_two_slabs = jnp.split(add_ranks(attention_here), chips, axis=-1)
    attention_two_here = from_x(attention_two_slabs)

    def spread_columns(row):
        blocks = row.reshape(ranks, 1, -1)
        both = jnp.where(jnp.arange(2)[None, :, None] == core, blocks, 0.0)
        return both.reshape(-1, width)

    tables = []
    for sums in (first_sums, second_sums):
        gain_two, bias_four, bias_five, inner_sum, gain_one, bias_two, bias_three, query_sum, value_sum = sums
        common = jnp.stack([gain_one, gain_two, bias_two, bias_three, bias_four, bias_five])
        common = jnp.where(core == 0, relative(common), 0.0)
        tables.append(
            jnp.concatenate(
                [common[:2], spread_columns(query_sum), spread_columns(value_sum), common[2:], spread_columns(inner_sum)]
            )
        )
    table = jnp.stack(tables)
    table = jnp.where(counted, table, 0.0) if repeats > 1 else table
    table = table + to_other_core(table)
    table, table_sent = choose(section, (table[0], table[1])), move(
        choose(section, (table[1], table[0])), lambda s, d, t: (1 - s, d, t)
    )

    in_sent, first_in_spread, table_sent, *held = tie(
        in_sent, first_in_spread, table_sent, *attention_two_here, *back_here
    )
    table = table + table_sent
    beside = [move(table, lambda s, d, t: (s, d ^ (2 * k), t)) for k in range(1, chips)]
    attention_two = add(attention_two_slabs[0], held[: chips - 1])
    attention_two_sent = from_section(attention_two, 1)
    back_here = held[chips - 1 :]
    in_own, in_here = hops_z(by_section(add(in_one, [in_sent]), in_two))

    attention_one_sent, attention_two_sent, *beside = tie(attention_one_sent, attention_two_sent, *beside)
    table = sum(beside, table)
    attention_own, attention_here = hops_z(add(attention_one, [attention_one_sent]))
    first_placed = place_rows(first_in_spread, 0)
    back_shard = finish(add(back_own, back_here))
    table = sum([move(table, lambda s, d, t: (s, d, (t + j) % ranks)) for j in range(1, ranks)], table)
    attention_one_sent, *in_here = tie(attention_one_sent, *in_here)
    attention_two = add(attention_two, [attention_two_sent])
    in_shard = finish(add(in_own, in_here))
    input_grads = by_section(first_placed, second_placed).astype(WIDE)[None]
    attention_shard = finish(by_section(add(attention_own, attention_here), attention_two))
    qkv_shard, out_shard = attention_shard[:, : 3 * head_half], attention_shard[:, 3 * head_half :]
    qkv_grad = jnp.transpose(qkv_shard.reshape(2, 3, head_half, local), (3, 1, 0, 2)).reshape(local, 3, -1)
    out_grad_w = out_shard.reshape(-1, local)
    in_grad = jnp.transpose(in_shard.reshape(-1, local))
    back_grad = back_shard.reshape(-1, local)
    sliced = lax.dynamic_slice_in_dim(table[: gain_count + bias_count], copy_at * local, local, 1)
    inner = lax.dynamic_index_in_dim(
        table[gain_count + bias_count :].reshape(copies, -1), copy_at, 0, keepdims=False
    )
    return (
        outputs,
        input_grads,
        qkv_grad[None],
        out_grad_w[None],
        in_grad[None],
        back_grad[None],
        sliced[None, :gain_count],
        sliced[None, gain_count:],
        inner[None],
    )


def solution(mesh):
    return jax.shard_map(
        on_device,
        mesh=mesh,
        in_specs=(
            P(None, ("dp", "tensor"), None),
            P(None, "dp", None),
            P("section", "dp", None, "tensor"),
            P("section", "tensor", "dp"),
            P("section", "dp", "tensor"),
            P("section", "tensor", "dp"),
            P("section", None, "dp"),
            P("section", None, "dp"),
            P("section", "dp"),
            P(None, ("dp", "tensor"), None),
        ),
        out_specs=(
            P("section", None, ("dp", "tensor"), None),
            P("section", None, ("dp", "tensor"), None),
            P("section", "dp", None, "tensor"),
            P("section", "tensor", "dp"),
            P("section", "dp", "tensor"),
            P("section", "tensor", "dp"),
            P("section", None, "dp"),
            P("section", None, "dp"),
            P("section", "dp"),
        ),
        check_vma=False,
    )
```

```python
import functools

import jax
import jax.numpy as jnp
from jax import lax
from jax.experimental import pallas as pl
from jax.experimental.pallas import tpu as pltpu
from jax.sharding import PartitionSpec as P

HEAD_DIM = 64
AXES = ("section", "dp", "tensor")
LOW = jnp.bfloat16
WIDE = jnp.float32


def move(value, target):
    sections, copies, ranks = (lax.axis_size(axis) for axis in AXES)
    pairs = []
    for s in range(sections):
        for d in range(copies):
            for t in range(ranks):
                goal = target(s, d, t)
                if goal is not None:
                    pairs.append(
                        ((s * copies + d) * ranks + t, (goal[0] * copies + goal[1]) * ranks + goal[2])
                    )
    return lax.ppermute(value, AXES, pairs)


def to_other_core(value):
    return move(value, lambda s, d, t: (s, d ^ 1, t))


def by_core(core, kept, received, axis):
    return jnp.where(
        core == 0,
        jnp.concatenate([kept, received], axis=axis),
        jnp.concatenate([received, kept], axis=axis),
    )


def choose(place, options):
    chosen = options[0]
    for at, option in enumerate(options[1:], 1):
        chosen = jnp.where(place == at, option, chosen)
    return chosen


def after(value, *others):
    return lax.optimization_barrier((value,) + others)[0]


def tie(*values):
    return lax.optimization_barrier(values)


def matmul(lhs_mat, rhs_mat):
    return jnp.dot(lhs_mat, rhs_mat, preferred_element_type=WIDE)


def lhs_inner(lhs_mat, rhs_mat):
    return lax.dot_general(
        lhs_mat, rhs_mat, (((0,), (0,)), ((), ())), preferred_element_type=WIDE
    )


def rhs_inner(lhs_mat, rhs_mat):
    return lax.dot_general(
        lhs_mat, rhs_mat, (((1,), (1,)), ((), ())), preferred_element_type=WIDE
    )


def core_sum(partial):
    low = partial.astype(LOW)
    return low.astype(WIDE) + to_other_core(low).astype(WIDE)


def norm_parts(summed):
    centered = summed - jnp.mean(summed, axis=-1, keepdims=True)
    variance = jnp.mean(centered * centered, axis=-1, keepdims=True)
    scale = lax.rsqrt(variance + 1e-05)
    return centered * scale, scale


def norm_backward(summed, gain_row, grad):
    unit, scale = norm_parts(summed)
    gain_grad = jnp.sum(grad * unit, axis=0)
    bias_grad = jnp.sum(grad, axis=0)
    inner = grad * gain_row
    result = scale * (
        inner
        - jnp.mean(inner, axis=-1, keepdims=True)
        - unit * jnp.mean(inner * unit, axis=-1, keepdims=True)
    )
    return result, gain_grad, bias_grad


def gelu_pair(values):
    below = 0.5 * (1.0 + lax.erf(values * (0.5**0.5)))
    density = jnp.exp(-0.5 * values * values) * (0.3989422804014327)
    return values * below, below + values * density


def segment_ids(seq_lens, row_count):
    seq_ends = jnp.cumsum(seq_lens)
    positions = jnp.arange(row_count, dtype=jnp.int32)
    return jnp.sum((positions[:, None] >= seq_ends[None, :]).astype(jnp.int32), axis=1)


def flash_params():
    return dict(
        cost_estimate=pl.CostEstimate(flops=0, transcendentals=0, bytes_accessed=0),
        compiler_params=pltpu.CompilerParams(vmem_limit_bytes=48 * 1024 * 1024),
    )


def head_lanes(values, head):
    lane = lax.broadcasted_iota(jnp.int32, values.shape, 1)
    return jnp.where((lane // HEAD_DIM) == head, values, jnp.zeros_like(values))


def keys_by_queries(keys, queries):
    return lax.dot_general(keys, queries, (((1,), (1,)), ((), ())), preferred_element_type=WIDE)


def key_windows(seq_lens, rows, size):
    widths = tuple(sorted({min(rows, width) for width in (512, 640, 768, rows)}))
    ends = jnp.cumsum(seq_lens)
    first = jnp.arange(rows // size, dtype=jnp.int32)[:, None] * size
    lowest = jnp.max(jnp.where(ends[None, :] <= first, ends[None, :], 0), axis=1)
    highest = jnp.min(jnp.where(ends[None, :] >= first + size, ends[None, :], rows), axis=1)
    start, kind = jnp.zeros_like(lowest), jnp.full_like(lowest, len(widths) - 1)
    for at in range(len(widths) - 2, -1, -1):
        begin = jnp.minimum(lowest // 128 * 128, rows - widths[at])
        fits = highest - begin <= widths[at]
        start = jnp.where(fits, begin, start)
        kind = jnp.where(fits, at, kind)
    return start.astype(jnp.int32), kind.astype(jnp.int32), widths


def each_width(kind, widths, body):
    for at, width in enumerate(widths):
        @pl.when(kind == at)
        def _(width=width):
            body(width)


def forward_kernel(
    widths, start_ref, kind_ref, query_ref, key_ref, value_ref, seg_key_ref, seg_query_ref, out_ref, logsum_ref
):
    block = pl.program_id(1)
    heads = query_ref.shape[1] // HEAD_DIM

    def body(width):
        window = pl.ds(pl.multiple_of(start_ref[block], 128), width)
        allowed = seg_key_ref[window, :] == seg_query_ref[...]
        queries = query_ref[...] * jnp.asarray(HEAD_DIM ** (-0.5), LOW)
        keys, values = key_ref[window, :], value_ref[window, :]
        parts = []
        for head in range(heads):
            scores = keys_by_queries(keys, head_lanes(queries, head))
            scores = jnp.where(allowed, scores, -1000000000.0)
            highest = jnp.max(scores, axis=0, keepdims=True)
            raised = jnp.exp(scores - highest)
            totals = jnp.sum(raised, axis=0, keepdims=True)
            context = lhs_inner(values, raised.astype(LOW))
            rows = slice(head * HEAD_DIM, (head + 1) * HEAD_DIM)
            parts.append(context[rows] / totals)
            logsum_ref[0, head : head + 1, :] = highest + jnp.log(totals)
        out_ref[...] = jnp.concatenate(parts, axis=0).T.astype(LOW)

    each_width(kind_ref[block], widths, body)


def backward_kernel(
    widths, start_ref, kind_ref, query_ref, key_ref, value_ref, seg_key_ref, seg_query_ref, logsum_ref, grad_ref,
    out_ref, sum_ref, key_grad, value_grad,
):
    block = pl.program_id(1)
    size, lanes = query_ref.shape
    heads = lanes // HEAD_DIM
    factor = HEAD_DIM ** (-0.5)

    @pl.when(block == 0)
    def _():
        key_grad[...] = jnp.zeros_like(key_grad)
        value_grad[...] = jnp.zeros_like(value_grad)
        sum_ref[...] = jnp.zeros_like(sum_ref)

    def body(width):
        window = pl.ds(pl.multiple_of(start_ref[block], 128), width)
        allowed = seg_key_ref[window, :] == seg_query_ref[...]
        queries = query_ref[...] * jnp.asarray(factor, LOW)
        grads = grad_ref[...]
        keys, values = key_ref[window, :], value_ref[window, :]
        weight_low, score_low, query_heads, grad_heads, query_parts = [], [], [], [], []
        for head in range(heads):
            query_head, grad_head = head_lanes(queries, head), head_lanes(grads, head)
            scores = jnp.where(allowed, keys_by_queries(keys, query_head), -1000000000.0)
            weights = jnp.exp(scores - logsum_ref[0, head : head + 1, :])
            weight_grad = keys_by_queries(values, grad_head)
            centre = jnp.sum(weight_grad * weights, axis=0, keepdims=True)
            score_grad = (weights * (weight_grad - centre)).astype(LOW)
            rows = slice(head * HEAD_DIM, (head + 1) * HEAD_DIM)
            query_parts.append(lhs_inner(keys, score_grad)[rows] * factor)
            weight_low.append(weights.astype(LOW))
            score_low.append(score_grad)
            query_heads.append(query_head)
            grad_heads.append(grad_head)
        key_grad[window, :] += matmul(
            jnp.concatenate(score_low, axis=1), jnp.concatenate(query_heads, axis=0)
        )
        value_grad[window, :] += matmul(
            jnp.concatenate(weight_low, axis=1), jnp.concatenate(grad_heads, axis=0)
        )
        query_grad = jnp.concatenate(query_parts, axis=0).T
        out_ref[pl.ds(pl.multiple_of(block * size, size), size), :lanes] = query_grad.astype(LOW)
        sum_ref[0, 0:1, :] += jnp.sum(query_grad, axis=0, keepdims=True)

    each_width(kind_ref[block], widths, body)

    @pl.when(block == pl.num_programs(1) - 1)
    def _():
        out_ref[:, lanes : 2 * lanes] = key_grad[...].astype(LOW)
        out_ref[:, 2 * lanes :] = value_grad[...].astype(LOW)
        sum_ref[0, 1:2, :] = jnp.sum(value_grad[...], axis=0, keepdims=True)


def attention_specs(rows, lanes, size):
    return [
        pl.BlockSpec((size, lanes), lambda pair, block, *_: (block, 3 * pair)),
        pl.BlockSpec((rows, lanes), lambda pair, block, *_: (0, 3 * pair + 1)),
        pl.BlockSpec((rows, lanes), lambda pair, block, *_: (0, 3 * pair + 2)),
        pl.BlockSpec((rows, 1), lambda pair, block, *_: (0, 0)),
        pl.BlockSpec((1, size), lambda pair, block, *_: (0, block)),
    ]


def attend_forward(packed, segments, seq_lens, lanes):
    rows = packed.shape[0]
    pairs = packed.shape[1] // (3 * lanes)
    heads = lanes // HEAD_DIM
    size = min(256, rows)
    start, kind, widths = key_windows(seq_lens, rows, size)
    return pl.pallas_call(
        functools.partial(forward_kernel, widths),
        grid_spec=pltpu.PrefetchScalarGridSpec(
            num_scalar_prefetch=2,
            grid=(pairs, rows // size),
            in_specs=attention_specs(rows, lanes, size),
            out_specs=[
                pl.BlockSpec((size, lanes), lambda pair, block, *_: (block, pair)),
                pl.BlockSpec((1, heads, size), lambda pair, block, *_: (pair, 0, block)),
            ],
        ),
        out_shape=[
            jax.ShapeDtypeStruct((rows, pairs * lanes), LOW),
            jax.ShapeDtypeStruct((pairs, heads, rows), WIDE),
        ],
        **flash_params(),
    )(start, kind, packed, packed, packed, segments[:, None], segments[None, :])


def attend_backward(packed, segments, seq_lens, logsums, context_grad, lanes):
    rows = packed.shape[0]
    pairs = packed.shape[1] // (3 * lanes)
    heads = lanes // HEAD_DIM
    size = min(256, rows)
    start, kind, widths = key_windows(seq_lens, rows, size)
    return pl.pallas_call(
        functools.partial(backward_kernel, widths),
        grid_spec=pltpu.PrefetchScalarGridSpec(
            num_scalar_prefetch=2,
            grid=(pairs, rows // size),
            in_specs=attention_specs(rows, lanes, size)
            + [
                pl.BlockSpec((1, heads, size), lambda pair, block, *_: (pair, 0, block)),
                pl.BlockSpec((size, lanes), lambda pair, block, *_: (block, pair)),
            ],
            out_specs=[
                pl.BlockSpec((rows, 3 * lanes), lambda pair, block, *_: (0, pair)),
                pl.BlockSpec((1, 2, lanes), lambda pair, block, *_: (pair, 0, 0)),
            ],
            scratch_shapes=[pltpu.VMEM((rows, lanes), WIDE), pltpu.VMEM((rows, lanes), WIDE)],
        ),
        out_shape=[
            jax.ShapeDtypeStruct((rows, pairs * 3 * lanes), LOW),
            jax.ShapeDtypeStruct((pairs, 2, lanes), WIDE),
        ],
        **flash_params(),
    )(start, kind, packed, packed, packed, segments[:, None], segments[None, :], logsums, context_grad)


def pair_columns(packed, head_half, lanes, back=False):
    ranks = lanes // head_half
    if ranks == 1:
        return packed
    order = (3, ranks) if back else (ranks, 3)
    shaped = packed.reshape(packed.shape[0], -1, order[0], order[1], head_half)
    return jnp.swapaxes(shaped, 2, 3).reshape(packed.shape)


def layer_forward(rows, segments, seq_lens, weights, small, late_weights=None):
    w_qkv, w_out, w_in = weights[:3]
    gains, biases, offset, inner_bias, head_half = small
    lanes = max(head_half, 128)
    packed = (rhs_inner(rows, w_qkv) + offset).astype(LOW)
    packed = pair_columns(packed, head_half, lanes)
    context, logsums = attend_forward(packed, segments, seq_lens, lanes)
    first_sum = rows.astype(WIDE) + core_sum(matmul(context, w_out)) + biases[2]
    middle = (norm_parts(first_sum)[0] * gains[0] + biases[3]).astype(LOW)
    active, slope = gelu_pair(rhs_inner(middle, w_in) + inner_bias)
    active, slope = active.astype(LOW), slope.astype(LOW)
    if late_weights is None:
        w_back = weights[3]
    else:
        active, late = late_weights(active)
        w_back = late[0]
    second_sum = middle.astype(WIDE) + core_sum(matmul(active, w_back)) + biases[4]
    result = norm_parts(second_sum)[0] * gains[1] + biases[5]
    saved = (rows, packed, logsums, context, first_sum, middle, active, slope, second_sum)
    return result, saved, late if late_weights is not None else None


def slab_grads(hidden, features, chips):
    cut = features.shape[1] // chips
    return [lhs_inner(hidden, features[:, k * cut : (k + 1) * cut]).astype(LOW) for k in range(chips)]


def backward_hidden(saved, grad_rows, weights, small):
    _, _, w_in, w_back = weights
    gains = small[0]
    middle, active, slope, second_sum = saved[5:]
    second_grad, gain_two, bias_two = norm_backward(second_sum, gains[1], grad_rows.astype(WIDE))
    branch_grad = second_grad.astype(LOW)
    hidden_low = (rhs_inner(branch_grad, w_back) * slope.astype(WIDE)).astype(LOW)
    middle_grad = second_grad + core_sum(matmul(hidden_low, w_in))
    inner_sum = matmul(jnp.ones((8, hidden_low.shape[0]), LOW), hidden_low)[0]
    sums = (gain_two, jnp.sum(second_grad, axis=0), bias_two, inner_sum)
    return middle_grad, branch_grad, hidden_low, sums


def backward_attention(saved, segments, seq_lens, middle_grad, weights, small):
    _, w_out, _, _ = weights
    gains, head_half = small[0], small[4]
    _, packed, logsums, _, first_sum = saved[:5]
    first_grad, gain_one, bias_one = norm_backward(first_sum, gains[0], middle_grad)
    attended_grad = first_grad.astype(LOW)
    context_grad = rhs_inner(attended_grad, w_out).astype(LOW)
    lanes = max(head_half, 128)
    packed_low, column_sums = attend_backward(packed, segments, seq_lens, logsums, context_grad, lanes)
    packed_low = pair_columns(packed_low, head_half, lanes, back=True)
    sums = (gain_one, jnp.sum(first_grad, axis=0), bias_one) + tuple(
        column_sums[:, at].reshape(-1) for at in range(2)
    )
    return first_grad, attended_grad, packed_low, sums


def on_device(
    block_input, seq_lengths, w_qkv, w_out, w_in, w_back, gains, biases, ffn_bias, out_grad
):
    ranks = lax.axis_size("tensor")
    copies = lax.axis_size("dp")
    chips = copies // 2
    section = lax.axis_index("section")
    copy_at = lax.axis_index("dp")
    rank = lax.axis_index("tensor")
    core = copy_at % 2
    chip = copy_at // 2
    micro_count, own_rows, width = block_input.shape
    repeats = ranks // micro_count
    local = gains.shape[-1]
    counted = (rank % repeats) == 0

    def relative(value):
        slabs = jnp.split(value, chips, axis=-1)
        return jnp.concatenate([choose(chip ^ k, slabs) for k in range(chips)], axis=-1)

    def fetch_rows(block, *before):
        half = own_rows // 2
        kept = choose(core, (block[:, :half], block[:, half:]))
        given = choose(core, (block[:, half:], block[:, :half]))
        received = move(given, lambda s, d, t: (s, d ^ 1, t) if d % 2 == s else None)
        mine = jnp.where(core == section, kept, received)
        mine = jnp.repeat(mine, repeats, axis=0) if repeats > 1 else mine
        mine = after(mine, *before) if before else mine
        mine = lax.all_to_all(mine, "tensor", split_axis=0, concat_axis=0, tiled=True)
        whole = by_core(core, mine, to_other_core(mine), 1)
        return relative(whole.reshape(ranks * own_rows, width))

    def spread_both(first, second):
        chosen = relative(jnp.where(core == 0, first, second)).reshape(ranks, own_rows, width)
        spread = lax.all_to_all(chosen, "tensor", split_axis=0, concat_axis=0, tiled=True)
        return spread.reshape(micro_count, repeats, own_rows, width)[:, 0]

    def place_both(spread):
        moved = move(spread, lambda s, d, t: (d % 2, (d // 2) * 2 + s, t) if d % 2 != s else None)
        return jnp.where(core == section, spread, moved)

    def spread_rows(value):
        parts = relative(value).reshape(ranks, own_rows, width)
        half = own_rows // 2
        mine = choose(core, (parts[:, :half], parts[:, half:]))
        spread = lax.all_to_all(mine, "tensor", split_axis=0, concat_axis=0, tiled=True)
        return spread.reshape((micro_count, repeats) + spread.shape[1:])[:, 0]

    def place_rows(spread, layer):
        halves = []
        for half in range(2):
            own = lambda s, d: half == layer and s == layer and d % 2 == layer
            moved = move(
                spread,
                lambda s, d, t: (layer, (d // 2) * 2 + s, t) if d % 2 == half and not own(s, d) else None,
            )
            if half == layer:
                moved = jnp.where((section == layer) & (core == layer), spread, moved)
            halves.append(moved)
        return jnp.concatenate(halves, axis=1)

    def by_section(first, second):
        return jnp.where(section == 0, first, second)

    def own_half(halves):
        kept = choose(core, (halves[0], halves[1]))
        given = choose(core, (halves[1], halves[0]))
        return by_core(core, kept, to_other_core(given), 1)

    def relay(upward, downward):
        upward.append(move(upward[-1], lambda s, d, t: (s, d, t + 1) if t + 1 < ranks else None))
        downward.append(move(downward[-1], lambda s, d, t: (s, d, t - 1) if t > 0 else None))

    def assemble(upward, downward):
        own = upward[0]
        item = jnp.zeros((ranks,) + own.shape, LOW)
        item = lax.dynamic_update_index_in_dim(item, own, rank, 0)
        for j in range(1, ranks):
            arrived = jnp.where(rank >= j, upward[j], downward[ranks - j])
            item = lax.dynamic_update_index_in_dim(item, arrived, (rank + ranks - j) % ranks, 0)
        return item

    def over_ranks(own):
        upward, downward = [own], [own]
        for _ in range(1, ranks):
            relay(upward, downward)
        return assemble(upward, downward)

    def chips_once(item):
        across = move(item, lambda s, d, t: (1 - s, d, t))
        along = [move(item, lambda s, d, t: (s, d ^ (2 * k), t)) for k in range(1, chips)]
        return across, along

    def chips_twice(item, across, along):
        part = item.shape[0] // 2
        uppers = [move(across[:part], lambda s, d, t: (s, d ^ (2 * k), t)) for k in range(1, chips)]
        lowers = [move(along[k - 1][part:], lambda s, d, t: (1 - s, d, t)) for k in range(1, chips)]
        return uppers, lowers

    def both_layers(item, across, along, uppers, lowers):
        far = [jnp.concatenate(pair, axis=0) for pair in zip(uppers, lowers)]
        mine, other = [item] + along, [across] + far
        result = []
        for layer in range(2):
            slabs = [jnp.where(section == layer, m, o) for m, o in zip(mine, other)]
            result.append(jnp.concatenate(slabs, axis=-1))
        return result

    def over_chips(item):
        across, along = chips_once(item)
        return both_layers(item, across, along, *chips_twice(item, across, along))

    def from_x(slabs):
        return [move(slabs[k], lambda s, d, t: (s, d ^ (2 * k), t)) for k in range(1, chips)]

    def from_section(part, layer):
        return move(part, lambda s, d, t: (layer, d, t) if s != layer else None)

    def add(part, received):
        total = part.astype(WIDE)
        for other in received:
            total = total + other.astype(WIDE)
        return total.astype(LOW)

    def from_z(parts):
        return lax.all_to_all(parts, "tensor", split_axis=0, concat_axis=0, tiled=True)

    def add_ranks(parts):
        return jnp.sum(parts.astype(WIDE), axis=0).astype(LOW)

    def hops_z(parts):
        own = lax.dynamic_index_in_dim(parts, rank, 0, keepdims=False)
        received = [
            move(
                lax.dynamic_index_in_dim(parts, (rank + j) % ranks, 0, keepdims=False),
                lambda s, d, t: (s, d, (t + j) % ranks),
            )
            for j in range(1, ranks)
        ]
        return own, received

    def ranked(slab):
        return slab.reshape((ranks, -1) + slab.shape[1:])

    def counted_only(slabs):
        return [jnp.where(counted, slab, jnp.zeros((), LOW)) for slab in slabs] if repeats > 1 else slabs

    def finish(shard):
        parts = jnp.split(shard, 2, axis=1)
        kept = choose(core, parts)
        given = choose(core, parts[::-1])
        return by_core(core, kept[None], to_other_core(given)[None], 0).astype(WIDE)

    head_half = w_qkv.shape[-1] // 2
    hidden_half = w_in.shape[-1] // 2
    in_first = jnp.moveaxis(w_in[0].reshape(local, 2, hidden_half), 0, 2)
    qkv_first = jnp.transpose(w_qkv[0].reshape(local, 3, 2, head_half), (2, 1, 3, 0))
    qkv_first = qkv_first.reshape(2, 3 * head_half, local)
    out_first = w_out[0].reshape(2, head_half, local)
    back_first = w_back[0].reshape(2, hidden_half, local)
    later = hidden_half // 2
    gain_count, bias_count = gains.shape[1], biases.shape[1]
    table = jnp.concatenate([gains[0], biases[0], ffn_bias.reshape(-1, local)], axis=0)
    table_rows = table.shape[0]
    table = jnp.pad(table, ((0, -table_rows % 16), (0, 0)))
    table = jnp.broadcast_to(table, (2,) + table.shape)
    attention_own = own_half(jnp.concatenate([qkv_first, out_first, table], axis=1))
    back_own = own_half(back_first)
    in_own = own_half(in_first)
    back_two = jnp.stack(over_chips(back_own[later:]))
    attention_item = over_ranks(attention_own)
    attention_item, back_two = tie(attention_item, back_two)
    across, along = chips_once(attention_item)
    rows = fetch_rows(block_input, attention_item)
    in_own = after(in_own, attention_item)
    upward, downward = [in_own], [in_own]
    for at in range(1, ranks):
        relay(upward, downward)
        if at == 1:
            upward[-1], downward[-1], seq_lengths = tie(upward[-1], downward[-1], seq_lengths)
        if at == ranks // 2:
            upward[-1], downward[-1], across, *along = tie(upward[-1], downward[-1], across, *along)
            uppers, lowers = chips_twice(attention_item, across, along)
    upward[-1], downward[-1], *far = tie(upward[-1], downward[-1], *uppers, *lowers)
    attention_all = both_layers(attention_item, across, along, far[: chips - 1], far[chips - 1 :])
    in_item = assemble(upward, downward)
    in_across, in_along = chips_once(in_item)
    back_one = after(back_own[:later], in_item)
    back_up, back_down = [back_one], [back_one]
    for at in range(1, ranks):
        relay(back_up, back_down)
        if at == 1:
            rows, back_up[-1], back_down[-1] = tie(rows, back_up[-1], back_down[-1])
    back_item = assemble(back_up, back_down)
    back_item, back_two, in_across, *in_along = tie(back_item, back_two, in_across, *in_along)
    in_all = both_layers(in_item, in_across, in_along, *chips_twice(in_item, in_across, in_along))
    across, along = chips_once(back_item)
    upward, downward = [back_two], [back_two]
    for _ in range(1, ranks):
        relay(upward, downward)

    def late_weights(active):
        tied = tie(active, across, upward[-1], downward[-1], *along)
        here = (back_item, tied[1], list(tied[4:]))
        halves = zip(
            both_layers(*here, *chips_twice(*here)),
            jnp.moveaxis(assemble(upward[:-1] + [tied[2]], downward[:-1] + [tied[3]]), 1, 0),
        )
        return tied[0], [jnp.concatenate(pair, axis=1).reshape(-1, width) for pair in halves]

    weights = [
        (
            attention_all[layer][:, : 3 * head_half].reshape(-1, width),
            attention_all[layer][:, 3 * head_half : 4 * head_half].reshape(-1, width),
            in_all[layer].reshape(-1, width),
        )
        for layer in range(2)
    ]

    def head_columns(row):
        halves = row.reshape(ranks, 2, -1)
        return choose(core, (halves[:, 0], halves[:, 1])).reshape(-1)

    small = []
    for layer in range(2):
        table = attention_all[layer][0, 4 * head_half : 4 * head_half + table_rows].astype(WIDE)
        whole = relative(table)
        query_bias = head_columns(whole[gain_count])
        value_bias = head_columns(whole[gain_count + 1])
        query_bias, value_bias = query_bias.reshape(ranks, 1, -1), value_bias.reshape(ranks, 1, -1)
        offset = jnp.concatenate([query_bias, jnp.zeros_like(query_bias), value_bias], axis=1).reshape(-1)
        inner_bias = whole[gain_count + bias_count :].reshape(-1, copies, local)
        inner_bias = head_columns(jnp.swapaxes(inner_bias, 0, 1).reshape(-1))
        small.append((table[:gain_count], table[gain_count : gain_count + bias_count], offset, inner_bias, head_half))

    lengths = jnp.where(core == section, seq_lengths, to_other_core(seq_lengths))[:, 0]
    lengths = lax.dynamic_index_in_dim(lengths, rank // repeats, 0, keepdims=False)
    segments = segment_ids(lengths, ranks * own_rows)
    live = (segments < lengths.shape[0])[:, None]

    first_out, first_saved, late = layer_forward(rows, segments, lengths, weights[0], small[0], late_weights)
    weights = [weights[layer] + (late[layer],) for layer in range(2)]
    first_low = first_out.astype(LOW)
    cotangent = fetch_rows(out_grad, back_two)
    cotangent = jnp.where(live, cotangent, jnp.zeros((), LOW))
    second_out, second_saved, _ = layer_forward(first_low, segments, lengths, weights[1], small[1])
    spread = spread_both(first_low, second_out.astype(LOW))

    def hidden_grads(hidden, features):
        return [ranked(slab) for slab in counted_only(slab_grads(hidden, features, chips))]

    def attention_grads(saved, attended_grad, packed_low):
        qkv = hidden_grads(packed_low, saved[0])
        out = hidden_grads(saved[3], attended_grad)
        return [jnp.concatenate(pair, axis=1) for pair in zip(qkv, out)]

    middle_grad, branch_grad, hidden_low, second_sums = backward_hidden(
        second_saved, cotangent, weights[1], small[1]
    )
    back_slabs = hidden_grads(second_saved[6], branch_grad)
    back_here = from_x(back_slabs)
    in_slabs = hidden_grads(hidden_low, second_saved[5])
    in_here = from_x(in_slabs)
    first_grad, attended_grad, packed_low, more_sums = backward_attention(
        second_saved, segments, lengths, middle_grad, weights[1], small[1]
    )
    second_sums += more_sums
    packed_low, spread, *back_here = tie(packed_low, spread, *back_here)
    back_two = add(back_slabs[0], back_here)
    back_sent = from_section(back_two, 1)
    placed = place_both(spread)
    second_in = first_grad + core_sum(matmul(packed_low, weights[1][0]))
    qkv, out = [
        ranked(counted_only([lhs_inner(hidden, features).astype(LOW)])[0])
        for hidden, features in ((packed_low, second_saved[0]), (second_saved[3], attended_grad))
    ]
    attention_here = from_z(jnp.concatenate([qkv, out], axis=1))
    second_low = second_in.astype(LOW)

    middle_grad, branch_grad, hidden_low, first_sums = backward_hidden(
        first_saved, second_low, weights[0], small[0]
    )
    middle_grad, back_sent, placed, *in_here = tie(middle_grad, back_sent, placed, *in_here)
    back_two = add(back_two, [back_sent])
    in_two = add(in_slabs[0], in_here)
    in_sent = from_section(in_two, 1)
    outputs = placed.astype(WIDE)[None]
    second_in_spread = spread_rows(second_low)
    back_slabs = hidden_grads(first_saved[6], branch_grad)
    back_here = from_x(back_slabs)
    in_slabs = hidden_grads(hidden_low, first_saved[5])
    in_here = from_x(in_slabs)
    first_grad, attended_grad, packed_low, more_sums = backward_attention(
        first_saved, segments, lengths, middle_grad, weights[0], small[0]
    )
    first_sums += more_sums
    packed_low, in_sent, second_in_spread, *back_here = tie(packed_low, in_sent, second_in_spread, *back_here)
    in_two = add(in_two, [in_sent])
    back_one = add(back_slabs[0], back_here)
    back_sent = from_section(back_one, 0)
    second_placed = place_rows(second_in_spread, 1)
    first_in = first_grad + core_sum(matmul(packed_low, weights[0][0]))
    attention_slabs = attention_grads(first_saved, attended_grad, packed_low)
    attention_one_here = from_x(attention_slabs)
    first_in, attention_here, back_sent, *held = tie(
        first_in, attention_here, back_sent, *in_here, *attention_one_here, *attention_slabs
    )
    in_one = add(in_slabs[0], held[: chips - 1])
    attention_one_here, attention_slabs = held[chips - 1 : 2 * chips - 2], held[2 * chips - 2 :]
    attention_one = add(attention_slabs[0], attention_one_here)
    in_sent = from_section(in_one, 0)
    attention_one_sent = from_section(attention_one, 0)
    back_own, back_here = hops_z(by_section(add(back_one, [back_sent]), back_two))
    first_in_spread = spread_rows(first_in.astype(LOW))
    attention_two_slabs = jnp.split(add_ranks(attention_here), chips, axis=-1)
    attention_two_here = from_x(attention_two_slabs)

    def spread_columns(row):
        blocks = row.reshape(ranks, 1, -1)
        both = jnp.where(jnp.arange(2)[None, :, None] == core, blocks, 0.0)
        return both.reshape(-1, width)

    tables = []
    for sums in (first_sums, second_sums):
        gain_two, bias_four, bias_five, inner_sum, gain_one, bias_two, bias_three, query_sum, value_sum = sums
        common = jnp.stack([gain_one, gain_two, bias_two, bias_three, bias_four, bias_five])
        common = jnp.where(core == 0, relative(common), 0.0)
        tables.append(
            jnp.concatenate(
                [common[:2], spread_columns(query_sum), spread_columns(value_sum), common[2:], spread_columns(inner_sum)]
            )
        )
    table = jnp.stack(tables)
    table = jnp.where(counted, table, 0.0) if repeats > 1 else table
    table = table + to_other_core(table)

    in_sent, first_in_spread, table, *held = tie(
        in_sent, first_in_spread, table, *attention_two_here, *back_here
    )
    table, table_sent = choose(section, (table[0], table[1])), move(
        choose(section, (table[1], table[0])), lambda s, d, t: (1 - s, d, t)
    )
    attention_two = add(attention_two_slabs[0], held[: chips - 1])
    attention_two_sent = from_section(attention_two, 1)
    back_here = held[chips - 1 :]
    in_own, in_here = hops_z(by_section(add(in_one, [in_sent]), in_two))

    attention_one_sent, attention_two_sent, table_sent = tie(attention_one_sent, attention_two_sent, table_sent)
    table = table + table_sent
    table = sum([move(table, lambda s, d, t: (s, d ^ (2 * k), t)) for k in range(1, chips)], table)
    attention_own, attention_here = hops_z(add(attention_one, [attention_one_sent]))
    first_placed = place_rows(first_in_spread, 0)
    back_shard = finish(add(back_own, back_here))
    table = sum([move(table, lambda s, d, t: (s, d, (t + j) % ranks)) for j in range(1, ranks)], table)
    attention_one_sent, *in_here = tie(attention_one_sent, *in_here)
    attention_two = add(attention_two, [attention_two_sent])
    in_shard = finish(add(in_own, in_here))
    input_grads = by_section(first_placed, second_placed).astype(WIDE)[None]
    attention_shard = finish(by_section(add(attention_own, attention_here), attention_two))
    qkv_shard, out_shard = attention_shard[:, : 3 * head_half], attention_shard[:, 3 * head_half :]
    qkv_grad = jnp.transpose(qkv_shard.reshape(2, 3, head_half, local), (3, 1, 0, 2)).reshape(local, 3, -1)
    out_grad_w = out_shard.reshape(-1, local)
    in_grad = jnp.transpose(in_shard.reshape(-1, local))
    back_grad = back_shard.reshape(-1, local)
    sliced = lax.dynamic_slice_in_dim(table[: gain_count + bias_count], copy_at * local, local, 1)
    inner = lax.dynamic_index_in_dim(
        table[gain_count + bias_count :].reshape(copies, -1), copy_at, 0, keepdims=False
    )
    return (
        outputs,
        input_grads,
        qkv_grad[None],
        out_grad_w[None],
        in_grad[None],
        back_grad[None],
        sliced[None, :gain_count],
        sliced[None, gain_count:],
        inner[None],
    )


def solution(mesh):
    return jax.shard_map(
        on_device,
        mesh=mesh,
        in_specs=(
            P(None, ("dp", "tensor"), None),
            P(None, "dp", None),
            P("section", "dp", None, "tensor"),
            P("section", "tensor", "dp"),
            P("section", "dp", "tensor"),
            P("section", "tensor", "dp"),
            P("section", None, "dp"),
            P("section", None, "dp"),
            P("section", "dp"),
            P(None, ("dp", "tensor"), None),
        ),
        out_specs=(
            P("section", None, ("dp", "tensor"), None),
            P("section", None, ("dp", "tensor"), None),
            P("section", "dp", None, "tensor"),
            P("section", "tensor", "dp"),
            P("section", "dp", "tensor"),
            P("section", "tensor", "dp"),
            P("section", None, "dp"),
            P("section", None, "dp"),
            P("section", "dp"),
        ),
        check_vma=False,
    )
```
